32 devices in a mesh: dp: 8 (over z, core), tensor: 4 (over y, x).
Axes of the slice: x: 2, y: 2, z: 4, core: 2. Of those that a mesh axis runs over, the one named last changes fastest.
Arguments:
- inputs: bfloat16 [8192, 2048], P(('dp', 'tensor')), may hold values from -6 to 6
- cotangent: bfloat16 [8192, 2048], P(('dp', 'tensor')), may hold values from -6 to 6
- gains: float32 [2, 2048], replicated, may hold values from 0.1 to 1.9
- shifts: float32 [2, 2048], replicated, may hold values from -2 to 2
- qkv_weight: float32 [3, 2048, 2048], P(None, 'dp', 'tensor'), may hold values from -0.125 to 0.125
- biases: float32 [3, 32, 64], P(None, 'tensor', 'dp'), may hold values from -3 to 3
- out_weight: float32 [2048, 2048], P('tensor', 'dp'), may hold values from -1 to 1
- gate_up: float32 [2, 2048, 5632], P(None, 'dp', 'tensor'), may hold values from -0.125 to 0.125
- down_weight: float32 [5632, 2048], P('tensor', 'dp'), may hold values from -0.078125 to 0.078125
- momentum_gains: float32 [2, 2048], replicated, may hold values from -160 to 160
- momentum_shifts: float32 [2, 2048], replicated, may hold values from -160 to 160
- momentum_qkv: float32 [3, 2048, 2048], P(None, 'dp', 'tensor'), may hold values from -112 to 112
- momentum_biases: float32 [3, 32, 64], P(None, 'tensor', 'dp'), may hold values from -112 to 112
- momentum_out: float32 [2048, 2048], P('tensor', 'dp'), may hold values from -28 to 28
- momentum_gate: float32 [2, 2048, 5632], P(None, 'dp', 'tensor'), may hold values from -56 to 56
- momentum_down: float32 [5632, 2048], P('tensor', 'dp'), may hold values from -112 to 112
- variance_gains: float32 [2, 2048], replicated, may hold values from 245.76 to 3276.8
- variance_shifts: float32 [2, 2048], replicated, may hold values from 245.76 to 3276.8
- variance_qkv: float32 [3, 2048, 2048], P(None, 'dp', 'tensor'), may hold values from 81.92 to 1638.4
- variance_biases: float32 [3, 32, 64], P(None, 'tensor', 'dp'), may hold values from 81.92 to 1638.4
- variance_out: float32 [2048, 2048], P('tensor', 'dp'), may hold values from 5.7344 to 81.92
- variance_gate: float32 [2, 2048, 5632], P(None, 'dp', 'tensor'), may hold values from 24.576 to 327.68
- variance_down: float32 [5632, 2048], P('tensor', 'dp'), may hold values from 81.92 to 1228.8
Outputs:
- block_out: bfloat16 [8192, 2048], P(('dp', 'tensor'))
- input_grad: float32 [8192, 2048], P(('dp', 'tensor'))
- gains_grad: float32 [2, 2048], replicated
- shifts_grad: float32 [2, 2048], replicated
- qkv_grad: float32 [3, 2048, 2048], P(None, 'dp', 'tensor')
- biases_grad: float32 [3, 32, 64], P(None, 'tensor', 'dp')
- out_grad: float32 [2048, 2048], P('tensor', 'dp')
- gate_grad: float32 [2, 2048, 5632], P(None, 'dp', 'tensor')
- down_grad: float32 [5632, 2048], P('tensor', 'dp')
- new_gains: float32 [2, 2048], replicated
- new_shifts: float32 [2, 2048], replicated
- new_qkv: float32 [3, 2048, 2048], P(None, 'dp', 'tensor')
- new_biases: float32 [3, 32, 64], P(None, 'tensor', 'dp')
- new_out: float32 [2048, 2048], P('tensor', 'dp')
- new_gate: float32 [2, 2048, 5632], P(None, 'dp', 'tensor')
- new_down: float32 [5632, 2048], P('tensor', 'dp')
- new_momentum_gains: float32 [2, 2048], replicated
- new_momentum_shifts: float32 [2, 2048], replicated
- new_momentum_qkv: float32 [3, 2048, 2048], P(None, 'dp', 'tensor')
- new_momentum_biases: float32 [3, 32, 64], P(None, 'tensor', 'dp')
- new_momentum_out: float32 [2048, 2048], P('tensor', 'dp')
- new_momentum_gate: float32 [2, 2048, 5632], P(None, 'dp', 'tensor')
- new_momentum_down: float32 [5632, 2048], P('tensor', 'dp')
- new_variance_gains: float32 [2, 2048], replicated
- new_variance_shifts: float32 [2, 2048], replicated
- new_variance_qkv: float32 [3, 2048, 2048], P(None, 'dp', 'tensor')
- new_variance_biases: float32 [3, 32, 64], P(None, 'tensor', 'dp')
- new_variance_out: float32 [2048, 2048], P('tensor', 'dp')
- new_variance_gate: float32 [2, 2048, 5632], P(None, 'dp', 'tensor')
- new_variance_down: float32 [5632, 2048], P('tensor', 'dp')
The draws below stay inside these ranges and needn't reach their ends.
All inputs are finite; a program needn't handle non-finite values.
Results may differ from the reference program's by a relative error of at most 0.015.
Values may be sent and summed in bfloat16 or wider, within the bound.
A program may use at most 256 MiB of HBM per device.

```python
import math
import jax
import jax.numpy as jnp
from jax import lax

D = 2048
HEADS = 32
HEAD_DIM = 64
ROT = 16
FF = 5632
SEQ = 1024
ADAM_STEP = 3
TOKENS = 8192


def levels(own_key, extent, split, low, largest):
    factor_of, own = 1.0, jax.random.fold_in(own_key, 6)
    for axis_at, shards_of in split:
        draws = jnp.exp(jax.random.uniform(jax.random.fold_in(own, axis_at), (shards_of,), jnp.float32, low / len(split), largest / len(split)))
        factor_of = factor_of * jnp.repeat(draws, extent[axis_at] // shards_of).reshape([-1 if axis == axis_at else 1 for axis in range(len(extent))])
    return factor_of


def bell_draw(stream_key, extent, width, most, shards=(), kind=jnp.bfloat16):
    result = width * jax.random.normal(stream_key, extent, jnp.float32)
    if shards:
        result = result * levels(stream_key, extent, shards, -0.22, 0.18)
    return jnp.clip(result, -most, most).astype(kind)


def setup_inputs(seed: int = 0) -> dict:
    key_list = jax.random.split(jax.random.key(seed), 24)
    inputs = bell_draw(key_list[0], (TOKENS, D), 1.0, 6.0, ((0, 32),))
    cotangent = bell_draw(key_list[1], (TOKENS, D), 1.0, 6.0, ((0, 32),))
    gains = jnp.clip(1.0 + 0.18 * jax.random.normal(key_list[2], (2, D), jnp.float32), 0.1, 1.9)
    shifts = bell_draw(key_list[3], (2, D), 0.3, 2.0, (), jnp.float32)
    qkv_weight = bell_draw(key_list[4], (3, D, D), D ** -0.5, 0.125, ((1, 8), (2, 4)), jnp.float32)
    biases = bell_draw(key_list[5], (3, HEADS, HEAD_DIM), 0.5, 3.0, ((1, 4), (2, 8)), jnp.float32)
    out_weight = bell_draw(key_list[6], (D, D), (D // 64) ** -0.5, 1.0, ((0, 4), (1, 8)), jnp.float32)
    gate_up = bell_draw(key_list[7], (2, D, FF), D ** -0.5, 0.125, ((1, 8), (2, 4)), jnp.float32)
    down_weight = bell_draw(key_list[8], (FF, D), FF ** -0.5, 0.078125, ((0, 4), (1, 8)), jnp.float32)
    momentum_gains = bell_draw(key_list[9], (2, D), (0.3 * TOKENS ** 0.5), 160.0, (), jnp.float32)
    momentum_shifts = bell_draw(key_list[10], (2, D), (0.3 * TOKENS ** 0.5), 160.0, (), jnp.float32)
    momentum_qkv = bell_draw(key_list[11], (3, D, D), (0.2 * TOKENS ** 0.5), 112.0, ((1, 8), (2, 4)), jnp.float32)
    momentum_biases = bell_draw(key_list[12], (3, HEADS, HEAD_DIM), (0.2 * TOKENS ** 0.5), 112.0, ((1, 4), (2, 8)), jnp.float32)
    momentum_out = bell_draw(key_list[13], (D, D), (0.05 * TOKENS ** 0.5), 28.0, ((0, 4), (1, 8)), jnp.float32)
    momentum_gate = bell_draw(key_list[14], (2, D, FF), (0.1 * TOKENS ** 0.5), 56.0, ((1, 8), (2, 4)), jnp.float32)
    momentum_down = bell_draw(key_list[15], (FF, D), (0.2 * TOKENS ** 0.5), 112.0, ((0, 4), (1, 8)), jnp.float32)
    variance_gains = jnp.clip(jnp.exp(jax.random.uniform(key_list[16], (2, D), jnp.float32, math.log(245.76), math.log(3276.8))), 245.76, 3276.8)
    variance_shifts = jnp.clip(jnp.exp(jax.random.uniform(key_list[17], (2, D), jnp.float32, math.log(245.76), math.log(3276.8))), 245.76, 3276.8)
    variance_qkv = jnp.clip(jnp.exp(math.log(1638.4) - 2.9957323 * jax.random.uniform(key_list[18], (3, D, D), jnp.float32) ** levels(key_list[18], (3, D, D), ((1, 8), (2, 4)), -0.2, 0.2)), 81.92, 1638.4)
    variance_biases = jnp.clip(jnp.exp(math.log(1638.4) - 2.9957323 * jax.random.uniform(key_list[19], (3, HEADS, HEAD_DIM), jnp.float32) ** levels(key_list[19], (3, HEADS, HEAD_DIM), ((1, 4), (2, 8)), -0.2, 0.2)), 81.92, 1638.4)
    variance_out = jnp.clip(jnp.exp(math.log(81.92) - 2.65926 * jax.random.uniform(key_list[20], (D, D), jnp.float32) ** levels(key_list[20], (D, D), ((0, 4), (1, 8)), -0.2, 0.2)), 5.7344, 81.92)
    variance_gate = jnp.clip(jnp.exp(math.log(327.68) - 2.5902671 * jax.random.uniform(key_list[21], (2, D, FF), jnp.float32) ** levels(key_list[21], (2, D, FF), ((1, 8), (2, 4)), -0.2, 0.2)), 24.576, 327.68)
    variance_down = jnp.clip(jnp.exp(math.log(1228.8) - 2.7080503 * jax.random.uniform(key_list[22], (FF, D), jnp.float32) ** levels(key_list[22], (FF, D), ((0, 4), (1, 8)), -0.2, 0.2)), 81.92, 1228.8)
    return dict(inputs=inputs, cotangent=cotangent, gains=gains, shifts=shifts, qkv_weight=qkv_weight, biases=biases, out_weight=out_weight, gate_up=gate_up, down_weight=down_weight, momentum_gains=momentum_gains, momentum_shifts=momentum_shifts, momentum_qkv=momentum_qkv, momentum_biases=momentum_biases, momentum_out=momentum_out, momentum_gate=momentum_gate, momentum_down=momentum_down, variance_gains=variance_gains, variance_shifts=variance_shifts, variance_qkv=variance_qkv, variance_biases=variance_biases, variance_out=variance_out, variance_gate=variance_gate, variance_down=variance_down)


@jax.custom_vjp
def low(v):
    return lax.optimization_barrier(v.astype(jnp.bfloat16)).astype(jnp.float32)

@jax.custom_vjp
def low_back(v):
    return v

def low_keep(v):
    return (low(v), None)

def low_pass(kept, grad):
    return (grad,)

def back_keep(v):
    return (v, None)

def back_low(kept, grad):
    return (low(grad),)
low.defvjp(low_keep, low_pass)
low_back.defvjp(back_keep, back_low)
learn_rate = 0.03
vector_rate = 0.25
decay_rate = 0.1
adam_eps = 1e-08

def matmul(left, right):
    return jnp.dot(left, right, precision=lax.Precision.HIGHEST, preferred_element_type=jnp.float32)

def layer_norm(values, gain, shift):
    centred = values - lax.optimization_barrier(jnp.mean(values, -1, keepdims=True))
    recip = lax.rsqrt(lax.optimization_barrier(jnp.mean(centred * centred, -1, keepdims=True)) + 1e-05)
    return centred * recip * gain + shift

def rotate(values, sign):
    row_count = values.shape[0]
    halfway = ROT // 2
    position = (jnp.arange(row_count) % SEQ).astype(jnp.float32)
    frequency = jnp.power(10000.0, -2.0 * jnp.arange(halfway).astype(jnp.float32) / ROT)
    angles = position[:, None] * frequency[None, :]
    cosine = jnp.cos(angles)[:, None, :]
    sine = sign * jnp.sin(angles)[:, None, :]
    leading = values[..., :halfway]
    trailing = values[..., halfway:2 * halfway]
    return jnp.concatenate([leading * cosine - trailing * sine, trailing * cosine + leading * sine, values[..., 2 * halfway:]], -1)

def attend(triple):
    query, keys, values = triple
    scores = low_back(0.125 * jnp.einsum('qhd,khd->hqk', query, keys, precision=lax.Precision.HIGHEST))
    allowed = jnp.arange(SEQ)[:, None] >= jnp.arange(SEQ)[None, :]
    scores = jnp.where(allowed[None], scores, -1e+30)
    top = lax.optimization_barrier(jnp.max(scores, -1, keepdims=True))
    expo = jnp.exp(scores - top)
    probs = expo / lax.optimization_barrier(jnp.sum(expo, -1, keepdims=True))
    return jnp.einsum('hqk,khd->qhd', low(probs), values, precision=lax.Precision.HIGHEST)

def forward(xin, gains, shifts, qkv_weight, biases, out_weight, gate_up, down_weight):
    w_query = low(qkv_weight[0])
    w_key = low(qkv_weight[1])
    w_value = low(qkv_weight[2])
    w_output = low(out_weight)
    w_gate = low(gate_up[0])
    w_upward = low(gate_up[1])
    w_down = low(down_weight)
    bias_query = low(biases[0].reshape(D))
    bias_key = low(biases[1].reshape(D))
    bias_value = low(biases[2].reshape(D))
    block_rows = math.gcd(TOKENS, SEQ * max(1, 4096 // SEQ))

    def layer_step(carry, rows_in):
        normed = low(layer_norm(rows_in, gains[0], shifts[0]))
        query = low_back(matmul(normed, w_query) + bias_query)
        keys = low_back(matmul(normed, w_key) + bias_key)
        values = low_back(matmul(normed, w_value) + bias_value)
        shaped = (block_rows, HEADS, HEAD_DIM)
        query_rot = low(rotate(query.reshape(shaped), 1.0))
        key_rot = low(rotate(keys.reshape(shaped), 1.0))
        value_low = low(values.reshape(shaped))
        seq_shape = (block_rows // SEQ, SEQ, HEADS, HEAD_DIM)
        attended = lax.map(jax.checkpoint(attend), (query_rot.reshape(seq_shape), key_rot.reshape(seq_shape), value_low.reshape(seq_shape)))
        heads = low(low_back(attended.reshape(block_rows, D)))
        resid = rows_in + low_back(matmul(heads, w_output))
        second = low(layer_norm(resid, gains[1], shifts[1]))
        gate = low_back(matmul(second, w_gate))
        upward = low_back(matmul(second, w_upward))
        hidden = low(jax.nn.silu(gate) * upward)
        return (carry, resid + low_back(matmul(hidden, w_down)))
    _, outputs = lax.scan(layer_step, jnp.zeros((), jnp.float32), xin.reshape(TOKENS // block_rows, block_rows, D))
    return outputs.reshape(TOKENS, D)

def adamw(weight, grad, moment, second, decay, rate):
    moment_new = 0.9 * moment + 0.1 * grad
    second_new = 0.95 * second + 0.05 * grad * grad
    fixed_one = 1.0 - 0.9 ** ADAM_STEP
    fixed_two = 1.0 - 0.95 ** ADAM_STEP
    change = moment_new / fixed_one / (jnp.sqrt(second_new / fixed_two) + adam_eps) + decay * weight
    return (weight - rate * change, moment_new, second_new)

def reference(inputs, cotangent, gains, shifts, qkv_weight, biases, out_weight, gate_up, down_weight, momentum_gains, momentum_shifts, momentum_qkv, momentum_biases, momentum_out, momentum_gate, momentum_down, variance_gains, variance_shifts, variance_qkv, variance_biases, variance_out, variance_gate, variance_down):
    xin = inputs.astype(jnp.float32)
    outputs, pullback = jax.vjp(forward, xin, gains, shifts, qkv_weight, biases, out_weight, gate_up, down_weight)
    grads = pullback(cotangent.astype(jnp.float32))
    gain_new = adamw(gains, grads[1], momentum_gains, variance_gains, 0.0, vector_rate)
    shift_new = adamw(shifts, grads[2], momentum_shifts, variance_shifts, 0.0, vector_rate)
    qkv_new = adamw(qkv_weight, grads[3], momentum_qkv, variance_qkv, decay_rate, learn_rate)
    bias_new = adamw(biases, grads[4], momentum_biases, variance_biases, 0.0, vector_rate)
    out_new = adamw(out_weight, grads[5], momentum_out, variance_out, decay_rate, learn_rate)
    gate_new = adamw(gate_up, grads[6], momentum_gate, variance_gate, decay_rate, learn_rate)
    down_new = adamw(down_weight, grads[7], momentum_down, variance_down, decay_rate, learn_rate)
    return (outputs.astype(jnp.bfloat16), grads[0], grads[1], grads[2], grads[3], grads[4], grads[5], grads[6], grads[7], gain_new[0], shift_new[0], qkv_new[0], bias_new[0], out_new[0], gate_new[0], down_new[0], gain_new[1], shift_new[1], qkv_new[1], bias_new[1], out_new[1], gate_new[1], down_new[1], gain_new[2], shift_new[2], qkv_new[2], bias_new[2], out_new[2], gate_new[2], down_new[2])
```

```python
import functools

import jax
import jax.numpy as jnp
import numpy as np
from jax import lax
from jax.experimental import pallas as pl
from jax.experimental.layout import Layout, with_layout_constraint
from jax.experimental.pallas import tpu as pltpu
from jax.sharding import PartitionSpec as P

ROT = 16
SEQ = 1024
ADAM_STEP = 3


norm_eps = 1e-05
learn_rate = 0.03
vector_rate = 0.25
decay_rate = 0.1
adam_eps = 1e-08


def layer_norm(values, gain, shift):
    centred = values - jnp.mean(values, -1, keepdims=True)
    recip = lax.rsqrt(jnp.mean(centred * centred, -1, keepdims=True) + norm_eps)
    normed = centred * recip
    return (normed * gain + shift, normed, recip)


def norm_back(grad, normed, recip, gain):
    scaled = grad * gain
    inner = (
        scaled
        - jnp.mean(scaled, -1, keepdims=True)
        - normed * jnp.mean(scaled * normed, -1, keepdims=True)
    )
    return recip * inner


def adamw(weight, grad, moment, second, decay, rate):
    moment_new = 0.9 * moment + 0.1 * grad
    second_new = 0.95 * second + 0.05 * grad * grad
    fixed_one = 1.0 - 0.9**ADAM_STEP
    fixed_two = 1.0 - 0.95**ADAM_STEP
    change = moment_new / fixed_one / (jnp.sqrt(second_new / fixed_two) + adam_eps) + decay * weight
    return (weight - rate * change, moment_new, second_new)


def lane_head(shape, head_size):
    return lax.broadcasted_iota(jnp.int32, shape, len(shape) - 1) // head_size


def turn(values, tables, sign=1.0):
    width = values.shape[-1]
    own, ahead, behind = (jnp.concatenate([table] * (width // table.shape[-1]), 1) for table in tables)
    ahead = pltpu.roll(values, width - ROT // 2, 1) * ahead
    behind = pltpu.roll(values, ROT // 2, 1) * behind
    return values * own + sign * (ahead + behind)


def turn_tables(head_size):
    halfway = ROT // 2
    lane = np.arange(max(128, head_size)) % head_size
    position = np.arange(SEQ).astype(np.float32)
    frequency = np.power(np.float32(10000.0), -2.0 * (lane % halfway).astype(np.float32) / ROT)
    angles = position[:, None] * frequency.astype(np.float32)[None, :]
    cosine, sine = np.cos(angles), np.sin(angles)
    tables = [
        np.where(lane < ROT, cosine, 1.0),
        np.where(lane < halfway, -sine, 0.0),
        np.where((lane >= halfway) & (lane < ROT), sine, 0.0),
    ]
    return jnp.asarray(np.stack(tables).astype(np.float32))


LOG2E = 1.4426950408889634
NT = (((1,), (1,)), ((), ()))
NN = (((1,), (0,)), ((), ()))
TN = (((0,), (0,)), ((), ()))


def mxu(left, right, dims):
    return lax.dot_general(left, right, dims, preferred_element_type=jnp.float32)


def forward_kernel(head_size, lin_ref, bias_ref, table_ref, qkv_ref, out_ref, lse_ref):
    rows, width = out_ref.shape
    low = jnp.bfloat16
    step = min(256, rows)
    for part in range(3):
        for begin in range(0, rows, step):
            here = slice(begin, begin + step)
            values = lin_ref[part, here, :] + bias_ref[part : part + 1, :]
            if part < 2:
                values = turn(values, [table_ref[i, here, :] for i in range(3)])
            qkv_ref[part, here, :] = values.astype(low)
    owner = lane_head((step, width), head_size)
    lanes = lax.broadcasted_iota(jnp.int32, (step, 128), 1)
    for begin in range(0, rows, step):
        end = begin + step
        query = qkv_ref[0, begin:end, :]
        result = jnp.zeros((step, width), jnp.float32)
        logs = jnp.zeros((step, 128), jnp.float32)
        keep = lax.broadcasted_iota(jnp.int32, (step, step), 0) >= lax.broadcasted_iota(
            jnp.int32, (step, step), 1
        )
        for head in range(width // head_size):
            mine = jnp.where(owner == head, query, jnp.zeros_like(query))
            scores = mxu(mine, qkv_ref[1, :end, :], NT)
            last = jnp.where(keep, scores[:, begin:], -1e30)
            scores = jnp.concatenate([scores[:, :begin], last], 1) if begin else last
            top = jnp.max(scores, 1, keepdims=True)
            expo = jnp.exp2((scores - top) * (0.125 * LOG2E))
            total = jnp.sum(expo, 1, keepdims=True)
            found = mxu(expo.astype(low), qkv_ref[2, :end, :], NN)
            result = jnp.where(owner == head, found / total, result)
            logs = jnp.where(lanes == head, top * (0.125 * LOG2E) + jnp.log2(total), logs)
        out_ref[begin:end, :] = result.astype(low)
        lse_ref[:, begin:end] = logs.T[:8]


def attention_forward(lin, bias, head_size):
    _, rows, width = lin.shape
    lanes = min(256, width)
    groups = width // lanes
    tables = turn_tables(head_size)
    low = jnp.bfloat16
    return pl.pallas_call(
        functools.partial(forward_kernel, head_size),
        grid=(rows // SEQ, groups),
        out_shape=(
            jax.ShapeDtypeStruct((3, rows, width), low),
            jax.ShapeDtypeStruct((rows, width), low),
            jax.ShapeDtypeStruct((groups, 8, rows), jnp.float32),
        ),
        in_specs=[
            pl.BlockSpec((3, SEQ, lanes), lambda i, j: (0, i, j)),
            pl.BlockSpec((3, lanes), lambda i, j: (0, j)),
            pl.BlockSpec(tables.shape, lambda i, j: (0, 0, 0)),
        ],
        out_specs=(
            pl.BlockSpec((3, SEQ, lanes), lambda i, j: (0, i, j)),
            pl.BlockSpec((SEQ, lanes), lambda i, j: (i, j)),
            pl.BlockSpec((None, 8, SEQ), lambda i, j: (j, 0, i)),
        ),
        compiler_params=pltpu.CompilerParams(vmem_limit_bytes=48 * 1024 * 1024),
        cost_estimate=pl.CostEstimate(
            flops=rows * SEQ * width * 8, bytes_accessed=rows * width * 26, transcendentals=0
        ),
        name="attend_forward",
    )(lin, bias, tables)


def backward_kernel(head_size, qkv_ref, grad_ref, lse_ref, table_ref, out_ref, sum_ref, acc_ref):
    _, rows, width = qkv_ref.shape
    low = jnp.bfloat16
    step = min(256, rows)
    owner = lane_head((step, width), head_size)
    acc_ref[...] = jnp.zeros_like(acc_ref)
    blank = jnp.zeros((step, width), low)
    for begin in range(0, rows, step):
        end = begin + step
        query = qkv_ref[0, begin:end, :]
        grad = grad_ref[begin:end, :]
        keep = lax.broadcasted_iota(jnp.int32, (step, step), 1) >= lax.broadcasted_iota(
            jnp.int32, (step, step), 0
        )
        query_grad = jnp.zeros((step, width), jnp.float32)
        for head in range(width // head_size):
            mine = jnp.where(owner == head, query, blank)
            grad_mine = jnp.where(owner == head, grad, blank)
            scores = mxu(qkv_ref[1, :end, :], mine, NT)
            expo = jnp.exp2(scores * (0.125 * LOG2E) - lse_ref[head : head + 1, begin:end])
            last = jnp.where(keep, expo[begin:, :], 0.0)
            probs = jnp.concatenate([expo[:begin], last], 0) if begin else last
            prob_grad = mxu(qkv_ref[2, :end, :], grad_mine, NT)
            inner = jnp.sum(probs * prob_grad, 0, keepdims=True)
            score_grad = (probs * (prob_grad - inner)).astype(low)
            acc_ref[0, :end, :] += mxu(score_grad, mine, NN)
            acc_ref[1, :end, :] += mxu(probs.astype(low), grad_mine, NN)
            found = mxu(score_grad, qkv_ref[1, :end, :], TN)
            query_grad = jnp.where(owner == head, found, query_grad)
        turned = turn(0.125 * query_grad, [table_ref[i, begin:end, :] for i in range(3)], -1.0).astype(low)
        out_ref[0, begin:end, :] = turned
        added = jnp.sum(turned.astype(jnp.float32), 0, keepdims=True)
        sum_ref[0:1, :] = added if begin == 0 else sum_ref[0:1, :] + added
    for begin in range(0, rows, step):
        here = slice(begin, begin + step)
        turned = turn(0.125 * acc_ref[0, here, :], [table_ref[i, here, :] for i in range(3)], -1.0).astype(low)
        out_ref[1, here, :] = turned
        added = jnp.sum(turned.astype(jnp.float32), 0, keepdims=True)
        sum_ref[1:2, :] = added if begin == 0 else sum_ref[1:2, :] + added
        turned = acc_ref[1, here, :].astype(low)
        out_ref[2, here, :] = turned
        added = jnp.sum(turned.astype(jnp.float32), 0, keepdims=True)
        sum_ref[2:3, :] = added if begin == 0 else sum_ref[2:3, :] + added


def attention_backward(qkv, grad, logs, head_size):
    _, rows, width = qkv.shape
    lanes = min(256, width)
    groups = width // lanes
    tables = turn_tables(head_size)
    low = jnp.bfloat16
    grads, sums = pl.pallas_call(
        functools.partial(backward_kernel, head_size),
        grid=(rows // SEQ, groups),
        out_shape=(
            jax.ShapeDtypeStruct((3, rows, width), low),
            jax.ShapeDtypeStruct((rows // SEQ, 3, width), jnp.float32),
        ),
        in_specs=[
            pl.BlockSpec((3, SEQ, lanes), lambda i, j: (0, i, j)),
            pl.BlockSpec((SEQ, lanes), lambda i, j: (i, j)),
            pl.BlockSpec((None, 8, SEQ), lambda i, j: (j, 0, i)),
            pl.BlockSpec(tables.shape, lambda i, j: (0, 0, 0)),
        ],
        out_specs=(
            pl.BlockSpec((3, SEQ, lanes), lambda i, j: (0, i, j)),
            pl.BlockSpec((None, 3, lanes), lambda i, j: (i, 0, j)),
        ),
        scratch_shapes=[pltpu.VMEM((2, SEQ, lanes), jnp.float32)],
        compiler_params=pltpu.CompilerParams(vmem_limit_bytes=48 * 1024 * 1024),
        cost_estimate=pl.CostEstimate(
            flops=rows * SEQ * width * 20, bytes_accessed=rows * width * 26, transcendentals=0
        ),
        name="attend_backward",
    )(qkv, grad, logs, tables)
    return grads, jnp.sum(sums, 0)


MESH = pl.DeviceIdType.MESH


def partners():
    me = lax.axis_index("tensor")
    return me, me + 1 - 2 * (me % 2), (me + 2) % 4


def greet(devices):
    barrier = pltpu.get_barrier_semaphore()
    for device in devices:
        pl.semaphore_signal(barrier, inc=1, device_id={"tensor": device}, device_id_type=MESH)
    pl.semaphore_wait(barrier, len(devices))


def gather_kernel(block_ref, whole_ref, send_sem, recv_sem, local_sem):
    me, along_x, along_y = partners()
    rows = block_ref.shape[0]
    half = rows // 2

    def part(owner, which):
        return whole_ref.at[pl.ds(pl.multiple_of(owner * rows + which * half, half), half)]

    def send(source, owner, which, target, index):
        copy = pltpu.make_async_remote_copy(
            src_ref=source,
            dst_ref=part(owner, which),
            send_sem=send_sem.at[index],
            recv_sem=recv_sem.at[index],
            device_id={"tensor": target},
            device_id_type=MESH,
        )
        copy.start()
        return copy

    mine = pltpu.make_async_copy(block_ref, whole_ref.at[pl.ds(pl.multiple_of(me * rows, rows), rows)], local_sem)
    mine.start()
    greet((along_x, along_y))
    halves = [block_ref.at[pl.ds(0, half)], block_ref.at[pl.ds(half, half)]]
    x_first = send(halves[0], me, 0, along_x, 0)
    y_first = send(halves[1], me, 1, along_y, 1)
    x_second = send(halves[1], me, 1, along_x, 2)
    y_second = send(halves[0], me, 0, along_y, 3)
    x_first.wait_recv()
    y_third = send(part(along_x, 0), along_x, 0, along_y, 4)
    y_first.wait_recv()
    x_third = send(part(along_y, 1), along_y, 1, along_x, 5)
    for copy in (x_second, y_second, y_third, x_third):
        copy.wait_recv()
    for copy in (x_first, y_first, x_second, y_second, y_third, x_third):
        copy.wait_send()
    mine.wait()


def square_gather(block):
    rows, width = block.shape
    return pl.pallas_call(
        gather_kernel,
        out_shape=jax.ShapeDtypeStruct((4 * rows, width), block.dtype),
        in_specs=[pl.BlockSpec(memory_space=pltpu.VMEM)],
        out_specs=pl.BlockSpec(memory_space=pl.ANY),
        scratch_shapes=[
            pltpu.SemaphoreType.DMA((6,)),
            pltpu.SemaphoreType.DMA((6,)),
            pltpu.SemaphoreType.DMA,
        ],
        compiler_params=pltpu.CompilerParams(collective_id=0, has_side_effects=True),
        cost_estimate=pl.CostEstimate(flops=0, bytes_accessed=rows * width * 120, transcendentals=0),
        name="square_gather",
    )(block)


def reduce_kernel(terms_ref, ready_ref, out_ref, first_x, first_y, staged, second, send_sem, recv_sem):
    del ready_ref
    me, along_x, along_y = partners()
    rows = out_ref.shape[0]
    half = rows // 2
    corner = 3 - me

    def term(owner, which):
        return terms_ref.at[pl.ds(pl.multiple_of(owner * rows + which * half, half), half)]

    def send(source, target_ref, target, index):
        copy = pltpu.make_async_remote_copy(
            src_ref=source,
            dst_ref=target_ref,
            send_sem=send_sem.at[index],
            recv_sem=recv_sem.at[index],
            device_id={"tensor": target},
            device_id_type=MESH,
        )
        copy.start()
        return copy

    greet((along_x, along_y))
    x_on = send(term(corner, 0), first_x.at[1], along_x, 0)
    y_on = send(term(corner, 1), first_y.at[1], along_y, 1)
    x_own = send(term(along_x, 0), first_x.at[0], along_x, 2)
    y_own = send(term(along_y, 1), first_y.at[0], along_y, 3)

    def added(one, two):
        return (one.astype(jnp.float32) + two.astype(jnp.float32)).astype(jnp.bfloat16)

    x_on.wait_recv()
    staged[0] = added(term(along_y, 0)[...], first_x[1])
    y_last = send(staged.at[0], second.at[0], along_y, 4)
    y_on.wait_recv()
    staged[1] = added(term(along_x, 1)[...], first_y[1])
    x_last = send(staged.at[1], second.at[1], along_x, 5)
    x_own.wait_recv()
    out_ref[:half] = term(me, 0)[...].astype(jnp.float32) + first_x[0].astype(jnp.float32)
    y_own.wait_recv()
    out_ref[half:] = term(me, 1)[...].astype(jnp.float32) + first_y[0].astype(jnp.float32)
    y_last.wait_recv()
    out_ref[:half] += second[0].astype(jnp.float32)
    x_last.wait_recv()
    out_ref[half:] += second[1].astype(jnp.float32)
    for copy in (x_on, y_on, x_own, y_own, y_last, x_last):
        copy.wait_send()


def square_reduce(terms, ready, name):
    rows, width = terms.shape[0] // 4, terms.shape[1]
    part = pltpu.VMEM((2, rows // 2, width), jnp.bfloat16)
    return pl.pallas_call(
        reduce_kernel,
        out_shape=jax.ShapeDtypeStruct((rows, width), jnp.float32),
        in_specs=[pl.BlockSpec(memory_space=pltpu.VMEM), pl.BlockSpec(memory_space=pl.ANY)],
        out_specs=pl.BlockSpec(memory_space=pltpu.VMEM),
        scratch_shapes=[
            part,
            part,
            part,
            part,
            pltpu.SemaphoreType.DMA((6,)),
            pltpu.SemaphoreType.DMA((6,)),
        ],
        compiler_params=pltpu.CompilerParams(
            collective_id=name, has_side_effects=True, vmem_limit_bytes=24 * 1024 * 1024
        ),
        cost_estimate=pl.CostEstimate(flops=0, bytes_accessed=rows * width * 240, transcendentals=0),
        name="square_reduce",
    )(terms, ready)


def start_kernel(
    a_ref, dy_ref, bias_ref, wq_ref, wo_ref, a_all, dy_all, bias_all, wq_all, wo_all,
    square_send, square_recv, bias_send, bias_recv, line_send, line_recv, core_send, core_recv, local_sem,
):
    place, along_x, along_y = partners()
    me = lax.axis_index("dp")
    chip, core = me // 2, me % 2
    sibling = me + 1 - 2 * core
    rows = a_ref.shape[0]
    half = rows // 2
    depth = wq_ref.shape[1]

    def start(source, target, send_sem, recv_sem, device):
        copy = pltpu.make_async_remote_copy(
            src_ref=source, dst_ref=target, send_sem=send_sem, recv_sem=recv_sem,
            device_id=device, device_id_type=MESH,
        )
        copy.start()
        return copy

    def piece(part, owner):
        if part < 3:
            return wq_all.at[part, pl.ds(pl.multiple_of(owner * depth, depth), depth)]
        width = wo_ref.shape[1]
        return wo_all.at[:, pl.ds(pl.multiple_of(owner * width, width), width)]

    def own(part):
        return wq_ref.at[part] if part < 3 else wo_ref

    def turned(step):
        return 2 * ((chip + step) % 4) + core

    locals_ = [
        pltpu.make_async_copy(a_ref, a_all.at[pl.ds(pl.multiple_of(place * rows, rows), rows)], local_sem.at[0]),
        pltpu.make_async_copy(dy_ref, dy_all.at[pl.ds(pl.multiple_of(place * rows, rows), rows)], local_sem.at[1]),
    ] + [pltpu.make_async_copy(own(part), piece(part, me), local_sem.at[2 + part]) for part in range(4)]
    for copy in locals_:
        copy.start()
    bias_all[me] = bias_ref[...]

    barrier = pltpu.get_barrier_semaphore()
    for step in range(1, 8):
        pl.semaphore_signal(barrier, inc=1, device_id={"dp": (me + step) % 8}, device_id_type=MESH)
    for device in (along_x, along_y):
        pl.semaphore_signal(barrier, inc=1, device_id={"tensor": device}, device_id_type=MESH)
    pl.semaphore_wait(barrier, 9)

    def rows_of(whole, owner, which):
        return whole.at[pl.ds(pl.multiple_of(owner * rows + which * half, half), half)]

    def square_first(block, whole, base):
        halves = [block.at[pl.ds(0, half)], block.at[pl.ds(half, half)]]
        plan = [(0, along_x), (1, along_y), (1, along_x), (0, along_y)]
        return [
            start(halves[which], rows_of(whole, place, which), square_send.at[base + i], square_recv.at[base + i], {"tensor": device})
            for i, (which, device) in enumerate(plan)
        ]

    def square_next(whole, base, copies):
        copies[0].wait_recv()
        on_y = start(rows_of(whole, along_x, 0), rows_of(whole, along_x, 0), square_send.at[base + 4], square_recv.at[base + 4], {"tensor": along_y})
        copies[1].wait_recv()
        on_x = start(rows_of(whole, along_y, 1), rows_of(whole, along_y, 1), square_send.at[base + 5], square_recv.at[base + 5], {"tensor": along_x})
        return copies + [on_y, on_x]

    a_copies = square_first(a_ref, a_all, 0)
    bias_copies = [
        start(bias_all.at[me], bias_all.at[me], bias_send.at[step], bias_recv.at[step], {"dp": (me + step) % 8})
        for step in range(1, 8)
    ]

    def line(part, slot, step, source=None):
        owner = me if source is None else source
        return pltpu.make_async_remote_copy(
            src_ref=own(part) if source is None else piece(part, source),
            dst_ref=piece(part, owner),
            send_sem=line_send.at[part, slot if source is None else 0],
            recv_sem=line_recv.at[part, slot],
            device_id={"dp": turned(step)},
            device_id_type=MESH,
        )

    def to_sibling(part, slot):
        owner = turned(slot)
        return start(
            own(part) if slot == 0 else piece(part, owner), piece(part, owner),
            core_send.at[part, slot], core_recv.at[part, slot], {"dp": sibling},
        )

    for part in range(4):
        line(part, 2, 2).start()

        @pl.when(chip % 2 == 0)
        def _():
            line(part, 3, 1).start()

        @pl.when(chip % 2 == 1)
        def _():
            line(part, 1, 3).start()

    def came(part, slot):
        line(part, slot, 4 - slot).wait_recv()

    def onward(part):
        @pl.when(chip == 2)
        def _():
            line(part, 1, 1, turned(2)).start()
            line(part, 1, 3).start()

        @pl.when(chip == 1)
        def _():
            line(part, 3, 3, turned(2)).start()
            line(part, 3, 1).start()

    siblings = [to_sibling(part, 0) for part in range(4)]
    a_copies = square_next(a_all, 0, a_copies)
    dy_copies = square_first(dy_ref, dy_all, 6)
    for part in range(4):
        came(part, 2)
        onward(part)
        siblings.append(to_sibling(part, 2))
    dy_copies = square_next(dy_all, 6, dy_copies)
    for part in range(4):
        for slot in (1, 3):
            came(part, slot)
            siblings.append(to_sibling(part, slot))
    for copy in a_copies[2:] + dy_copies[2:] + bias_copies + siblings:
        copy.wait_recv()
    for copy in a_copies + dy_copies + bias_copies + siblings:
        copy.wait_send()
    for part in range(4):
        line(part, 2, 2).wait_send()

        @pl.when(chip < 3)
        def _():
            line(part, 3, 1).wait_send()

        @pl.when(chip > 0)
        def _():
            line(part, 1, 3).wait_send()

        @pl.when(chip == 2)
        def _():
            line(part, 1, 1, turned(2)).wait_send()

        @pl.when(chip == 1)
        def _():
            line(part, 3, 3, turned(2)).wait_send()

    for copy in locals_:
        copy.wait()


def start_gather(a, dy, bias, wq, wo):
    dma = pltpu.SemaphoreType.DMA
    anywhere = pl.BlockSpec(memory_space=pl.ANY)
    local_ = pl.BlockSpec(memory_space=pltpu.VMEM)
    shape = jax.ShapeDtypeStruct
    return pl.pallas_call(
        start_kernel,
        out_shape=(
            shape((4 * a.shape[0], a.shape[1]), a.dtype),
            shape((4 * dy.shape[0], dy.shape[1]), dy.dtype),
            shape((8, *bias.shape), bias.dtype),
            shape((wq.shape[0], 8 * wq.shape[1], wq.shape[2]), wq.dtype),
            shape((wo.shape[0], 8 * wo.shape[1]), wo.dtype),
        ),
        in_specs=[local_] * 5,
        out_specs=(anywhere, anywhere, local_, anywhere, anywhere),
        scratch_shapes=[
            dma((12,)), dma((12,)), dma((8,)), dma((8,)),
            dma((4, 4)), dma((4, 4)), dma((4, 4)), dma((4, 4)), dma((6,)),
        ],
        compiler_params=pltpu.CompilerParams(collective_id=2, has_side_effects=True),
        cost_estimate=pl.CostEstimate(flops=0, bytes_accessed=200_000_000, transcendentals=0),
        name="start_gather",
    )(a, dy, bias, wq, wo)


def total_kernel(split, values_ref, out_ref, corners, came, mine, slots_ref, send_sem, recv_sem):
    place, along_x, along_y = partners()
    me = lax.axis_index("dp")
    chip, sibling = me // 2, me + 1 - 2 * (me % 2)
    others = [{"tensor": device} for device in (along_x, along_y, 3 - place)]
    others += [{"dp": sibling}] + [{"dp": (me + 2 * step) % 8} for step in (1, 2, 3)]
    barrier = pltpu.get_barrier_semaphore()
    for other in others:
        pl.semaphore_signal(barrier, inc=1, device_id=other, device_id_type=MESH)
    pl.semaphore_wait(barrier, len(others))

    def start(source, target, index):
        copy = pltpu.make_async_remote_copy(
            src_ref=source,
            dst_ref=target,
            send_sem=send_sem.at[index],
            recv_sem=recv_sem.at[index],
            device_id=others[index],
            device_id_type=MESH,
        )
        copy.start()
        return copy

    corners[place] = values_ref[:, :split]
    copies = [start(corners.at[place], corners.at[place], index) for index in range(3)]
    for copy in copies:
        copy.wait_recv()
    mine[:, :split] = (corners[0] + corners[1]) + (corners[2] + corners[3])
    mine[:, split:] = values_ref[:, split:]
    copies.append(start(mine, came, 3))
    copies[3].wait_recv()
    slots_ref[chip] = mine[...] + came[...]
    last = [start(slots_ref.at[chip], slots_ref.at[chip], index) for index in (4, 5, 6)]
    for copy in last:
        copy.wait_recv()
    out_ref[...] = (slots_ref[0] + slots_ref[1]) + (slots_ref[2] + slots_ref[3])
    for copy in copies + last:
        copy.wait_send()


def slice_total(values, split):
    dma = pltpu.SemaphoreType.DMA
    shape = values.shape
    return pl.pallas_call(
        functools.partial(total_kernel, split),
        out_shape=jax.ShapeDtypeStruct(shape, values.dtype),
        in_specs=[pl.BlockSpec(memory_space=pltpu.VMEM)],
        out_specs=pl.BlockSpec(memory_space=pltpu.VMEM),
        scratch_shapes=[
            pltpu.VMEM((4, 8, split), values.dtype),
            pltpu.VMEM(shape, values.dtype),
            pltpu.VMEM(shape, values.dtype),
            pltpu.VMEM((4, *shape), values.dtype),
            dma((7,)),
            dma((7,)),
        ],
        compiler_params=pltpu.CompilerParams(collective_id=3, has_side_effects=True),
        cost_estimate=pl.CostEstimate(flops=0, bytes_accessed=30_000_000, transcendentals=0),
        name="slice_total",
    )(values)


def after(late, early):
    return lax.optimization_barrier((late, early))[0]


class Plain:
    def gather_rows(self, block):
        return lax.all_gather(block, "tensor", axis=0, tiled=True)

    def reduce_rows(self, terms, ready, name):
        return lax.psum_scatter(terms, "tensor", scatter_dimension=0, tiled=True).astype(jnp.float32)

    def begin(self, a, dy, bias, w_qkv, w_output):
        return (
            self.gather_rows(a),
            self.gather_rows(dy),
            lax.all_gather(bias, "dp", axis=2, tiled=True),
            gather_dp(w_qkv, 1),
            gather_dp(w_output, 1),
        )

    def totals(self, vectors, sums):
        return lax.psum(vectors, ("dp", "tensor")), lax.psum(sums, "dp")


class Line(Plain):
    def gather_rows(self, block):
        return square_gather(block)

    def reduce_rows(self, terms, ready, name):
        return square_reduce(terms, ready, name)

    def begin(self, a, dy, bias, w_qkv, w_output):
        parts, heads, few = bias.shape
        flat = bias.astype(jnp.float32).reshape(-1)
        width = -(-flat.shape[0] // 1024) * 1024
        flat = jnp.pad(flat, (0, width - flat.shape[0])).reshape(8, -1)
        a, dy, came, w_qkv, w_output = start_gather(a, dy, flat, w_qkv, w_output)
        came = came.reshape(8, -1)[:, : parts * heads * few].reshape(8, parts, heads, few)
        return a, dy, came.transpose(1, 2, 0, 3).reshape(parts, heads, -1), w_qkv, w_output

    def totals(self, vectors, sums):
        split = vectors.size // 8
        flat = sums.reshape(-1)
        width = -(-flat.shape[0] // 1024) * 1024
        flat = jnp.pad(flat, (0, width - flat.shape[0])).reshape(8, -1)
        total = slice_total(jnp.concatenate([vectors.reshape(8, split), flat], 1), split)
        return (
            total[:, :split].reshape(vectors.shape),
            total[:, split:].reshape(-1)[: sums.size].reshape(sums.shape),
        )


def row_major(values):
    return with_layout_constraint(values, Layout(tuple(range(values.ndim))))


def gather_dp(block, axis):
    return row_major(lax.all_gather(block.astype(jnp.bfloat16), "dp", axis=axis, tiled=True))


def scatter_dp(terms, axis):
    return lax.psum_scatter(terms.astype(jnp.bfloat16), "dp", scatter_dimension=axis, tiled=True).astype(
        jnp.float32
    )


def local(
    routes,
    inputs,
    cotangent,
    gains,
    shifts,
    qkv_weight,
    biases,
    out_weight,
    gate_up,
    down_weight,
    momentum_gains,
    momentum_shifts,
    momentum_qkv,
    momentum_biases,
    momentum_out,
    momentum_gate,
    momentum_down,
    variance_gains,
    variance_shifts,
    variance_qkv,
    variance_biases,
    variance_out,
    variance_gate,
    variance_down,
):
    low = jnp.bfloat16
    local_heads = biases.shape[1]
    local_width = qkv_weight.shape[2]
    head_size = local_width // local_heads
    xin = inputs.astype(jnp.float32)
    first_out, first_normed, first_recip = layer_norm(xin, gains[0], shifts[0])
    a_all, dy_all, bias_all, w_qkv, w_output = routes.begin(
        first_out.astype(low), cotangent, biases.astype(low), qkv_weight.astype(low), out_weight.astype(low)
    )
    bias_all = bias_all.reshape(3, local_width).astype(jnp.float32)
    w_gate_up = gather_dp(after(gate_up, w_output), 1)
    lin = jnp.einsum("rd,kdc->krc", a_all, w_qkv, preferred_element_type=jnp.float32)
    qkv, heads, logs = attention_forward(lin, bias_all, head_size)
    resid = xin + routes.reduce_rows(mxu(heads, w_output, NN).astype(low), logs, 4)
    second_out, second_normed, second_recip = layer_norm(resid, gains[1], shifts[1])
    m_all = routes.gather_rows(second_out.astype(low))
    w_down = gather_dp(after(down_weight, (w_gate_up, m_all)), 1)
    gate_vals = jnp.einsum("rd,kdc->krc", m_all, w_gate_up, preferred_element_type=jnp.float32)
    gate_lin, upward = gate_vals[0], gate_vals[1]
    sigmoid_gate = jax.nn.sigmoid(gate_lin)
    silu_gate = gate_lin * sigmoid_gate
    hidden = (silu_gate * upward).astype(low)
    down_terms = mxu(hidden, dy_all, TN).astype(low)
    down_grad = scatter_dp(down_terms, 1)
    w_down = after(w_down, down_terms)
    hidden_grad = mxu(dy_all, w_down, NT)
    gate_grad_low = (
        hidden_grad * upward * sigmoid_gate * (1.0 + gate_lin * (1.0 - sigmoid_gate))
    ).astype(low)
    up_grad_low = (hidden_grad * silu_gate).astype(low)
    both_grads = jnp.stack([gate_grad_low, up_grad_low], 0)
    gate_terms = jnp.einsum("rd,krc->kdc", m_all, both_grads, preferred_element_type=jnp.float32)
    gate_terms = row_major(gate_terms.astype(low))
    second_terms = jnp.einsum(
        "krc,kdc->rd", both_grads, w_gate_up, preferred_element_type=jnp.float32
    ).astype(low)
    block_terms = mxu(hidden, w_down, NN).astype(low)
    gate_grad = scatter_dp(after(gate_terms, (down_grad, second_terms, block_terms)), 1)
    second_grad = routes.reduce_rows(second_terms, down_grad, 5)
    resid_grad = cotangent.astype(jnp.float32) + norm_back(
        second_grad, second_normed, second_recip, gains[1]
    )
    gain_second = jnp.sum(second_grad * second_normed, 0)
    shift_second = jnp.sum(second_grad, 0)
    resid_full = routes.gather_rows(resid_grad.astype(low))
    out_terms = mxu(heads, resid_full, TN).astype(low)
    heads_grad = mxu(resid_full, w_output, NT).astype(low)
    lin_grads, bias_terms = attention_backward(qkv, heads_grad, logs, head_size)
    qkv_terms = jnp.einsum("rd,krc->kdc", a_all, lin_grads, preferred_element_type=jnp.float32)
    qkv_terms = row_major(qkv_terms.astype(low))
    out_grad = scatter_dp(after(out_terms, (gate_grad, lin_grads)), 1)
    down_sum = routes.reduce_rows(block_terms, bias_terms, 6)
    qkv_grad = scatter_dp(after(qkv_terms, (out_grad, down_sum)), 1)
    first_terms = jnp.einsum(
        "krc,kdc->rd", lin_grads, w_qkv, preferred_element_type=jnp.float32
    ).astype(low)
    first_grad = routes.reduce_rows(first_terms, bias_terms, 7)
    input_grad = resid_grad + norm_back(first_grad, first_normed, first_recip, gains[0])
    vectors = jnp.stack(
        [jnp.sum(first_grad * first_normed, 0), gain_second, jnp.sum(first_grad, 0), shift_second]
    )
    vectors, bias_sum = routes.totals(vectors, bias_terms)
    gains_grad, shifts_grad = vectors[:2], vectors[2:]
    out_grad, down_grad, gate_grad = after((out_grad, down_grad, gate_grad), first_grad)
    per_dp = biases.shape[2]
    biases_grad = lax.dynamic_slice_in_dim(
        bias_sum.reshape(3, local_heads, head_size), lax.axis_index("dp") * per_dp, per_dp, 2
    )
    block_out = (resid + down_sum).astype(low)
    gain_new = adamw(gains, gains_grad, momentum_gains, variance_gains, 0.0, vector_rate)
    shift_new = adamw(shifts, shifts_grad, momentum_shifts, variance_shifts, 0.0, vector_rate)
    qkv_new = adamw(qkv_weight, qkv_grad, momentum_qkv, variance_qkv, decay_rate, learn_rate)
    bias_new = adamw(biases, biases_grad, momentum_biases, variance_biases, 0.0, vector_rate)
    out_new = adamw(out_weight, out_grad, momentum_out, variance_out, decay_rate, learn_rate)
    gate_new = adamw(gate_up, gate_grad, momentum_gate, variance_gate, decay_rate, learn_rate)
    down_new = adamw(down_weight, down_grad, momentum_down, variance_down, decay_rate, learn_rate)
    return (
        block_out,
        input_grad,
        gains_grad,
        shifts_grad,
        qkv_grad,
        biases_grad,
        out_grad,
        gate_grad,
        down_grad,
        gain_new[0],
        shift_new[0],
        qkv_new[0],
        bias_new[0],
        out_new[0],
        gate_new[0],
        down_new[0],
        gain_new[1],
        shift_new[1],
        qkv_new[1],
        bias_new[1],
        out_new[1],
        gate_new[1],
        down_new[1],
        gain_new[2],
        shift_new[2],
        qkv_new[2],
        bias_new[2],
        out_new[2],
        gate_new[2],
        down_new[2],
    )


def solution(mesh):
    routes = Line() if dict(mesh.shape) == {"dp": 8, "tensor": 4} else Plain()

    def step(*arrays):
        return local(routes, *arrays)

    return jax.shard_map(
        step,
        mesh=mesh,
        in_specs=(
            P(("dp", "tensor"), None),
            P(("dp", "tensor"), None),
            P(),
            P(),
            P(None, "dp", "tensor"),
            P(None, "tensor", "dp"),
            P("tensor", "dp"),
            P(None, "dp", "tensor"),
            P("tensor", "dp"),
            P(),
            P(),
            P(None, "dp", "tensor"),
            P(None, "tensor", "dp"),
            P("tensor", "dp"),
            P(None, "dp", "tensor"),
            P("tensor", "dp"),
            P(),
            P(),
            P(None, "dp", "tensor"),
            P(None, "tensor", "dp"),
            P("tensor", "dp"),
            P(None, "dp", "tensor"),
            P("tensor", "dp"),
        ),
        out_specs=(
            P(("dp", "tensor"), None),
            P(("dp", "tensor"), None),
            P(),
            P(),
            P(None, "dp", "tensor"),
            P(None, "tensor", "dp"),
            P("tensor", "dp"),
            P(None, "dp", "tensor"),
            P("tensor", "dp"),
            P(),
            P(),
            P(None, "dp", "tensor"),
            P(None, "tensor", "dp"),
            P("tensor", "dp"),
            P(None, "dp", "tensor"),
            P("tensor", "dp"),
            P(),
            P(),
            P(None, "dp", "tensor"),
            P(None, "tensor", "dp"),
            P("tensor", "dp"),
            P(None, "dp", "tensor"),
            P("tensor", "dp"),
            P(),
            P(),
            P(None, "dp", "tensor"),
            P(None, "tensor", "dp"),
            P("tensor", "dp"),
            P(None, "dp", "tensor"),
            P("tensor", "dp"),
        ),
        check_vma=False,
    )
```

```python
import functools

import jax
import jax.numpy as jnp
import numpy as np
from jax import lax
from jax.experimental import pallas as pl
from jax.experimental.layout import Layout, with_layout_constraint
from jax.experimental.pallas import tpu as pltpu
from jax.sharding import PartitionSpec as P

ROT = 16
SEQ = 1024
ADAM_STEP = 3


norm_eps = 1e-05
learn_rate = 0.03
vector_rate = 0.25
decay_rate = 0.1
adam_eps = 1e-08


def layer_norm(values, gain, shift):
    centred = values - jnp.mean(values, -1, keepdims=True)
    recip = lax.rsqrt(jnp.mean(centred * centred, -1, keepdims=True) + norm_eps)
    normed = centred * recip
    return (normed * gain + shift, normed, recip)


def norm_back(grad, normed, recip, gain):
    scaled = grad * gain
    inner = (
        scaled
        - jnp.mean(scaled, -1, keepdims=True)
        - normed * jnp.mean(scaled * normed, -1, keepdims=True)
    )
    return recip * inner


def adamw(weight, grad, moment, second, decay, rate):
    moment_new = 0.9 * moment + 0.1 * grad
    second_new = 0.95 * second + 0.05 * grad * grad
    fixed_one = 1.0 - 0.9**ADAM_STEP
    fixed_two = 1.0 - 0.95**ADAM_STEP
    change = moment_new / fixed_one / (jnp.sqrt(second_new / fixed_two) + adam_eps) + decay * weight
    return (weight - rate * change, moment_new, second_new)


def lane_head(shape, head_size):
    return lax.broadcasted_iota(jnp.int32, shape, len(shape) - 1) // head_size


def turn(values, tables, sign=1.0):
    width = values.shape[-1]
    own, ahead, behind = (jnp.concatenate([table] * (width // table.shape[-1]), 1) for table in tables)
    ahead = pltpu.roll(values, width - ROT // 2, 1) * ahead
    behind = pltpu.roll(values, ROT // 2, 1) * behind
    return values * own + sign * (ahead + behind)


def turn_tables(head_size):
    halfway = ROT // 2
    lane = np.arange(max(128, head_size)) % head_size
    position = np.arange(SEQ).astype(np.float32)
    frequency = np.power(np.float32(10000.0), -2.0 * (lane % halfway).astype(np.float32) / ROT)
    angles = position[:, None] * frequency.astype(np.float32)[None, :]
    cosine, sine = np.cos(angles), np.sin(angles)
    tables = [
        np.where(lane < ROT, cosine, 1.0),
        np.where(lane < halfway, -sine, 0.0),
        np.where((lane >= halfway) & (lane < ROT), sine, 0.0),
    ]
    return jnp.asarray(np.stack(tables).astype(np.float32))


LOG2E = 1.4426950408889634
NT = (((1,), (1,)), ((), ()))
NN = (((1,), (0,)), ((), ()))
TN = (((0,), (0,)), ((), ()))


def mxu(left, right, dims):
    return lax.dot_general(left, right, dims, preferred_element_type=jnp.float32)


def forward_kernel(head_size, lin_ref, bias_ref, table_ref, qkv_ref, out_ref, lse_ref):
    rows, width = out_ref.shape
    low = jnp.bfloat16
    step = min(256, rows)
    for part in range(3):
        for begin in range(0, rows, step):
            here = slice(begin, begin + step)
            values = lin_ref[part, here, :] + bias_ref[part : part + 1, :]
            if part < 2:
                values = turn(values, [table_ref[i, here, :] for i in range(3)])
            qkv_ref[part, here, :] = values.astype(low)
    owner = lane_head((step, width), head_size)
    lanes = lax.broadcasted_iota(jnp.int32, (step, 128), 1)
    for begin in range(0, rows, step):
        end = begin + step
        query = qkv_ref[0, begin:end, :]
        result = jnp.zeros((step, width), jnp.float32)
        logs = jnp.zeros((step, 128), jnp.float32)
        keep = lax.broadcasted_iota(jnp.int32, (step, step), 0) >= lax.broadcasted_iota(
            jnp.int32, (step, step), 1
        )
        for head in range(width // head_size):
            mine = jnp.where(owner == head, query, jnp.zeros_like(query))
            scores = mxu(mine, qkv_ref[1, :end, :], NT)
            last = jnp.where(keep, scores[:, begin:], -1e30)
            scores = jnp.concatenate([scores[:, :begin], last], 1) if begin else last
            top = jnp.max(scores, 1, keepdims=True)
            expo = jnp.exp2((scores - top) * (0.125 * LOG2E))
            total = jnp.sum(expo, 1, keepdims=True)
            found = mxu(expo.astype(low), qkv_ref[2, :end, :], NN)
            result = jnp.where(owner == head, found / total, result)
            logs = jnp.where(lanes == head, top * (0.125 * LOG2E) + jnp.log2(total), logs)
        out_ref[begin:end, :] = result.astype(low)
        lse_ref[:, begin:end] = logs.T[:8]


def attention_forward(lin, bias, head_size):
    _, rows, width = lin.shape
    lanes = min(256, width)
    groups = width // lanes
    tables = turn_tables(head_size)
    low = jnp.bfloat16
    return pl.pallas_call(
        functools.partial(forward_kernel, head_size),
        grid=(rows // SEQ, groups),
        out_shape=(
            jax.ShapeDtypeStruct((3, rows, width), low),
            jax.ShapeDtypeStruct((rows, width), low),
            jax.ShapeDtypeStruct((groups, 8, rows), jnp.float32),
        ),
        in_specs=[
            pl.BlockSpec((3, SEQ, lanes), lambda i, j: (0, i, j)),
            pl.BlockSpec((3, lanes), lambda i, j: (0, j)),
            pl.BlockSpec(tables.shape, lambda i, j: (0, 0, 0)),
        ],
        out_specs=(
            pl.BlockSpec((3, SEQ, lanes), lambda i, j: (0, i, j)),
            pl.BlockSpec((SEQ, lanes), lambda i, j: (i, j)),
            pl.BlockSpec((None, 8, SEQ), lambda i, j: (j, 0, i)),
        ),
        compiler_params=pltpu.CompilerParams(vmem_limit_bytes=48 * 1024 * 1024),
        cost_estimate=pl.CostEstimate(
            flops=rows * SEQ * width * 8, bytes_accessed=rows * width * 26, transcendentals=0
        ),
        name="attend_forward",
    )(lin, bias, tables)


def backward_kernel(head_size, qkv_ref, grad_ref, lse_ref, table_ref, out_ref, sum_ref, acc_ref):
    _, rows, width = qkv_ref.shape
    low = jnp.bfloat16
    step = min(256, rows)
    owner = lane_head((step, width), head_size)
    acc_ref[...] = jnp.zeros_like(acc_ref)
    blank = jnp.zeros((step, width), low)
    for begin in range(0, rows, step):
        end = begin + step
        query = qkv_ref[0, begin:end, :]
        grad = grad_ref[begin:end, :]
        keep = lax.broadcasted_iota(jnp.int32, (step, step), 1) >= lax.broadcasted_iota(
            jnp.int32, (step, step), 0
        )
        query_grad = jnp.zeros((step, width), jnp.float32)
        for head in range(width // head_size):
            mine = jnp.where(owner == head, query, blank)
            grad_mine = jnp.where(owner == head, grad, blank)
            scores = mxu(qkv_ref[1, :end, :], mine, NT)
            expo = jnp.exp2(scores * (0.125 * LOG2E) - lse_ref[head : head + 1, begin:end])
            last = jnp.where(keep, expo[begin:, :], 0.0)
            probs = jnp.concatenate([expo[:begin], last], 0) if begin else last
            prob_grad = mxu(qkv_ref[2, :end, :], grad_mine, NT)
            inner = jnp.sum(probs * prob_grad, 0, keepdims=True)
            score_grad = (probs * (prob_grad - inner)).astype(low)
            acc_ref[0, :end, :] += mxu(score_grad, mine, NN)
            acc_ref[1, :end, :] += mxu(probs.astype(low), grad_mine, NN)
            found = mxu(score_grad, qkv_ref[1, :end, :], TN)
            query_grad = jnp.where(owner == head, found, query_grad)
        turned = turn(0.125 * query_grad, [table_ref[i, begin:end, :] for i in range(3)], -1.0).astype(low)
        out_ref[0, begin:end, :] = turned
        added = jnp.sum(turned.astype(jnp.float32), 0, keepdims=True)
        sum_ref[0:1, :] = added if begin == 0 else sum_ref[0:1, :] + added
    for begin in range(0, rows, step):
        here = slice(begin, begin + step)
        turned = turn(0.125 * acc_ref[0, here, :], [table_ref[i, here, :] for i in range(3)], -1.0).astype(low)
        out_ref[1, here, :] = turned
        added = jnp.sum(turned.astype(jnp.float32), 0, keepdims=True)
        sum_ref[1:2, :] = added if begin == 0 else sum_ref[1:2, :] + added
        turned = acc_ref[1, here, :].astype(low)
        out_ref[2, here, :] = turned
        added = jnp.sum(turned.astype(jnp.float32), 0, keepdims=True)
        sum_ref[2:3, :] = added if begin == 0 else sum_ref[2:3, :] + added


def attention_backward(qkv, grad, logs, head_size):
    _, rows, width = qkv.shape
    lanes = min(256, width)
    groups = width // lanes
    tables = turn_tables(head_size)
    low = jnp.bfloat16
    grads, sums = pl.pallas_call(
        functools.partial(backward_kernel, head_size),
        grid=(rows // SEQ, groups),
        out_shape=(
            jax.ShapeDtypeStruct((3, rows, width), low),
            jax.ShapeDtypeStruct((rows // SEQ, 3, width), jnp.float32),
        ),
        in_specs=[
            pl.BlockSpec((3, SEQ, lanes), lambda i, j: (0, i, j)),
            pl.BlockSpec((SEQ, lanes), lambda i, j: (i, j)),
            pl.BlockSpec((None, 8, SEQ), lambda i, j: (j, 0, i)),
            pl.BlockSpec(tables.shape, lambda i, j: (0, 0, 0)),
        ],
        out_specs=(
            pl.BlockSpec((3, SEQ, lanes), lambda i, j: (0, i, j)),
            pl.BlockSpec((None, 3, lanes), lambda i, j: (i, 0, j)),
        ),
        scratch_shapes=[pltpu.VMEM((2, SEQ, lanes), jnp.float32)],
        compiler_params=pltpu.CompilerParams(vmem_limit_bytes=48 * 1024 * 1024),
        cost_estimate=pl.CostEstimate(
            flops=rows * SEQ * width * 20, bytes_accessed=rows * width * 26, transcendentals=0
        ),
        name="attend_backward",
    )(qkv, grad, logs, tables)
    return grads, jnp.sum(sums, 0)


MESH = pl.DeviceIdType.MESH


def partners():
    me = lax.axis_index("tensor")
    return me, me + 1 - 2 * (me % 2), (me + 2) % 4


def greet(devices):
    barrier = pltpu.get_barrier_semaphore()
    for device in devices:
        pl.semaphore_signal(barrier, inc=1, device_id={"tensor": device}, device_id_type=MESH)
    pl.semaphore_wait(barrier, len(devices))


def gather_kernel(block_ref, whole_ref, send_sem, recv_sem, local_sem):
    me, along_x, along_y = partners()
    rows = block_ref.shape[0]
    half = rows // 2

    def part(owner, which):
        return whole_ref.at[pl.ds(pl.multiple_of(owner * rows + which * half, half), half)]

    def send(source, owner, which, target, index):
        copy = pltpu.make_async_remote_copy(
            src_ref=source,
            dst_ref=part(owner, which),
            send_sem=send_sem.at[index],
            recv_sem=recv_sem.at[index],
            device_id={"tensor": target},
            device_id_type=MESH,
        )
        copy.start()
        return copy

    mine = pltpu.make_async_copy(block_ref, whole_ref.at[pl.ds(pl.multiple_of(me * rows, rows), rows)], local_sem)
    mine.start()
    greet((along_x, along_y))
    halves = [block_ref.at[pl.ds(0, half)], block_ref.at[pl.ds(half, half)]]
    x_first = send(halves[0], me, 0, along_x, 0)
    y_first = send(halves[1], me, 1, along_y, 1)
    x_second = send(halves[1], me, 1, along_x, 2)
    y_second = send(halves[0], me, 0, along_y, 3)
    x_first.wait_recv()
    y_third = send(part(along_x, 0), along_x, 0, along_y, 4)
    y_first.wait_recv()
    x_third = send(part(along_y, 1), along_y, 1, along_x, 5)
    for copy in (x_second, y_second, y_third, x_third):
        copy.wait_recv()
    for copy in (x_first, y_first, x_second, y_second, y_third, x_third):
        copy.wait_send()
    mine.wait()


def square_gather(block):
    rows, width = block.shape
    return pl.pallas_call(
        gather_kernel,
        out_shape=jax.ShapeDtypeStruct((4 * rows, width), block.dtype),
        in_specs=[pl.BlockSpec(memory_space=pltpu.VMEM)],
        out_specs=pl.BlockSpec(memory_space=pl.ANY),
        scratch_shapes=[
            pltpu.SemaphoreType.DMA((6,)),
            pltpu.SemaphoreType.DMA((6,)),
            pltpu.SemaphoreType.DMA,
        ],
        compiler_params=pltpu.CompilerParams(collective_id=0, has_side_effects=True),
        cost_estimate=pl.CostEstimate(flops=0, bytes_accessed=rows * width * 120, transcendentals=0),
        name="square_gather",
    )(block)


def reduce_kernel(terms_ref, ready_ref, out_ref, first_x, first_y, staged, second, send_sem, recv_sem):
    del ready_ref
    me, along_x, along_y = partners()
    rows = out_ref.shape[0]
    half = rows // 2
    corner = 3 - me

    def term(owner, which):
        return terms_ref.at[pl.ds(pl.multiple_of(owner * rows + which * half, half), half)]

    def send(source, target_ref, target, index):
        copy = pltpu.make_async_remote_copy(
            src_ref=source,
            dst_ref=target_ref,
            send_sem=send_sem.at[index],
            recv_sem=recv_sem.at[index],
            device_id={"tensor": target},
            device_id_type=MESH,
        )
        copy.start()
        return copy

    greet((along_x, along_y))
    x_on = send(term(corner, 0), first_x.at[1], along_x, 0)
    y_on = send(term(corner, 1), first_y.at[1], along_y, 1)
    x_own = send(term(along_x, 0), first_x.at[0], along_x, 2)
    y_own = send(term(along_y, 1), first_y.at[0], along_y, 3)

    def added(one, two):
        return (one.astype(jnp.float32) + two.astype(jnp.float32)).astype(jnp.bfloat16)

    x_on.wait_recv()
    staged[0] = added(term(along_y, 0)[...], first_x[1])
    y_last = send(staged.at[0], second.at[0], along_y, 4)
    y_on.wait_recv()
    staged[1] = added(term(along_x, 1)[...], first_y[1])
    x_last = send(staged.at[1], second.at[1], along_x, 5)
    x_own.wait_recv()
    out_ref[:half] = term(me, 0)[...].astype(jnp.float32) + first_x[0].astype(jnp.float32)
    y_own.wait_recv()
    out_ref[half:] = term(me, 1)[...].astype(jnp.float32) + first_y[0].astype(jnp.float32)
    y_last.wait_recv()
    out_ref[:half] += second[0].astype(jnp.float32)
    x_last.wait_recv()
    out_ref[half:] += second[1].astype(jnp.float32)
    for copy in (x_on, y_on, x_own, y_own, y_last, x_last):
        copy.wait_send()


def square_reduce(terms, ready, name):
    rows, width = terms.shape[0] // 4, terms.shape[1]
    part = pltpu.VMEM((2, rows // 2, width), jnp.bfloat16)
    return pl.pallas_call(
        reduce_kernel,
        out_shape=jax.ShapeDtypeStruct((rows, width), jnp.float32),
        in_specs=[pl.BlockSpec(memory_space=pltpu.VMEM), pl.BlockSpec(memory_space=pl.ANY)],
        out_specs=pl.BlockSpec(memory_space=pltpu.VMEM),
        scratch_shapes=[
            part,
            part,
            part,
            part,
            pltpu.SemaphoreType.DMA((6,)),
            pltpu.SemaphoreType.DMA((6,)),
        ],
        compiler_params=pltpu.CompilerParams(
            collective_id=name, has_side_effects=True, vmem_limit_bytes=24 * 1024 * 1024
        ),
        cost_estimate=pl.CostEstimate(flops=0, bytes_accessed=rows * width * 240, transcendentals=0),
        name="square_reduce",
    )(terms, ready)


def start_kernel(
    a_ref, dy_ref, bias_ref, wq_ref, wo_ref, a_all, dy_all, bias_all, wq_all, wo_all,
    square_send, square_recv, bias_send, bias_recv, line_send, line_recv, core_send, core_recv, local_sem,
):
    place, along_x, along_y = partners()
    me = lax.axis_index("dp")
    chip, core = me // 2, me % 2
    sibling = me + 1 - 2 * core
    rows = a_ref.shape[0]
    half = rows // 2
    depth = wq_ref.shape[1]

    def start(source, target, send_sem, recv_sem, device):
        copy = pltpu.make_async_remote_copy(
            src_ref=source, dst_ref=target, send_sem=send_sem, recv_sem=recv_sem,
            device_id=device, device_id_type=MESH,
        )
        copy.start()
        return copy

    def piece(part, owner):
        if part < 3:
            return wq_all.at[part, pl.ds(pl.multiple_of(owner * depth, depth), depth)]
        width = wo_ref.shape[1]
        return wo_all.at[:, pl.ds(pl.multiple_of(owner * width, width), width)]

    def own(part):
        return wq_ref.at[part] if part < 3 else wo_ref

    def turned(step):
        return 2 * ((chip + step) % 4) + core

    locals_ = [
        pltpu.make_async_copy(a_ref, a_all.at[pl.ds(pl.multiple_of(place * rows, rows), rows)], local_sem.at[0]),
        pltpu.make_async_copy(dy_ref, dy_all.at[pl.ds(pl.multiple_of(place * rows, rows), rows)], local_sem.at[1]),
    ] + [pltpu.make_async_copy(own(part), piece(part, me), local_sem.at[2 + part]) for part in range(4)]
    for copy in locals_:
        copy.start()
    bias_all[me] = bias_ref[...]

    barrier = pltpu.get_barrier_semaphore()
    for step in range(1, 8):
        pl.semaphore_signal(barrier, inc=1, device_id={"dp": (me + step) % 8}, device_id_type=MESH)
    for device in (along_x, along_y):
        pl.semaphore_signal(barrier, inc=1, device_id={"tensor": device}, device_id_type=MESH)
    pl.semaphore_wait(barrier, 9)

    def rows_of(whole, owner, which):
        return whole.at[pl.ds(pl.multiple_of(owner * rows + which * half, half), half)]

    def square_first(block, whole, base):
        halves = [block.at[pl.ds(0, half)], block.at[pl.ds(half, half)]]
        plan = [(0, along_x), (1, along_y), (1, along_x), (0, along_y)]
        return [
            start(halves[which], rows_of(whole, place, which), square_send.at[base + i], square_recv.at[base + i], {"tensor": device})
            for i, (which, device) in enumerate(plan)
        ]

    def square_next(whole, base, copies):
        copies[0].wait_recv()
        on_y = start(rows_of(whole, along_x, 0), rows_of(whole, along_x, 0), square_send.at[base + 4], square_recv.at[base + 4], {"tensor": along_y})
        copies[1].wait_recv()
        on_x = start(rows_of(whole, along_y, 1), rows_of(whole, along_y, 1), square_send.at[base + 5], square_recv.at[base + 5], {"tensor": along_x})
        return copies + [on_y, on_x]

    a_copies = square_first(a_ref, a_all, 0)
    bias_copies = [
        start(bias_all.at[me], bias_all.at[me], bias_send.at[step], bias_recv.at[step], {"dp": (me + step) % 8})
        for step in range(1, 8)
    ]

    def line(part, slot, step, source=None):
        owner = me if source is None else source
        return pltpu.make_async_remote_copy(
            src_ref=own(part) if source is None else piece(part, source),
            dst_ref=piece(part, owner),
            send_sem=line_send.at[part, slot if source is None else 0],
            recv_sem=line_recv.at[part, slot],
            device_id={"dp": turned(step)},
            device_id_type=MESH,
        )

    def to_sibling(part, slot):
        owner = turned(slot)
        return start(
            own(part) if slot == 0 else piece(part, owner), piece(part, owner),
            core_send.at[part, slot], core_recv.at[part, slot], {"dp": sibling},
        )

    for part in range(4):
        line(part, 2, 2).start()

        @pl.when(chip % 2 == 0)
        def _():
            line(part, 3, 1).start()

        @pl.when(chip % 2 == 1)
        def _():
            line(part, 1, 3).start()

    def came(part, slot):
        line(part, slot, 4 - slot).wait_recv()

    def onward(part):
        @pl.when(chip == 2)
        def _():
            line(part, 1, 1, turned(2)).start()
            line(part, 1, 3).start()

        @pl.when(chip == 1)
        def _():
            line(part, 3, 3, turned(2)).start()
            line(part, 3, 1).start()

    siblings = [to_sibling(part, 0) for part in range(4)]
    a_copies = square_next(a_all, 0, a_copies)
    dy_copies = square_first(dy_ref, dy_all, 6)
    for part in range(4):
        came(part, 2)
        onward(part)
        siblings.append(to_sibling(part, 2))
    dy_copies = square_next(dy_all, 6, dy_copies)
    for part in range(4):
        for slot in (1, 3):
            came(part, slot)
            siblings.append(to_sibling(part, slot))
    for copy in a_copies[2:] + dy_copies[2:] + bias_copies + siblings:
        copy.wait_recv()
    for copy in a_copies + dy_copies + bias_copies + siblings:
        copy.wait_send()
    for part in range(4):
        line(part, 2, 2).wait_send()

        @pl.when(chip < 3)
        def _():
            line(part, 3, 1).wait_send()

        @pl.when(chip > 0)
        def _():
            line(part, 1, 3).wait_send()

        @pl.when(chip == 2)
        def _():
            line(part, 1, 1, turned(2)).wait_send()

        @pl.when(chip == 1)
        def _():
            line(part, 3, 3, turned(2)).wait_send()

    for copy in locals_:
        copy.wait()


def start_gather(a, dy, bias, wq, wo):
    dma = pltpu.SemaphoreType.DMA
    anywhere = pl.BlockSpec(memory_space=pl.ANY)
    local_ = pl.BlockSpec(memory_space=pltpu.VMEM)
    shape = jax.ShapeDtypeStruct
    return pl.pallas_call(
        start_kernel,
        out_shape=(
            shape((4 * a.shape[0], a.shape[1]), a.dtype),
            shape((4 * dy.shape[0], dy.shape[1]), dy.dtype),
            shape((8, *bias.shape), bias.dtype),
            shape((wq.shape[0], 8 * wq.shape[1], wq.shape[2]), wq.dtype),
            shape((wo.shape[0], 8 * wo.shape[1]), wo.dtype),
        ),
        in_specs=[local_] * 5,
        out_specs=(anywhere, anywhere, local_, anywhere, anywhere),
        scratch_shapes=[
            dma((12,)), dma((12,)), dma((8,)), dma((8,)),
            dma((4, 4)), dma((4, 4)), dma((4, 4)), dma((4, 4)), dma((6,)),
        ],
        compiler_params=pltpu.CompilerParams(collective_id=2, has_side_effects=True),
        cost_estimate=pl.CostEstimate(flops=0, bytes_accessed=200_000_000, transcendentals=0),
        name="start_gather",
    )(a, dy, bias, wq, wo)


def tail_kernel(
    first_ref, block_ref, qkv_ref, proj_ref, normed_ref, recip_ref, gain_ref, grad_ref, resid_ref, second_ref, bias_ref,
    input_out, block_out, qkv_out, proj_out, vector_out, bias_out,
    square_x, square_y, staged, square_last, core_qkv, core_proj, near_qkv, near_proj,
    corners, vector_mine, vector_came, vector_slots, bias_mine, bias_came, bias_slots,
    square_send, square_recv, core_send, core_recv, line_send, line_recv, vector_send, vector_recv, bias_send, bias_recv,
):
    place, along_x, along_y = partners()
    corner = 3 - place
    me = lax.axis_index("dp")
    chip, core = me // 2, me % 2
    sibling = me + 1 - 2 * core
    rows = input_out.shape[0]
    half = rows // 2
    depth = qkv_out.shape[1]
    width = proj_out.shape[1]
    low, wide = jnp.bfloat16, jnp.float32

    def start(source, target, send_sem, recv_sem, device):
        copy = pltpu.make_async_remote_copy(
            src_ref=source, dst_ref=target, send_sem=send_sem, recv_sem=recv_sem,
            device_id=device, device_id_type=MESH,
        )
        copy.start()
        return copy

    barrier = pltpu.get_barrier_semaphore()
    chips = [{"dp": (me + 2 * step) % 8} for step in (1, 2, 3)]
    square = [{"tensor": device} for device in (along_x, along_y, corner)]
    for other in square + [{"dp": sibling}] + chips:
        pl.semaphore_signal(barrier, inc=1, device_id=other, device_id_type=MESH)
    pl.semaphore_wait(barrier, 7)

    def turned(slot, which):
        return 2 * ((chip + slot) % 4) + which

    def qkv_part(owner):
        return qkv_ref.at[:, pl.ds(pl.multiple_of(owner * depth, depth), depth)]

    def proj_part(owner):
        return proj_ref.at[:, pl.ds(pl.multiple_of(owner * width, width), width)]

    exchange = {}
    for slot in (3, 1, 2, 0):
        owner = turned(slot, 1 - core)
        exchange[slot] = [
            start(qkv_part(owner), core_qkv.at[slot], core_send.at[0, slot], core_recv.at[0, slot], {"dp": sibling}),
            start(proj_part(owner), core_proj.at[slot], core_send.at[1, slot], core_recv.at[1, slot], {"dp": sibling}),
        ]

    def square_first(terms, base, which):
        def term(owner, part):
            return terms.at[pl.ds(pl.multiple_of(owner * rows + part * half, half), half)]

        plan = [
            (term(corner, 0), square_x.at[which, 1], along_x),
            (term(corner, 1), square_y.at[which, 1], along_y),
            (term(along_x, 0), square_x.at[which, 0], along_x),
            (term(along_y, 1), square_y.at[which, 0], along_y),
        ]
        return [
            start(source, target, square_send.at[base + i], square_recv.at[base + i], {"tensor": device})
            for i, (source, target, device) in enumerate(plan)
        ]

    def rows_at(terms, owner, part):
        return terms[pl.ds(pl.multiple_of(owner * rows + part * half, half), half), :].astype(wide)

    def square_next(terms, base, which, copies):
        copies[0].wait_recv()
        staged[which, 0] = (rows_at(terms, along_y, 0) + square_x[which, 1].astype(wide)).astype(low)
        on_y = start(staged.at[which, 0], square_last.at[which, 0], square_send.at[base + 4], square_recv.at[base + 4], square[1])
        copies[1].wait_recv()
        staged[which, 1] = (rows_at(terms, along_x, 1) + square_y[which, 1].astype(wide)).astype(low)
        on_x = start(staged.at[which, 1], square_last.at[which, 1], square_send.at[base + 5], square_recv.at[base + 5], square[0])
        return copies + [on_y, on_x]

    def square_sum(terms, which, part):
        near = square_x if part == 0 else square_y
        return rows_at(terms, place, part) + near[which, 0].astype(wide) + square_last[which, part].astype(wide)

    first_copies = square_first(first_ref, 0, 0)

    def line(slot, step, part):
        device = {"dp": turned(step, core)}
        return [
            pltpu.make_async_remote_copy(
                src_ref=source.at[slot], dst_ref=target.at[part],
                send_sem=line_send.at[i, part], recv_sem=line_recv.at[i, part], device_id=device, device_id_type=MESH,
            )
            for i, (source, target) in enumerate(((core_qkv, near_qkv), (core_proj, near_proj)))
        ]

    def go(slot, step, part):
        for copy in line(slot, step, part):
            copy.start()

    def came(part):
        for copy in line(part, 1, part):
            copy.wait_recv()

    def sent(slot, step, part):
        for copy in line(slot, step, part):
            copy.wait_send()

    for slot in (3, 1, 2):
        for copy in exchange[slot]:
            copy.wait_recv()
        owner = turned(slot, core)
        for index in range(3):
            core_qkv[slot, index] = (
                core_qkv[slot, index].astype(wide) + qkv_part(owner)[index].astype(wide)
            ).astype(low)
        core_proj[slot] = (core_proj[slot].astype(wide) + proj_part(owner)[...].astype(wide)).astype(low)
        if slot == 3:

            @pl.when(chip == 0)
            def _():
                go(3, 1, 0)

            @pl.when((chip == 1) | (chip == 2))
            def _():
                go(3, 3, 3)

        elif slot == 1:

            @pl.when(chip == 3)
            def _():
                go(1, 3, 0)

            @pl.when((chip == 1) | (chip == 2))
            def _():
                go(1, 1, 1)

        else:

            @pl.when((chip == 0) | (chip == 3))
            def _():
                go(2, 2, 2)

    first_copies = square_next(first_ref, 0, 0, first_copies)
    block_copies = square_first(block_ref, 6, 1)
    for copy in first_copies[2:]:
        copy.wait_recv()
    gain = gain_ref[...]
    vector_gain = jnp.zeros_like(gain)
    vector_shift = jnp.zeros_like(gain)
    for part in range(2):
        here = slice(part * half, (part + 1) * half)
        grad = square_sum(first_ref, 0, part)
        normed = normed_ref[here, :]
        vector_gain += jnp.sum(grad * normed, 0, keepdims=True)
        vector_shift += jnp.sum(grad, 0, keepdims=True)
        scaled = grad * gain
        inner = (
            scaled
            - jnp.mean(scaled, -1, keepdims=True)
            - normed * jnp.mean(scaled * normed, -1, keepdims=True)
        )
        input_out[here, :] = grad_ref[here, :] + recip_ref[here, :] * inner
    corners[place, 0:1, :] = vector_gain
    corners[place, 1:2, :] = second_ref[0:1, :]
    corners[place, 2:3, :] = vector_shift
    corners[place, 3:4, :] = second_ref[1:2, :]
    vector_copies = [
        start(corners.at[place], corners.at[place], vector_send.at[i], vector_recv.at[i], square[i]) for i in range(3)
    ]
    bias_mine[...] = bias_ref[...]
    bias_copies = [start(bias_mine, bias_came, bias_send.at[0], bias_recv.at[0], {"dp": sibling})]

    def onward(slot, part):
        for i, (mine, came_) in enumerate(((core_qkv, near_qkv), (core_proj, near_proj))):
            mine[2] = (mine[2].astype(wide) + came_[0].astype(wide)).astype(low)

    @pl.when((chip == 1) | (chip == 2))
    def _():
        came(0)
        onward(2, 0)
        go(2, 2, 2)

    @pl.when(chip == 0)
    def _():
        sent(3, 1, 0)
        go(1, 1, 1)

    @pl.when(chip == 3)
    def _():
        sent(1, 3, 0)
        go(3, 3, 3)

    for copy in vector_copies:
        copy.wait_recv()
    vector_mine[...] = (corners[0] + corners[1]) + (corners[2] + corners[3])
    vector_copies.append(start(vector_mine, vector_came, vector_send.at[3], vector_recv.at[3], {"dp": sibling}))
    block_copies = square_next(block_ref, 6, 1, block_copies)
    vector_copies[3].wait_recv()
    bias_copies[0].wait_recv()
    vector_slots[chip] = vector_mine[...] + vector_came[...]
    bias_slots[chip] = bias_mine[...] + bias_came[...]
    vector_copies += [
        start(vector_slots.at[chip], vector_slots.at[chip], vector_send.at[4 + i], vector_recv.at[4 + i], chips[i])
        for i in range(3)
    ]
    bias_copies += [
        start(bias_slots.at[chip], bias_slots.at[chip], bias_send.at[1 + i], bias_recv.at[1 + i], chips[i])
        for i in range(3)
    ]
    for copy in exchange[0]:
        copy.wait_recv()
    for copy in block_copies[2:]:
        copy.wait_recv()
    for part in range(2):
        here = slice(part * half, (part + 1) * half)
        block_out[here, :] = (resid_ref[here, :] + square_sum(block_ref, 1, part)).astype(low)
    for copy in vector_copies[4:] + bias_copies[1:]:
        copy.wait_recv()
    vector_out[...] = (vector_slots[0] + vector_slots[1]) + (vector_slots[2] + vector_slots[3])
    bias_out[...] = (bias_slots[0] + bias_slots[1]) + (bias_slots[2] + bias_slots[3])

    came(2)

    @pl.when(chip > 0)
    def _():
        came(1)

    @pl.when(chip < 3)
    def _():
        came(3)

    below, above = (chip > 0), (chip < 3)
    owner = turned(0, core)

    def last(own, other, came_1, came_2, came_3):
        total = own.astype(wide) + other.astype(wide) + came_2.astype(wide)
        total = total + jnp.where(below, came_1.astype(wide), 0.0)
        return total + jnp.where(above, came_3.astype(wide), 0.0)

    for index in range(3):
        qkv_out[index] = last(
            qkv_part(owner)[index], core_qkv[0, index], near_qkv[1, index], near_qkv[2, index], near_qkv[3, index]
        )
    proj_out[...] = last(proj_part(owner)[...], core_proj[0], near_proj[1], near_proj[2], near_proj[3])

    for copy in first_copies + block_copies + vector_copies + bias_copies:
        copy.wait_send()
    for slot in range(4):
        for copy in exchange[slot]:
            copy.wait_send()
    sent(2, 2, 2)

    @pl.when(chip < 3)
    def _():
        sent(1, 1, 1)

    @pl.when(chip > 0)
    def _():
        sent(3, 3, 3)


def tail_reduce(first, block, qkv, proj, normed, recip, gain, grad, resid, second, bias):
    dma = pltpu.SemaphoreType.DMA
    low, wide = jnp.bfloat16, jnp.float32
    shape, vmem = jax.ShapeDtypeStruct, pltpu.VMEM
    rows, model = resid.shape
    parts, depth, columns = qkv.shape[0], qkv.shape[1] // 8, qkv.shape[2]
    width = proj.shape[1] // 8
    pair = vmem((2, 2, rows // 2, model), low)
    return pl.pallas_call(
        tail_kernel,
        out_shape=(
            shape((rows, model), wide),
            shape((rows, model), low),
            shape((parts, depth, columns), wide),
            shape((proj.shape[0], width), wide),
            shape((4, model), wide),
            shape(bias.shape, wide),
        ),
        in_specs=[pl.BlockSpec(memory_space=pltpu.VMEM)] * 11,
        out_specs=(pl.BlockSpec(memory_space=pltpu.VMEM),) * 6,
        scratch_shapes=[
            pair, pair, pair, pair,
            vmem((4, parts, depth, columns), low),
            vmem((4, proj.shape[0], width), low),
            vmem((4, parts, depth, columns), low),
            vmem((4, proj.shape[0], width), low),
            vmem((4, 4, model), wide),
            vmem((4, model), wide),
            vmem((4, model), wide),
            vmem((4, 4, model), wide),
            vmem(bias.shape, wide),
            vmem(bias.shape, wide),
            vmem((4, *bias.shape), wide),
            dma((12,)), dma((12,)), dma((2, 4)), dma((2, 4)), dma((2, 4)), dma((2, 4)),
            dma((7,)), dma((7,)), dma((4,)), dma((4,)),
        ],
        compiler_params=pltpu.CompilerParams(
            collective_id=3, has_side_effects=True, vmem_limit_bytes=60 * 1024 * 1024
        ),
        cost_estimate=pl.CostEstimate(flops=0, bytes_accessed=200_000_000, transcendentals=0),
        name="tail_reduce",
    )(first, block, qkv, proj, normed, recip, gain, grad, resid, second, bias)


def after(late, early):
    return lax.optimization_barrier((late, early))[0]


class Plain:
    def gather_rows(self, block):
        return lax.all_gather(block, "tensor", axis=0, tiled=True)

    def reduce_rows(self, terms, ready, name):
        return lax.psum_scatter(terms, "tensor", scatter_dimension=0, tiled=True).astype(jnp.float32)

    def begin(self, a, dy, bias, w_qkv, w_output):
        return (
            self.gather_rows(a),
            self.gather_rows(dy),
            lax.all_gather(bias, "dp", axis=2, tiled=True),
            gather_dp(w_qkv, 1),
            gather_dp(w_output, 1),
        )

    def finish(self, first, block, qkv, proj, normed, recip, gain, grad, resid, second, bias):
        first = self.reduce_rows(first, None, 0)
        vectors = jnp.stack([jnp.sum(first * normed, 0), second[0], jnp.sum(first, 0), second[1]])
        return (
            grad + norm_back(first, normed, recip, gain),
            (resid + self.reduce_rows(block, None, 0)).astype(jnp.bfloat16),
            scatter_dp(qkv, 1),
            scatter_dp(proj, 1),
            lax.psum(vectors, ("dp", "tensor")),
            lax.psum(bias, "dp"),
        )


class Line(Plain):
    def gather_rows(self, block):
        return square_gather(block)

    def reduce_rows(self, terms, ready, name):
        return square_reduce(terms, ready, name)

    def begin(self, a, dy, bias, w_qkv, w_output):
        parts, heads, few = bias.shape
        flat = bias.astype(jnp.float32).reshape(-1)
        width = -(-flat.shape[0] // 1024) * 1024
        flat = jnp.pad(flat, (0, width - flat.shape[0])).reshape(8, -1)
        a, dy, came, w_qkv, w_output = start_gather(a, dy, flat, w_qkv, w_output)
        came = came.reshape(8, -1)[:, : parts * heads * few].reshape(8, parts, heads, few)
        return a, dy, came.transpose(1, 2, 0, 3).reshape(parts, heads, -1), w_qkv, w_output

    def finish(self, first, block, qkv, proj, normed, recip, gain, grad, resid, second, bias):
        flat = bias.reshape(-1)
        width = -(-flat.shape[0] // 1024) * 1024
        flat = jnp.pad(flat, (0, width - flat.shape[0])).reshape(8, -1)
        *found, total = tail_reduce(
            first, block, qkv, proj, normed, recip, gain.reshape(1, -1), grad, resid, second, flat
        )
        return (*found, total.reshape(-1)[: bias.size].reshape(bias.shape))


def row_major(values):
    return with_layout_constraint(values, Layout(tuple(range(values.ndim))))


def gather_dp(block, axis):
    return row_major(lax.all_gather(block.astype(jnp.bfloat16), "dp", axis=axis, tiled=True))


def scatter_dp(terms, axis):
    return lax.psum_scatter(terms.astype(jnp.bfloat16), "dp", scatter_dimension=axis, tiled=True).astype(
        jnp.float32
    )


def local(
    routes,
    inputs,
    cotangent,
    gains,
    shifts,
    qkv_weight,
    biases,
    out_weight,
    gate_up,
    down_weight,
    momentum_gains,
    momentum_shifts,
    momentum_qkv,
    momentum_biases,
    momentum_out,
    momentum_gate,
    momentum_down,
    variance_gains,
    variance_shifts,
    variance_qkv,
    variance_biases,
    variance_out,
    variance_gate,
    variance_down,
):
    low = jnp.bfloat16
    local_heads = biases.shape[1]
    local_width = qkv_weight.shape[2]
    head_size = local_width // local_heads
    xin = inputs.astype(jnp.float32)
    first_out, first_normed, first_recip = layer_norm(xin, gains[0], shifts[0])
    a_all, dy_all, bias_all, w_qkv, w_output = routes.begin(
        first_out.astype(low), cotangent, biases.astype(low), qkv_weight.astype(low), out_weight.astype(low)
    )
    bias_all = bias_all.reshape(3, local_width).astype(jnp.float32)
    w_gate_up = gather_dp(after(gate_up.astype(low), w_output), 1)
    lin = jnp.einsum("rd,kdc->krc", a_all, w_qkv, preferred_element_type=jnp.float32)
    qkv, heads, logs = attention_forward(lin, bias_all, head_size)
    resid = xin + routes.reduce_rows(mxu(heads, w_output, NN).astype(low), logs, 4)
    second_out, second_normed, second_recip = layer_norm(resid, gains[1], shifts[1])
    m_all = routes.gather_rows(second_out.astype(low))
    w_down = gather_dp(after(down_weight.astype(low), (w_gate_up, m_all)), 1)
    gate_vals = jnp.einsum("rd,kdc->krc", m_all, w_gate_up, preferred_element_type=jnp.float32)
    gate_lin, upward = gate_vals[0], gate_vals[1]
    sigmoid_gate = jax.nn.sigmoid(gate_lin)
    silu_gate = gate_lin * sigmoid_gate
    hidden = (silu_gate * upward).astype(low)
    down_terms = mxu(hidden, dy_all, TN).astype(low)
    down_grad = scatter_dp(down_terms, 1)
    w_down = after(w_down, down_terms)
    hidden_grad = mxu(dy_all, w_down, NT)
    gate_grad_low = (
        hidden_grad * upward * sigmoid_gate * (1.0 + gate_lin * (1.0 - sigmoid_gate))
    ).astype(low)
    up_grad_low = (hidden_grad * silu_gate).astype(low)
    both_grads = jnp.stack([gate_grad_low, up_grad_low], 0)
    gate_terms = jnp.einsum("rd,krc->kdc", m_all, both_grads, preferred_element_type=jnp.float32)
    gate_terms = row_major(gate_terms.astype(low))
    second_terms = jnp.einsum(
        "krc,kdc->rd", both_grads, w_gate_up, preferred_element_type=jnp.float32
    ).astype(low)
    block_terms = mxu(hidden, w_down, NN).astype(low)
    gate_grad = scatter_dp(after(gate_terms, (down_grad, second_terms, block_terms)), 1)
    second_grad = routes.reduce_rows(second_terms, down_grad, 5)
    resid_grad = cotangent.astype(jnp.float32) + norm_back(
        second_grad, second_normed, second_recip, gains[1]
    )
    gain_second = jnp.sum(second_grad * second_normed, 0)
    shift_second = jnp.sum(second_grad, 0)
    resid_full = routes.gather_rows(resid_grad.astype(low))
    out_terms = mxu(heads, resid_full, TN).astype(low)
    heads_grad = mxu(resid_full, w_output, NT).astype(low)
    lin_grads, bias_terms = attention_backward(qkv, heads_grad, logs, head_size)
    qkv_terms = jnp.einsum("rd,krc->kdc", a_all, lin_grads, preferred_element_type=jnp.float32)
    qkv_terms = row_major(qkv_terms.astype(low))
    first_terms = jnp.einsum(
        "krc,kdc->rd", lin_grads, w_qkv, preferred_element_type=jnp.float32
    ).astype(low)
    input_grad, block_out, qkv_grad, out_grad, vectors, bias_sum = routes.finish(
        first_terms,
        block_terms,
        qkv_terms,
        out_terms,
        first_normed,
        first_recip,
        gains[0],
        resid_grad,
        resid,
        jnp.stack([gain_second, shift_second]),
        bias_terms,
    )
    gains_grad, shifts_grad = vectors[:2], vectors[2:]
    down_grad, gate_grad = after((down_grad, gate_grad), vectors)
    per_dp = biases.shape[2]
    biases_grad = lax.dynamic_slice_in_dim(
        bias_sum.reshape(3, local_heads, head_size), lax.axis_index("dp") * per_dp, per_dp, 2
    )
    gain_new = adamw(gains, gains_grad, momentum_gains, variance_gains, 0.0, vector_rate)
    shift_new = adamw(shifts, shifts_grad, momentum_shifts, variance_shifts, 0.0, vector_rate)
    qkv_new = adamw(qkv_weight, qkv_grad, momentum_qkv, variance_qkv, decay_rate, learn_rate)
    bias_new = adamw(biases, biases_grad, momentum_biases, variance_biases, 0.0, vector_rate)
    out_new = adamw(out_weight, out_grad, momentum_out, variance_out, decay_rate, learn_rate)
    gate_new = adamw(gate_up, gate_grad, momentum_gate, variance_gate, decay_rate, learn_rate)
    down_new = adamw(down_weight, down_grad, momentum_down, variance_down, decay_rate, learn_rate)
    return (
        block_out,
        input_grad,
        gains_grad,
        shifts_grad,
        qkv_grad,
        biases_grad,
        out_grad,
        gate_grad,
        down_grad,
        gain_new[0],
        shift_new[0],
        qkv_new[0],
        bias_new[0],
        out_new[0],
        gate_new[0],
        down_new[0],
        gain_new[1],
        shift_new[1],
        qkv_new[1],
        bias_new[1],
        out_new[1],
        gate_new[1],
        down_new[1],
        gain_new[2],
        shift_new[2],
        qkv_new[2],
        bias_new[2],
        out_new[2],
        gate_new[2],
        down_new[2],
    )


def solution(mesh):
    routes = Line() if dict(mesh.shape) == {"dp": 8, "tensor": 4} else Plain()

    def step(*arrays):
        return local(routes, *arrays)

    return jax.shard_map(
        step,
        mesh=mesh,
        in_specs=(
            P(("dp", "tensor"), None),
            P(("dp", "tensor"), None),
            P(),
            P(),
            P(None, "dp", "tensor"),
            P(None, "tensor", "dp"),
            P("tensor", "dp"),
            P(None, "dp", "tensor"),
            P("tensor", "dp"),
            P(),
            P(),
            P(None, "dp", "tensor"),
            P(None, "tensor", "dp"),
            P("tensor", "dp"),
            P(None, "dp", "tensor"),
            P("tensor", "dp"),
            P(),
            P(),
            P(None, "dp", "tensor"),
            P(None, "tensor", "dp"),
            P("tensor", "dp"),
            P(None, "dp", "tensor"),
            P("tensor", "dp"),
        ),
        out_specs=(
            P(("dp", "tensor"), None),
            P(("dp", "tensor"), None),
            P(),
            P(),
            P(None, "dp", "tensor"),
            P(None, "tensor", "dp"),
            P("tensor", "dp"),
            P(None, "dp", "tensor"),
            P("tensor", "dp"),
            P(),
            P(),
            P(None, "dp", "tensor"),
            P(None, "tensor", "dp"),
            P("tensor", "dp"),
            P(None, "dp", "tensor"),
            P("tensor", "dp"),
            P(),
            P(),
            P(None, "dp", "tensor"),
            P(None, "tensor", "dp"),
            P("tensor", "dp"),
            P(None, "dp", "tensor"),
            P("tensor", "dp"),
            P(),
            P(),
            P(None, "dp", "tensor"),
            P(None, "tensor", "dp"),
            P("tensor", "dp"),
            P(None, "dp", "tensor"),
            P("tensor", "dp"),
        ),
        check_vma=False,
    )
```

```python
import functools

import jax
import jax.numpy as jnp
import numpy as np
from jax import lax
from jax.experimental import pallas as pl
from jax.experimental.layout import Layout, with_layout_constraint
from jax.experimental.pallas import tpu as pltpu
from jax.sharding import PartitionSpec as P

ROT = 16
SEQ = 1024
ADAM_STEP = 3


norm_eps = 1e-05
learn_rate = 0.03
vector_rate = 0.25
decay_rate = 0.1
adam_eps = 1e-08


def layer_norm(values, gain, shift):
    centred = values - jnp.mean(values, -1, keepdims=True)
    recip = lax.rsqrt(jnp.mean(centred * centred, -1, keepdims=True) + norm_eps)
    normed = centred * recip
    return (normed * gain + shift, normed, recip)


def norm_back(grad, normed, recip, gain):
    scaled = grad * gain
    inner = (
        scaled
        - jnp.mean(scaled, -1, keepdims=True)
        - normed * jnp.mean(scaled * normed, -1, keepdims=True)
    )
    return recip * inner


def adamw(weight, grad, moment, second, decay, rate):
    moment_new = 0.9 * moment + 0.1 * grad
    second_new = 0.95 * second + 0.05 * grad * grad
    fixed_one = 1.0 - 0.9**ADAM_STEP
    fixed_two = 1.0 - 0.95**ADAM_STEP
    change = moment_new / fixed_one / (jnp.sqrt(second_new / fixed_two) + adam_eps) + decay * weight
    return (weight - rate * change, moment_new, second_new)


def lane_head(shape, head_size):
    return lax.broadcasted_iota(jnp.int32, shape, len(shape) - 1) // head_size


def turn(values, tables, sign=1.0):
    width = values.shape[-1]
    own, ahead, behind = (jnp.concatenate([table] * (width // table.shape[-1]), 1) for table in tables)
    ahead = pltpu.roll(values, width - ROT // 2, 1) * ahead
    behind = pltpu.roll(values, ROT // 2, 1) * behind
    return values * own + sign * (ahead + behind)


def turn_tables(head_size):
    halfway = ROT // 2
    lane = np.arange(max(128, head_size)) % head_size
    position = np.arange(SEQ).astype(np.float32)
    frequency = np.power(np.float32(10000.0), -2.0 * (lane % halfway).astype(np.float32) / ROT)
    angles = position[:, None] * frequency.astype(np.float32)[None, :]
    cosine, sine = np.cos(angles), np.sin(angles)
    tables = [
        np.where(lane < ROT, cosine, 1.0),
        np.where(lane < halfway, -sine, 0.0),
        np.where((lane >= halfway) & (lane < ROT), sine, 0.0),
    ]
    return jnp.asarray(np.stack(tables).astype(np.float32))


LOG2E = 1.4426950408889634
NT = (((1,), (1,)), ((), ()))
NN = (((1,), (0,)), ((), ()))
TN = (((0,), (0,)), ((), ()))


def mxu(left, right, dims):
    return lax.dot_general(left, right, dims, preferred_element_type=jnp.float32)


def forward_kernel(head_size, lin_ref, bias_ref, table_ref, qkv_ref, out_ref, lse_ref):
    rows, width = out_ref.shape
    low = jnp.bfloat16
    step = min(256, rows)
    for part in range(3):
        for begin in range(0, rows, step):
            here = slice(begin, begin + step)
            values = lin_ref[part, here, :] + bias_ref[part : part + 1, :]
            if part < 2:
                values = turn(values, [table_ref[i, here, :] for i in range(3)])
            qkv_ref[part, here, :] = values.astype(low)
    owner = lane_head((step, width), head_size)
    lanes = lax.broadcasted_iota(jnp.int32, (step, 128), 1)
    for begin in range(0, rows, step):
        end = begin + step
        query = qkv_ref[0, begin:end, :]
        result = jnp.zeros((step, width), jnp.float32)
        logs = jnp.zeros((step, 128), jnp.float32)
        keep = lax.broadcasted_iota(jnp.int32, (step, step), 0) >= lax.broadcasted_iota(
            jnp.int32, (step, step), 1
        )
        for head in range(width // head_size):
            mine = jnp.where(owner == head, query, jnp.zeros_like(query))
            scores = mxu(mine, qkv_ref[1, :end, :], NT)
            last = jnp.where(keep, scores[:, begin:], -1e30)
            scores = jnp.concatenate([scores[:, :begin], last], 1) if begin else last
            top = jnp.max(scores, 1, keepdims=True)
            expo = jnp.exp2((scores - top) * (0.125 * LOG2E))
            total = jnp.sum(expo, 1, keepdims=True)
            found = mxu(expo.astype(low), qkv_ref[2, :end, :], NN)
            result = jnp.where(owner == head, found / total, result)
            logs = jnp.where(lanes == head, top * (0.125 * LOG2E) + jnp.log2(total), logs)
        out_ref[begin:end, :] = result.astype(low)
        lse_ref[:, begin:end] = logs.T[:8]


def attention_forward(lin, bias, head_size):
    _, rows, width = lin.shape
    lanes = min(256, width)
    groups = width // lanes
    tables = turn_tables(head_size)
    low = jnp.bfloat16
    return pl.pallas_call(
        functools.partial(forward_kernel, head_size),
        grid=(rows // SEQ, groups),
        out_shape=(
            jax.ShapeDtypeStruct((3, rows, width), low),
            jax.ShapeDtypeStruct((rows, width), low),
            jax.ShapeDtypeStruct((groups, 8, rows), jnp.float32),
        ),
        in_specs=[
            pl.BlockSpec((3, SEQ, lanes), lambda i, j: (0, i, j)),
            pl.BlockSpec((3, lanes), lambda i, j: (0, j)),
            pl.BlockSpec(tables.shape, lambda i, j: (0, 0, 0)),
        ],
        out_specs=(
            pl.BlockSpec((3, SEQ, lanes), lambda i, j: (0, i, j)),
            pl.BlockSpec((SEQ, lanes), lambda i, j: (i, j)),
            pl.BlockSpec((None, 8, SEQ), lambda i, j: (j, 0, i)),
        ),
        compiler_params=pltpu.CompilerParams(vmem_limit_bytes=48 * 1024 * 1024),
        cost_estimate=pl.CostEstimate(
            flops=rows * SEQ * width * 8, bytes_accessed=rows * width * 26, transcendentals=0
        ),
        name="attend_forward",
    )(lin, bias, tables)


def backward_kernel(head_size, qkv_ref, grad_ref, lse_ref, table_ref, out_ref, sum_ref, acc_ref):
    _, rows, width = qkv_ref.shape
    low = jnp.bfloat16
    step = min(256, rows)
    owner = lane_head((step, width), head_size)
    acc_ref[...] = jnp.zeros_like(acc_ref)
    blank = jnp.zeros((step, width), low)
    for begin in range(0, rows, step):
        end = begin + step
        query = qkv_ref[0, begin:end, :]
        grad = grad_ref[begin:end, :]
        keep = lax.broadcasted_iota(jnp.int32, (step, step), 1) >= lax.broadcasted_iota(
            jnp.int32, (step, step), 0
        )
        query_grad = jnp.zeros((step, width), jnp.float32)
        for head in range(width // head_size):
            mine = jnp.where(owner == head, query, blank)
            grad_mine = jnp.where(owner == head, grad, blank)
            scores = mxu(qkv_ref[1, :end, :], mine, NT)
            expo = jnp.exp2(scores * (0.125 * LOG2E) - lse_ref[head : head + 1, begin:end])
            last = jnp.where(keep, expo[begin:, :], 0.0)
            probs = jnp.concatenate([expo[:begin], last], 0) if begin else last
            prob_grad = mxu(qkv_ref[2, :end, :], grad_mine, NT)
            inner = jnp.sum(probs * prob_grad, 0, keepdims=True)
            score_grad = (probs * (prob_grad - inner)).astype(low)
            acc_ref[0, :end, :] += mxu(score_grad, mine, NN)
            acc_ref[1, :end, :] += mxu(probs.astype(low), grad_mine, NN)
            found = mxu(score_grad, qkv_ref[1, :end, :], TN)
            query_grad = jnp.where(owner == head, found, query_grad)
        turned = turn(0.125 * query_grad, [table_ref[i, begin:end, :] for i in range(3)], -1.0).astype(low)
        out_ref[0, begin:end, :] = turned
        added = jnp.sum(turned.astype(jnp.float32), 0, keepdims=True)
        sum_ref[0:1, :] = added if begin == 0 else sum_ref[0:1, :] + added
    for begin in range(0, rows, step):
        here = slice(begin, begin + step)
        turned = turn(0.125 * acc_ref[0, here, :], [table_ref[i, here, :] for i in range(3)], -1.0).astype(low)
        out_ref[1, here, :] = turned
        added = jnp.sum(turned.astype(jnp.float32), 0, keepdims=True)
        sum_ref[1:2, :] = added if begin == 0 else sum_ref[1:2, :] + added
        turned = acc_ref[1, here, :].astype(low)
        out_ref[2, here, :] = turned
        added = jnp.sum(turned.astype(jnp.float32), 0, keepdims=True)
        sum_ref[2:3, :] = added if begin == 0 else sum_ref[2:3, :] + added


def attention_backward(qkv, grad, logs, head_size):
    _, rows, width = qkv.shape
    lanes = min(256, width)
    groups = width // lanes
    tables = turn_tables(head_size)
    low = jnp.bfloat16
    grads, sums = pl.pallas_call(
        functools.partial(backward_kernel, head_size),
        grid=(rows // SEQ, groups),
        out_shape=(
            jax.ShapeDtypeStruct((3, rows, width), low),
            jax.ShapeDtypeStruct((rows // SEQ, 3, width), jnp.float32),
        ),
        in_specs=[
            pl.BlockSpec((3, SEQ, lanes), lambda i, j: (0, i, j)),
            pl.BlockSpec((SEQ, lanes), lambda i, j: (i, j)),
            pl.BlockSpec((None, 8, SEQ), lambda i, j: (j, 0, i)),
            pl.BlockSpec(tables.shape, lambda i, j: (0, 0, 0)),
        ],
        out_specs=(
            pl.BlockSpec((3, SEQ, lanes), lambda i, j: (0, i, j)),
            pl.BlockSpec((None, 3, lanes), lambda i, j: (i, 0, j)),
        ),
        scratch_shapes=[pltpu.VMEM((2, SEQ, lanes), jnp.float32)],
        compiler_params=pltpu.CompilerParams(vmem_limit_bytes=48 * 1024 * 1024),
        cost_estimate=pl.CostEstimate(
            flops=rows * SEQ * width * 20, bytes_accessed=rows * width * 26, transcendentals=0
        ),
        name="attend_backward",
    )(qkv, grad, logs, tables)
    return grads, jnp.sum(sums, 0)


MESH = pl.DeviceIdType.MESH


def partners():
    me = lax.axis_index("tensor")
    return me, me + 1 - 2 * (me % 2), (me + 2) % 4


def greet(devices):
    barrier = pltpu.get_barrier_semaphore()
    for device in devices:
        pl.semaphore_signal(barrier, inc=1, device_id={"tensor": device}, device_id_type=MESH)
    pl.semaphore_wait(barrier, len(devices))


def gather_kernel(block_ref, whole_ref, send_sem, recv_sem, local_sem):
    me, along_x, along_y = partners()
    rows = block_ref.shape[0]
    half = rows // 2

    def part(owner, which):
        return whole_ref.at[pl.ds(pl.multiple_of(owner * rows + which * half, half), half)]

    def send(source, owner, which, target, index):
        copy = pltpu.make_async_remote_copy(
            src_ref=source,
            dst_ref=part(owner, which),
            send_sem=send_sem.at[index],
            recv_sem=recv_sem.at[index],
            device_id={"tensor": target},
            device_id_type=MESH,
        )
        copy.start()
        return copy

    mine = pltpu.make_async_copy(block_ref, whole_ref.at[pl.ds(pl.multiple_of(me * rows, rows), rows)], local_sem)
    mine.start()
    greet((along_x, along_y))
    halves = [block_ref.at[pl.ds(0, half)], block_ref.at[pl.ds(half, half)]]
    x_first = send(halves[0], me, 0, along_x, 0)
    y_first = send(halves[1], me, 1, along_y, 1)
    x_second = send(halves[1], me, 1, along_x, 2)
    y_second = send(halves[0], me, 0, along_y, 3)
    x_first.wait_recv()
    y_third = send(part(along_x, 0), along_x, 0, along_y, 4)
    y_first.wait_recv()
    x_third = send(part(along_y, 1), along_y, 1, along_x, 5)
    for copy in (x_second, y_second, y_third, x_third):
        copy.wait_recv()
    for copy in (x_first, y_first, x_second, y_second, y_third, x_third):
        copy.wait_send()
    mine.wait()


def square_gather(block):
    rows, width = block.shape
    return pl.pallas_call(
        gather_kernel,
        out_shape=jax.ShapeDtypeStruct((4 * rows, width), block.dtype),
        in_specs=[pl.BlockSpec(memory_space=pltpu.VMEM)],
        out_specs=pl.BlockSpec(memory_space=pl.ANY),
        scratch_shapes=[
            pltpu.SemaphoreType.DMA((6,)),
            pltpu.SemaphoreType.DMA((6,)),
            pltpu.SemaphoreType.DMA,
        ],
        compiler_params=pltpu.CompilerParams(collective_id=0, has_side_effects=True),
        cost_estimate=pl.CostEstimate(flops=0, bytes_accessed=rows * width * 120, transcendentals=0),
        name="square_gather",
    )(block)


def reduce_kernel(terms_ref, ready_ref, out_ref, first_x, first_y, staged, second, send_sem, recv_sem):
    del ready_ref
    me, along_x, along_y = partners()
    rows = out_ref.shape[0]
    half = rows // 2
    corner = 3 - me

    def term(owner, which):
        return terms_ref.at[pl.ds(pl.multiple_of(owner * rows + which * half, half), half)]

    def send(source, target_ref, target, index):
        copy = pltpu.make_async_remote_copy(
            src_ref=source,
            dst_ref=target_ref,
            send_sem=send_sem.at[index],
            recv_sem=recv_sem.at[index],
            device_id={"tensor": target},
            device_id_type=MESH,
        )
        copy.start()
        return copy

    greet((along_x, along_y))
    x_on = send(term(corner, 0), first_x.at[1], along_x, 0)
    y_on = send(term(corner, 1), first_y.at[1], along_y, 1)
    x_own = send(term(along_x, 0), first_x.at[0], along_x, 2)
    y_own = send(term(along_y, 1), first_y.at[0], along_y, 3)

    def added(one, two):
        return (one.astype(jnp.float32) + two.astype(jnp.float32)).astype(jnp.bfloat16)

    x_on.wait_recv()
    staged[0] = added(term(along_y, 0)[...], first_x[1])
    y_last = send(staged.at[0], second.at[0], along_y, 4)
    y_on.wait_recv()
    staged[1] = added(term(along_x, 1)[...], first_y[1])
    x_last = send(staged.at[1], second.at[1], along_x, 5)
    x_own.wait_recv()
    out_ref[:half] = term(me, 0)[...].astype(jnp.float32) + first_x[0].astype(jnp.float32)
    y_own.wait_recv()
    out_ref[half:] = term(me, 1)[...].astype(jnp.float32) + first_y[0].astype(jnp.float32)
    y_last.wait_recv()
    out_ref[:half] += second[0].astype(jnp.float32)
    x_last.wait_recv()
    out_ref[half:] += second[1].astype(jnp.float32)
    for copy in (x_on, y_on, x_own, y_own, y_last, x_last):
        copy.wait_send()


def square_reduce(terms, ready, name):
    rows, width = terms.shape[0] // 4, terms.shape[1]
    part = pltpu.VMEM((2, rows // 2, width), jnp.bfloat16)
    return pl.pallas_call(
        reduce_kernel,
        out_shape=jax.ShapeDtypeStruct((rows, width), jnp.float32),
        in_specs=[pl.BlockSpec(memory_space=pltpu.VMEM), pl.BlockSpec(memory_space=pl.ANY)],
        out_specs=pl.BlockSpec(memory_space=pltpu.VMEM),
        scratch_shapes=[
            part,
            part,
            part,
            part,
            pltpu.SemaphoreType.DMA((6,)),
            pltpu.SemaphoreType.DMA((6,)),
        ],
        compiler_params=pltpu.CompilerParams(
            collective_id=name, has_side_effects=True, vmem_limit_bytes=24 * 1024 * 1024
        ),
        cost_estimate=pl.CostEstimate(flops=0, bytes_accessed=rows * width * 240, transcendentals=0),
        name="square_reduce",
    )(terms, ready)


def start_kernel(
    x_ref, gain_ref, shift_ref, dy_ref, bias_ref, wq_wide, wo_wide, gate_wide, down_wide,
    a_all, dy_all, bias_all, wq_all, wo_all, normed_out, recip_out, gate_out, down_out,
    a_ref, wq_ref, wo_ref, gate_here, down_here,
    square_send, square_recv, bias_send, bias_recv, line_send, line_recv, core_send, core_recv, local_sem,
):
    place, along_x, along_y = partners()
    me = lax.axis_index("dp")
    chip, core = me // 2, me % 2
    sibling = me + 1 - 2 * core
    rows = a_ref.shape[0]
    low = jnp.bfloat16
    half = rows // 2
    depth = wq_ref.shape[1]

    def start(source, target, send_sem, recv_sem, device):
        copy = pltpu.make_async_remote_copy(
            src_ref=source, dst_ref=target, send_sem=send_sem, recv_sem=recv_sem,
            device_id=device, device_id_type=MESH,
        )
        copy.start()
        return copy

    def piece(part, owner):
        if part < 3:
            return wq_all.at[part, pl.ds(pl.multiple_of(owner * depth, depth), depth)]
        width = wo_ref.shape[1]
        return wo_all.at[:, pl.ds(pl.multiple_of(owner * width, width), width)]

    def own(part):
        return wq_ref.at[part] if part < 3 else wo_ref

    def turned(step):
        return 2 * ((chip + step) % 4) + core

    here = [
        pltpu.make_async_copy(gate_wide, gate_here, local_sem.at[6]),
        pltpu.make_async_copy(down_wide, down_here, local_sem.at[7]),
    ]
    for copy in here:
        copy.start()
    wq_ref[...] = wq_wide[...].astype(low)
    wo_ref[...] = wo_wide[...].astype(low)
    bias_all[me] = bias_ref[...]

    barrier = pltpu.get_barrier_semaphore()
    for step in range(1, 8):
        pl.semaphore_signal(barrier, inc=1, device_id={"dp": (me + step) % 8}, device_id_type=MESH)
    for device in (along_x, along_y):
        pl.semaphore_signal(barrier, inc=1, device_id={"tensor": device}, device_id_type=MESH)
    pl.semaphore_wait(barrier, 9)

    def rows_of(whole, owner, which):
        return whole.at[pl.ds(pl.multiple_of(owner * rows + which * half, half), half)]

    def square_first(block, whole, base):
        halves = [block.at[pl.ds(0, half)], block.at[pl.ds(half, half)]]
        plan = [(0, along_x), (1, along_y), (1, along_x), (0, along_y)]
        return [
            start(halves[which], rows_of(whole, place, which), square_send.at[base + i], square_recv.at[base + i], {"tensor": device})
            for i, (which, device) in enumerate(plan)
        ]

    def square_next(whole, base, copies):
        copies[0].wait_recv()
        on_y = start(rows_of(whole, along_x, 0), rows_of(whole, along_x, 0), square_send.at[base + 4], square_recv.at[base + 4], {"tensor": along_y})
        copies[1].wait_recv()
        on_x = start(rows_of(whole, along_y, 1), rows_of(whole, along_y, 1), square_send.at[base + 5], square_recv.at[base + 5], {"tensor": along_x})
        return copies + [on_y, on_x]

    bias_copies = [
        start(bias_all.at[me], bias_all.at[me], bias_send.at[step], bias_recv.at[step], {"dp": (me + step) % 8})
        for step in range(1, 8)
    ]

    def line(part, slot, step, source=None):
        owner = me if source is None else source
        return pltpu.make_async_remote_copy(
            src_ref=own(part) if source is None else piece(part, source),
            dst_ref=piece(part, owner),
            send_sem=line_send.at[part, slot if source is None else 0],
            recv_sem=line_recv.at[part, slot],
            device_id={"dp": turned(step)},
            device_id_type=MESH,
        )

    def to_sibling(part, slot):
        owner = turned(slot)
        return start(
            own(part) if slot == 0 else piece(part, owner), piece(part, owner),
            core_send.at[part, slot], core_recv.at[part, slot], {"dp": sibling},
        )

    for part in range(4):
        line(part, 2, 2).start()

        @pl.when(chip % 2 == 0)
        def _():
            line(part, 3, 1).start()

        @pl.when(chip % 2 == 1)
        def _():
            line(part, 1, 3).start()

    def came(part, slot):
        line(part, slot, 4 - slot).wait_recv()

    def onward(part):
        @pl.when(chip == 2)
        def _():
            line(part, 1, 1, turned(2)).start()
            line(part, 1, 3).start()

        @pl.when(chip == 1)
        def _():
            line(part, 3, 3, turned(2)).start()
            line(part, 3, 1).start()

    siblings = [to_sibling(part, 0) for part in range(4)]
    values = x_ref[...].astype(jnp.float32)
    centred = values - jnp.mean(values, -1, keepdims=True)
    recip = lax.rsqrt(jnp.mean(centred * centred, -1, keepdims=True) + norm_eps)
    recip_out[...] = recip
    normed_out[...] = centred * recip
    a_ref[...] = (normed_out[...] * gain_ref[...] + shift_ref[...]).astype(low)
    a_copies = square_first(a_ref, a_all, 0)
    locals_ = [
        pltpu.make_async_copy(a_ref, a_all.at[pl.ds(pl.multiple_of(place * rows, rows), rows)], local_sem.at[0]),
        pltpu.make_async_copy(dy_ref, dy_all.at[pl.ds(pl.multiple_of(place * rows, rows), rows)], local_sem.at[1]),
    ] + [pltpu.make_async_copy(own(part), piece(part, me), local_sem.at[2 + part]) for part in range(4)]
    for copy in locals_:
        copy.start()
    for copy, source, target in zip(here, (gate_here, down_here), (gate_out, down_out)):
        copy.wait()
        target[...] = source[...].astype(low)
    a_copies = square_next(a_all, 0, a_copies)
    dy_copies = square_first(dy_ref, dy_all, 6)
    for part in range(4):
        came(part, 2)
        onward(part)
        siblings.append(to_sibling(part, 2))
    dy_copies = square_next(dy_all, 6, dy_copies)
    for part in range(4):
        for slot in (1, 3):
            came(part, slot)
            siblings.append(to_sibling(part, slot))
    for copy in a_copies[2:] + dy_copies[2:] + bias_copies + siblings:
        copy.wait_recv()
    for copy in a_copies + dy_copies + bias_copies + siblings:
        copy.wait_send()
    for part in range(4):
        line(part, 2, 2).wait_send()

        @pl.when(chip < 3)
        def _():
            line(part, 3, 1).wait_send()

        @pl.when(chip > 0)
        def _():
            line(part, 1, 3).wait_send()

        @pl.when(chip == 2)
        def _():
            line(part, 1, 1, turned(2)).wait_send()

        @pl.when(chip == 1)
        def _():
            line(part, 3, 3, turned(2)).wait_send()

    for copy in locals_:
        copy.wait()


def start_gather(x, gain, shift, dy, bias, wq, wo, gate, down):
    dma = pltpu.SemaphoreType.DMA
    low, wide = jnp.bfloat16, jnp.float32
    anywhere = pl.BlockSpec(memory_space=pl.ANY)
    local_ = pl.BlockSpec(memory_space=pltpu.VMEM)
    shape = jax.ShapeDtypeStruct
    rows, model = x.shape
    return pl.pallas_call(
        start_kernel,
        out_shape=(
            shape((4 * rows, model), low),
            shape((4 * rows, model), low),
            shape((8, *bias.shape), bias.dtype),
            shape((wq.shape[0], 8 * wq.shape[1], wq.shape[2]), low),
            shape((wo.shape[0], 8 * wo.shape[1]), low),
            shape((rows, model), wide),
            shape((rows, 1), wide),
            shape(gate.shape, low),
            shape(down.shape, low),
        ),
        in_specs=[local_] * 7 + [anywhere] * 2,
        out_specs=(anywhere, anywhere, local_, anywhere, anywhere, local_, local_, local_, local_),
        scratch_shapes=[
            pltpu.VMEM((rows, model), low),
            pltpu.VMEM(wq.shape, low),
            pltpu.VMEM(wo.shape, low),
            pltpu.VMEM(gate.shape, wide),
            pltpu.VMEM(down.shape, wide),
            dma((12,)), dma((12,)), dma((8,)), dma((8,)),
            dma((4, 4)), dma((4, 4)), dma((4, 4)), dma((4, 4)), dma((8,)),
        ],
        compiler_params=pltpu.CompilerParams(
            collective_id=2, has_side_effects=True, vmem_limit_bytes=48 * 1024 * 1024
        ),
        cost_estimate=pl.CostEstimate(flops=0, bytes_accessed=200_000_000, transcendentals=0),
        name="start_gather",
    )(x, gain, shift, dy, bias, wq, wo, gate, down)


def last_kernel(
    first_ref, normed_ref, recip_ref, gain_ref, grad_ref, second_ref, bias_ref, input_out, vector_out, bias_out,
    square_x, square_y, staged, square_last,
    corners, vector_mine, vector_came, vector_slots, bias_mine, bias_came, bias_slots,
    square_send, square_recv, vector_send, vector_recv, bias_send, bias_recv,
):
    place, along_x, along_y = partners()
    corner = 3 - place
    me = lax.axis_index("dp")
    chip, sibling = me // 2, me + 1 - 2 * (me % 2)
    rows = input_out.shape[0]
    half = rows // 2
    low, wide = jnp.bfloat16, jnp.float32

    def start(source, target, send_sem, recv_sem, device):
        copy = pltpu.make_async_remote_copy(
            src_ref=source, dst_ref=target, send_sem=send_sem, recv_sem=recv_sem,
            device_id=device, device_id_type=MESH,
        )
        copy.start()
        return copy

    barrier = pltpu.get_barrier_semaphore()
    chips = [{"dp": (me + 2 * step) % 8} for step in (1, 2, 3)]
    square = [{"tensor": device} for device in (along_x, along_y, corner)]
    for other in square + [{"dp": sibling}] + chips:
        pl.semaphore_signal(barrier, inc=1, device_id=other, device_id_type=MESH)
    pl.semaphore_wait(barrier, 7)

    def term(owner, part):
        return first_ref.at[pl.ds(pl.multiple_of(owner * rows + part * half, half), half)]

    def rows_at(owner, part):
        return term(owner, part)[...].astype(wide)

    plan = [
        (term(corner, 0), square_x.at[1], square[0]),
        (term(corner, 1), square_y.at[1], square[1]),
        (term(along_x, 0), square_x.at[0], square[0]),
        (term(along_y, 1), square_y.at[0], square[1]),
    ]
    copies = [
        start(source, target, square_send.at[i], square_recv.at[i], device)
        for i, (source, target, device) in enumerate(plan)
    ]
    bias_mine[...] = bias_ref[...]
    bias_copies = [start(bias_mine, bias_came, bias_send.at[0], bias_recv.at[0], {"dp": sibling})]
    bias_copies[0].wait_recv()
    bias_slots[chip] = bias_mine[...] + bias_came[...]
    bias_copies += [
        start(bias_slots.at[chip], bias_slots.at[chip], bias_send.at[1 + i], bias_recv.at[1 + i], chips[i])
        for i in range(3)
    ]
    copies[0].wait_recv()
    staged[0] = (rows_at(along_y, 0) + square_x[1].astype(wide)).astype(low)
    copies.append(start(staged.at[0], square_last.at[0], square_send.at[4], square_recv.at[4], square[1]))
    copies[1].wait_recv()
    staged[1] = (rows_at(along_x, 1) + square_y[1].astype(wide)).astype(low)
    copies.append(start(staged.at[1], square_last.at[1], square_send.at[5], square_recv.at[5], square[0]))
    gain = gain_ref[...]
    vector_gain = jnp.zeros_like(gain)
    vector_shift = jnp.zeros_like(gain)
    for part, near in enumerate((square_x, square_y)):
        here = slice(part * half, (part + 1) * half)
        copies[2 + part].wait_recv()
        copies[4 + part].wait_recv()
        grad = rows_at(place, part) + near[0].astype(wide) + square_last[part].astype(wide)
        normed = normed_ref[here, :]
        vector_gain += jnp.sum(grad * normed, 0, keepdims=True)
        vector_shift += jnp.sum(grad, 0, keepdims=True)
        scaled = grad * gain
        inner = (
            scaled
            - jnp.mean(scaled, -1, keepdims=True)
            - normed * jnp.mean(scaled * normed, -1, keepdims=True)
        )
        input_out[here, :] = grad_ref[here, :] + recip_ref[here, :] * inner
    corners[place, 0:1, :] = vector_gain
    corners[place, 1:2, :] = second_ref[0:1, :]
    corners[place, 2:3, :] = vector_shift
    corners[place, 3:4, :] = second_ref[1:2, :]
    vector_copies = [
        start(corners.at[place], corners.at[place], vector_send.at[i], vector_recv.at[i], square[i]) for i in range(3)
    ]
    for copy in vector_copies:
        copy.wait_recv()
    vector_mine[...] = (corners[0] + corners[1]) + (corners[2] + corners[3])
    vector_copies.append(start(vector_mine, vector_came, vector_send.at[3], vector_recv.at[3], {"dp": sibling}))
    vector_copies[3].wait_recv()
    vector_slots[chip] = vector_mine[...] + vector_came[...]
    vector_copies += [
        start(vector_slots.at[chip], vector_slots.at[chip], vector_send.at[4 + i], vector_recv.at[4 + i], chips[i])
        for i in range(3)
    ]
    for copy in vector_copies[4:] + bias_copies[1:]:
        copy.wait_recv()
    vector_out[...] = (vector_slots[0] + vector_slots[1]) + (vector_slots[2] + vector_slots[3])
    bias_out[...] = (bias_slots[0] + bias_slots[1]) + (bias_slots[2] + bias_slots[3])
    for copy in copies + vector_copies + bias_copies:
        copy.wait_send()


def last_reduce(first, normed, recip, gain, grad, second, bias):
    dma = pltpu.SemaphoreType.DMA
    low, wide = jnp.bfloat16, jnp.float32
    shape, vmem = jax.ShapeDtypeStruct, pltpu.VMEM
    rows, model = normed.shape
    pair = vmem((2, rows // 2, model), low)
    return pl.pallas_call(
        last_kernel,
        out_shape=(shape((rows, model), wide), shape((4, model), wide), shape(bias.shape, wide)),
        in_specs=[pl.BlockSpec(memory_space=pltpu.VMEM)] * 7,
        out_specs=(pl.BlockSpec(memory_space=pltpu.VMEM),) * 3,
        scratch_shapes=[
            pair, pair, pair, pair,
            vmem((4, 4, model), wide),
            vmem((4, model), wide),
            vmem((4, model), wide),
            vmem((4, 4, model), wide),
            vmem(bias.shape, wide),
            vmem(bias.shape, wide),
            vmem((4, *bias.shape), wide),
            dma((6,)), dma((6,)), dma((7,)), dma((7,)), dma((4,)), dma((4,)),
        ],
        compiler_params=pltpu.CompilerParams(
            collective_id=3, has_side_effects=True, vmem_limit_bytes=40 * 1024 * 1024
        ),
        cost_estimate=pl.CostEstimate(flops=0, bytes_accessed=120_000_000, transcendentals=0),
        name="last_reduce",
    )(first, normed, recip, gain, grad, second, bias)


def after(late, early):
    return lax.optimization_barrier((late, early))[0]


class Plain:
    def gather_rows(self, block):
        return lax.all_gather(block, "tensor", axis=0, tiled=True)

    def reduce_rows(self, terms, ready, name):
        return lax.psum_scatter(terms, "tensor", scatter_dimension=0, tiled=True).astype(jnp.float32)

    def begin(self, x, gain, shift, dy, bias, w_qkv, w_output, gate_up, down):
        low = jnp.bfloat16
        out, normed, recip = layer_norm(x.astype(jnp.float32), gain, shift)
        return (
            self.gather_rows(out.astype(low)),
            self.gather_rows(dy),
            lax.all_gather(bias, "dp", axis=2, tiled=True),
            gather_dp(w_qkv.astype(low), 1),
            gather_dp(w_output.astype(low), 1),
            normed,
            recip,
            gate_up.astype(low),
            down.astype(low),
        )

    def finish(self, first, normed, recip, gain, grad, second, bias):
        first = self.reduce_rows(first, None, 0)
        vectors = jnp.stack([jnp.sum(first * normed, 0), second[0], jnp.sum(first, 0), second[1]])
        input_grad = grad + norm_back(first, normed, recip, gain)
        return input_grad, lax.psum(vectors, ("dp", "tensor")), lax.psum(bias, "dp")


class Line(Plain):
    def gather_rows(self, block):
        return square_gather(block)

    def reduce_rows(self, terms, ready, name):
        return square_reduce(terms, ready, name)

    def begin(self, x, gain, shift, dy, bias, w_qkv, w_output, gate_up, down):
        parts, heads, few = bias.shape
        a, dy, came, *others = start_gather(
            x, gain.reshape(1, -1), shift.reshape(1, -1), dy, self.flat(bias), w_qkv, w_output, gate_up, down
        )
        came = came.reshape(8, -1)[:, : parts * heads * few].reshape(8, parts, heads, few)
        return a, dy, came.transpose(1, 2, 0, 3).reshape(parts, heads, -1), *others

    def flat(self, values):
        values = values.astype(jnp.float32).reshape(-1)
        width = -(-values.shape[0] // 1024) * 1024
        return jnp.pad(values, (0, width - values.shape[0])).reshape(8, -1)

    def finish(self, first, normed, recip, gain, grad, second, bias):
        input_grad, vectors, total = last_reduce(
            first, normed, recip, gain.reshape(1, -1), grad, second, self.flat(bias)
        )
        return input_grad, vectors, total.reshape(-1)[: bias.size].reshape(bias.shape)


def row_major(values):
    return with_layout_constraint(values, Layout(tuple(range(values.ndim))))


def gather_dp(block, axis):
    return row_major(lax.all_gather(block.astype(jnp.bfloat16), "dp", axis=axis, tiled=True))


def scatter_dp(terms, axis):
    return lax.psum_scatter(terms.astype(jnp.bfloat16), "dp", scatter_dimension=axis, tiled=True)


def local(
    routes,
    inputs,
    cotangent,
    gains,
    shifts,
    qkv_weight,
    biases,
    out_weight,
    gate_up,
    down_weight,
    momentum_gains,
    momentum_shifts,
    momentum_qkv,
    momentum_biases,
    momentum_out,
    momentum_gate,
    momentum_down,
    variance_gains,
    variance_shifts,
    variance_qkv,
    variance_biases,
    variance_out,
    variance_gate,
    variance_down,
):
    low = jnp.bfloat16
    local_heads = biases.shape[1]
    local_width = qkv_weight.shape[2]
    head_size = local_width // local_heads
    xin = inputs.astype(jnp.float32)
    a_all, dy_all, bias_all, w_qkv, w_output, first_normed, first_recip, gate_low, down_low = routes.begin(
        inputs, gains[0], shifts[0], cotangent, biases.astype(low), qkv_weight, out_weight, gate_up, down_weight
    )
    bias_all = bias_all.reshape(3, local_width).astype(jnp.float32)
    w_gate_up = gather_dp(after(gate_low, w_output), 1)
    lin = jnp.einsum("rd,kdc->krc", a_all, w_qkv, preferred_element_type=jnp.float32)
    qkv, heads, logs = attention_forward(lin, bias_all, head_size)
    resid = xin + routes.reduce_rows(mxu(heads, w_output, NN).astype(low), logs, 4)
    second_out, second_normed, second_recip = layer_norm(resid, gains[1], shifts[1])
    m_all = routes.gather_rows(second_out.astype(low))
    w_down = gather_dp(after(down_low, (w_gate_up, m_all)), 1)
    gate_vals = jnp.einsum("rd,kdc->krc", m_all, w_gate_up, preferred_element_type=jnp.float32)
    gate_lin, upward = gate_vals[0], gate_vals[1]
    sigmoid_gate = jax.nn.sigmoid(gate_lin)
    silu_gate = gate_lin * sigmoid_gate
    hidden = (silu_gate * upward).astype(low)
    down_terms = mxu(hidden, dy_all, TN).astype(low)
    down_grad = scatter_dp(down_terms, 1)
    w_down = after(w_down, down_terms)
    hidden_grad = mxu(dy_all, w_down, NT)
    gate_grad_low = (
        hidden_grad * upward * sigmoid_gate * (1.0 + gate_lin * (1.0 - sigmoid_gate))
    ).astype(low)
    up_grad_low = (hidden_grad * silu_gate).astype(low)
    both_grads = jnp.stack([gate_grad_low, up_grad_low], 0)
    gate_terms = jnp.einsum("rd,krc->kdc", m_all, both_grads, preferred_element_type=jnp.float32)
    gate_terms = row_major(gate_terms.astype(low))
    second_terms = jnp.einsum(
        "krc,kdc->rd", both_grads, w_gate_up, preferred_element_type=jnp.float32
    ).astype(low)
    block_terms = mxu(hidden, w_down, NN).astype(low)
    gate_grad = scatter_dp(after(gate_terms, (down_grad, second_terms, block_terms)), 1)
    second_grad = routes.reduce_rows(second_terms, down_grad, 5)
    resid_grad = cotangent.astype(jnp.float32) + norm_back(
        second_grad, second_normed, second_recip, gains[1]
    )
    gain_second = jnp.sum(second_grad * second_normed, 0)
    shift_second = jnp.sum(second_grad, 0)
    resid_full = routes.gather_rows(resid_grad.astype(low))
    out_terms = mxu(heads, resid_full, TN).astype(low)
    heads_grad = mxu(resid_full, w_output, NT).astype(low)
    lin_grads, bias_terms = attention_backward(qkv, heads_grad, logs, head_size)
    qkv_terms = jnp.einsum("rd,krc->kdc", a_all, lin_grads, preferred_element_type=jnp.float32)
    qkv_terms = row_major(qkv_terms.astype(low))
    first_terms = jnp.einsum(
        "krc,kdc->rd", lin_grads, w_qkv, preferred_element_type=jnp.float32
    ).astype(low)
    out_grad = scatter_dp(after(out_terms, (gate_grad, qkv_terms)), 1)
    down_sum = routes.reduce_rows(block_terms, qkv_terms, 6)
    qkv_grad = scatter_dp(after(qkv_terms, (out_grad, down_sum)), 1)
    block_out = (resid + down_sum).astype(low)
    input_grad, vectors, bias_sum = routes.finish(
        after(first_terms, down_sum),
        first_normed,
        first_recip,
        gains[0],
        resid_grad,
        jnp.stack([gain_second, shift_second]),
        bias_terms,
    )
    gains_grad, shifts_grad = vectors[:2], vectors[2:]
    down_grad, gate_grad, out_grad = (
        grad.astype(jnp.float32) for grad in after((down_grad, gate_grad, out_grad), vectors)
    )
    qkv_grad = qkv_grad.astype(jnp.float32)
    per_dp = biases.shape[2]
    biases_grad = lax.dynamic_slice_in_dim(
        bias_sum.reshape(3, local_heads, head_size), lax.axis_index("dp") * per_dp, per_dp, 2
    )
    gain_new = adamw(gains, gains_grad, momentum_gains, variance_gains, 0.0, vector_rate)
    shift_new = adamw(shifts, shifts_grad, momentum_shifts, variance_shifts, 0.0, vector_rate)
    qkv_new = adamw(qkv_weight, qkv_grad, momentum_qkv, variance_qkv, decay_rate, learn_rate)
    bias_new = adamw(biases, biases_grad, momentum_biases, variance_biases, 0.0, vector_rate)
    out_new = adamw(out_weight, out_grad, momentum_out, variance_out, decay_rate, learn_rate)
    gate_new = adamw(gate_up, gate_grad, momentum_gate, variance_gate, decay_rate, learn_rate)
    down_new = adamw(down_weight, down_grad, momentum_down, variance_down, decay_rate, learn_rate)
    return (
        block_out,
        input_grad,
        gains_grad,
        shifts_grad,
        qkv_grad,
        biases_grad,
        out_grad,
        gate_grad,
        down_grad,
        gain_new[0],
        shift_new[0],
        qkv_new[0],
        bias_new[0],
        out_new[0],
        gate_new[0],
        down_new[0],
        gain_new[1],
        shift_new[1],
        qkv_new[1],
        bias_new[1],
        out_new[1],
        gate_new[1],
        down_new[1],
        gain_new[2],
        shift_new[2],
        qkv_new[2],
        bias_new[2],
        out_new[2],
        gate_new[2],
        down_new[2],
    )


def solution(mesh):
    routes = Line() if dict(mesh.shape) == {"dp": 8, "tensor": 4} else Plain()

    def step(*arrays):
        return local(routes, *arrays)

    return jax.shard_map(
        step,
        mesh=mesh,
        in_specs=(
            P(("dp", "tensor"), None),
            P(("dp", "tensor"), None),
            P(),
            P(),
            P(None, "dp", "tensor"),
            P(None, "tensor", "dp"),
            P("tensor", "dp"),
            P(None, "dp", "tensor"),
            P("tensor", "dp"),
            P(),
            P(),
            P(None, "dp", "tensor"),
            P(None, "tensor", "dp"),
            P("tensor", "dp"),
            P(None, "dp", "tensor"),
            P("tensor", "dp"),
            P(),
            P(),
            P(None, "dp", "tensor"),
            P(None, "tensor", "dp"),
            P("tensor", "dp"),
            P(None, "dp", "tensor"),
            P("tensor", "dp"),
        ),
        out_specs=(
            P(("dp", "tensor"), None),
            P(("dp", "tensor"), None),
            P(),
            P(),
            P(None, "dp", "tensor"),
            P(None, "tensor", "dp"),
            P("tensor", "dp"),
            P(None, "dp", "tensor"),
            P("tensor", "dp"),
            P(),
            P(),
            P(None, "dp", "tensor"),
            P(None, "tensor", "dp"),
            P("tensor", "dp"),
            P(None, "dp", "tensor"),
            P("tensor", "dp"),
            P(),
            P(),
            P(None, "dp", "tensor"),
            P(None, "tensor", "dp"),
            P("tensor", "dp"),
            P(None, "dp", "tensor"),
            P("tensor", "dp"),
            P(),
            P(),
            P(None, "dp", "tensor"),
            P(None, "tensor", "dp"),
            P("tensor", "dp"),
            P(None, "dp", "tensor"),
            P("tensor", "dp"),
        ),
        check_vma=False,
    )
```

```python
import functools

import jax
import jax.numpy as jnp
import numpy as np
from jax import lax
from jax.experimental import pallas as pl
from jax.experimental.layout import Layout, with_layout_constraint
from jax.experimental.pallas import tpu as pltpu
from jax.sharding import PartitionSpec as P

ROT = 16
SEQ = 1024
ADAM_STEP = 3


norm_eps = 1e-05
learn_rate = 0.03
vector_rate = 0.25
decay_rate = 0.1
adam_eps = 1e-08


def layer_norm(values, gain, shift):
    centred = values - jnp.mean(values, -1, keepdims=True)
    recip = lax.rsqrt(jnp.mean(centred * centred, -1, keepdims=True) + norm_eps)
    normed = centred * recip
    return (normed * gain + shift, normed, recip)


def norm_back(grad, normed, recip, gain):
    scaled = grad * gain
    inner = (
        scaled
        - jnp.mean(scaled, -1, keepdims=True)
        - normed * jnp.mean(scaled * normed, -1, keepdims=True)
    )
    return recip * inner


def adamw(weight, grad, moment, second, decay, rate):
    moment_new = 0.9 * moment + 0.1 * grad
    second_new = 0.95 * second + 0.05 * grad * grad
    fixed_one = 1.0 - 0.9**ADAM_STEP
    fixed_two = 1.0 - 0.95**ADAM_STEP
    change = moment_new / fixed_one / (jnp.sqrt(second_new / fixed_two) + adam_eps) + decay * weight
    return (weight - rate * change, moment_new, second_new)


def lane_head(shape, head_size):
    return lax.broadcasted_iota(jnp.int32, shape, len(shape) - 1) // head_size


def turn(values, tables, sign=1.0):
    width = values.shape[-1]
    own, ahead, behind = (jnp.concatenate([table] * (width // table.shape[-1]), 1) for table in tables)
    ahead = pltpu.roll(values, width - ROT // 2, 1) * ahead
    behind = pltpu.roll(values, ROT // 2, 1) * behind
    return values * own + sign * (ahead + behind)


def turn_tables(head_size):
    halfway = ROT // 2
    lane = np.arange(max(128, head_size)) % head_size
    position = np.arange(SEQ).astype(np.float32)
    frequency = np.power(np.float32(10000.0), -2.0 * (lane % halfway).astype(np.float32) / ROT)
    angles = position[:, None] * frequency.astype(np.float32)[None, :]
    cosine, sine = np.cos(angles), np.sin(angles)
    tables = [
        np.where(lane < ROT, cosine, 1.0),
        np.where(lane < halfway, -sine, 0.0),
        np.where((lane >= halfway) & (lane < ROT), sine, 0.0),
    ]
    return jnp.asarray(np.stack(tables).astype(np.float32))


LOG2E = 1.4426950408889634
NT = (((1,), (1,)), ((), ()))
NN = (((1,), (0,)), ((), ()))
TN = (((0,), (0,)), ((), ()))


def mxu(left, right, dims):
    return lax.dot_general(left, right, dims, preferred_element_type=jnp.float32)


def forward_kernel(head_size, lin_ref, bias_ref, table_ref, qkv_ref, out_ref, lse_ref):
    rows, width = out_ref.shape
    low = jnp.bfloat16
    step = min(256, rows)
    for part in range(3):
        for begin in range(0, rows, step):
            here = slice(begin, begin + step)
            values = lin_ref[part, here, :] + bias_ref[part : part + 1, :]
            if part < 2:
                values = turn(values, [table_ref[i, here, :] for i in range(3)])
            qkv_ref[part, here, :] = values.astype(low)
    owner = lane_head((step, width), head_size)
    lanes = lax.broadcasted_iota(jnp.int32, (step, 128), 1)
    for begin in range(0, rows, step):
        end = begin + step
        query = qkv_ref[0, begin:end, :]
        result = jnp.zeros((step, width), jnp.float32)
        logs = jnp.zeros((step, 128), jnp.float32)
        keep = lax.broadcasted_iota(jnp.int32, (step, step), 0) >= lax.broadcasted_iota(
            jnp.int32, (step, step), 1
        )
        for head in range(width // head_size):
            mine = jnp.where(owner == head, query, jnp.zeros_like(query))
            scores = mxu(mine, qkv_ref[1, :end, :], NT)
            last = jnp.where(keep, scores[:, begin:], -1e30)
            scores = jnp.concatenate([scores[:, :begin], last], 1) if begin else last
            top = jnp.max(scores, 1, keepdims=True)
            expo = jnp.exp2((scores - top) * (0.125 * LOG2E))
            total = jnp.sum(expo, 1, keepdims=True)
            found = mxu(expo.astype(low), qkv_ref[2, :end, :], NN)
            result = jnp.where(owner == head, found / total, result)
            logs = jnp.where(lanes == head, top * (0.125 * LOG2E) + jnp.log2(total), logs)
        out_ref[begin:end, :] = result.astype(low)
        lse_ref[:, begin:end] = logs.T[:8]


def attention_forward(lin, bias, head_size):
    _, rows, width = lin.shape
    lanes = min(256, width)
    groups = width // lanes
    tables = turn_tables(head_size)
    low = jnp.bfloat16
    return pl.pallas_call(
        functools.partial(forward_kernel, head_size),
        grid=(rows // SEQ, groups),
        out_shape=(
            jax.ShapeDtypeStruct((3, rows, width), low),
            jax.ShapeDtypeStruct((rows, width), low),
            jax.ShapeDtypeStruct((groups, 8, rows), jnp.float32),
        ),
        in_specs=[
            pl.BlockSpec((3, SEQ, lanes), lambda i, j: (0, i, j)),
            pl.BlockSpec((3, lanes), lambda i, j: (0, j)),
            pl.BlockSpec(tables.shape, lambda i, j: (0, 0, 0)),
        ],
        out_specs=(
            pl.BlockSpec((3, SEQ, lanes), lambda i, j: (0, i, j)),
            pl.BlockSpec((SEQ, lanes), lambda i, j: (i, j)),
            pl.BlockSpec((None, 8, SEQ), lambda i, j: (j, 0, i)),
        ),
        compiler_params=pltpu.CompilerParams(vmem_limit_bytes=48 * 1024 * 1024),
        cost_estimate=pl.CostEstimate(
            flops=rows * SEQ * width * 8, bytes_accessed=rows * width * 26, transcendentals=0
        ),
        name="attend_forward",
    )(lin, bias, tables)


def backward_kernel(head_size, qkv_ref, grad_ref, lse_ref, table_ref, out_ref, sum_ref, acc_ref):
    _, rows, width = qkv_ref.shape
    low = jnp.bfloat16
    step = min(256, rows)
    owner = lane_head((step, width), head_size)
    acc_ref[...] = jnp.zeros_like(acc_ref)
    blank = jnp.zeros((step, width), low)
    for begin in range(0, rows, step):
        end = begin + step
        query = qkv_ref[0, begin:end, :]
        grad = grad_ref[begin:end, :]
        keep = lax.broadcasted_iota(jnp.int32, (step, step), 1) >= lax.broadcasted_iota(
            jnp.int32, (step, step), 0
        )
        query_grad = jnp.zeros((step, width), jnp.float32)
        for head in range(width // head_size):
            mine = jnp.where(owner == head, query, blank)
            grad_mine = jnp.where(owner == head, grad, blank)
            scores = mxu(qkv_ref[1, :end, :], mine, NT)
            expo = jnp.exp2(scores * (0.125 * LOG2E) - lse_ref[head : head + 1, begin:end])
            last = jnp.where(keep, expo[begin:, :], 0.0)
            probs = jnp.concatenate([expo[:begin], last], 0) if begin else last
            prob_grad = mxu(qkv_ref[2, :end, :], grad_mine, NT)
            inner = jnp.sum(probs * prob_grad, 0, keepdims=True)
            score_grad = (probs * (prob_grad - inner)).astype(low)
            acc_ref[0, :end, :] += mxu(score_grad, mine, NN)
            acc_ref[1, :end, :] += mxu(probs.astype(low), grad_mine, NN)
            found = mxu(score_grad, qkv_ref[1, :end, :], TN)
            query_grad = jnp.where(owner == head, found, query_grad)
        turned = turn(0.125 * query_grad, [table_ref[i, begin:end, :] for i in range(3)], -1.0).astype(low)
        out_ref[0, begin:end, :] = turned
        added = jnp.sum(turned.astype(jnp.float32), 0, keepdims=True)
        sum_ref[0:1, :] = added if begin == 0 else sum_ref[0:1, :] + added
    for begin in range(0, rows, step):
        here = slice(begin, begin + step)
        turned = turn(0.125 * acc_ref[0, here, :], [table_ref[i, here, :] for i in range(3)], -1.0).astype(low)
        out_ref[1, here, :] = turned
        added = jnp.sum(turned.astype(jnp.float32), 0, keepdims=True)
        sum_ref[1:2, :] = added if begin == 0 else sum_ref[1:2, :] + added
        turned = acc_ref[1, here, :].astype(low)
        out_ref[2, here, :] = turned
        added = jnp.sum(turned.astype(jnp.float32), 0, keepdims=True)
        sum_ref[2:3, :] = added if begin == 0 else sum_ref[2:3, :] + added


def attention_backward(qkv, grad, logs, head_size):
    _, rows, width = qkv.shape
    lanes = min(256, width)
    groups = width // lanes
    tables = turn_tables(head_size)
    low = jnp.bfloat16
    grads, sums = pl.pallas_call(
        functools.partial(backward_kernel, head_size),
        grid=(rows // SEQ, groups),
        out_shape=(
            jax.ShapeDtypeStruct((3, rows, width), low),
            jax.ShapeDtypeStruct((rows // SEQ, 3, width), jnp.float32),
        ),
        in_specs=[
            pl.BlockSpec((3, SEQ, lanes), lambda i, j: (0, i, j)),
            pl.BlockSpec((SEQ, lanes), lambda i, j: (i, j)),
            pl.BlockSpec((None, 8, SEQ), lambda i, j: (j, 0, i)),
            pl.BlockSpec(tables.shape, lambda i, j: (0, 0, 0)),
        ],
        out_specs=(
            pl.BlockSpec((3, SEQ, lanes), lambda i, j: (0, i, j)),
            pl.BlockSpec((None, 3, lanes), lambda i, j: (i, 0, j)),
        ),
        scratch_shapes=[pltpu.VMEM((2, SEQ, lanes), jnp.float32)],
        compiler_params=pltpu.CompilerParams(vmem_limit_bytes=48 * 1024 * 1024),
        cost_estimate=pl.CostEstimate(
            flops=rows * SEQ * width * 20, bytes_accessed=rows * width * 26, transcendentals=0
        ),
        name="attend_backward",
    )(qkv, grad, logs, tables)
    return grads, jnp.sum(sums, 0)


MESH = pl.DeviceIdType.MESH


def partners():
    me = lax.axis_index("tensor")
    return me, me + 1 - 2 * (me % 2), (me + 2) % 4


def greet(devices):
    barrier = pltpu.get_barrier_semaphore()
    for device in devices:
        pl.semaphore_signal(barrier, inc=1, device_id={"tensor": device}, device_id_type=MESH)
    pl.semaphore_wait(barrier, len(devices))


def gather_kernel(block_ref, whole_ref, send_sem, recv_sem, local_sem):
    me, along_x, along_y = partners()
    rows = block_ref.shape[0]
    half = rows // 2

    def part(owner, which):
        return whole_ref.at[pl.ds(pl.multiple_of(owner * rows + which * half, half), half)]

    def send(source, owner, which, target, index):
        copy = pltpu.make_async_remote_copy(
            src_ref=source,
            dst_ref=part(owner, which),
            send_sem=send_sem.at[index],
            recv_sem=recv_sem.at[index],
            device_id={"tensor": target},
            device_id_type=MESH,
        )
        copy.start()
        return copy

    mine = pltpu.make_async_copy(block_ref, whole_ref.at[pl.ds(pl.multiple_of(me * rows, rows), rows)], local_sem)
    mine.start()
    greet((along_x, along_y))
    halves = [block_ref.at[pl.ds(0, half)], block_ref.at[pl.ds(half, half)]]
    x_first = send(halves[0], me, 0, along_x, 0)
    y_first = send(halves[1], me, 1, along_y, 1)
    x_second = send(halves[1], me, 1, along_x, 2)
    y_second = send(halves[0], me, 0, along_y, 3)
    x_first.wait_recv()
    y_third = send(part(along_x, 0), along_x, 0, along_y, 4)
    y_first.wait_recv()
    x_third = send(part(along_y, 1), along_y, 1, along_x, 5)
    for copy in (x_second, y_second, y_third, x_third):
        copy.wait_recv()
    for copy in (x_first, y_first, x_second, y_second, y_third, x_third):
        copy.wait_send()
    mine.wait()


def square_gather(block):
    rows, width = block.shape
    return pl.pallas_call(
        gather_kernel,
        out_shape=jax.ShapeDtypeStruct((4 * rows, width), block.dtype),
        in_specs=[pl.BlockSpec(memory_space=pltpu.VMEM)],
        out_specs=pl.BlockSpec(memory_space=pl.ANY),
        scratch_shapes=[
            pltpu.SemaphoreType.DMA((6,)),
            pltpu.SemaphoreType.DMA((6,)),
            pltpu.SemaphoreType.DMA,
        ],
        compiler_params=pltpu.CompilerParams(collective_id=0, has_side_effects=True),
        cost_estimate=pl.CostEstimate(flops=0, bytes_accessed=rows * width * 120, transcendentals=0),
        name="square_gather",
    )(block)


def reduce_kernel(terms_ref, ready_ref, out_ref, first_x, first_y, staged, second, send_sem, recv_sem):
    del ready_ref
    me, along_x, along_y = partners()
    rows = out_ref.shape[0]
    half = rows // 2
    corner = 3 - me

    def term(owner, which):
        return terms_ref.at[pl.ds(pl.multiple_of(owner * rows + which * half, half), half)]

    def send(source, target_ref, target, index):
        copy = pltpu.make_async_remote_copy(
            src_ref=source,
            dst_ref=target_ref,
            send_sem=send_sem.at[index],
            recv_sem=recv_sem.at[index],
            device_id={"tensor": target},
            device_id_type=MESH,
        )
        copy.start()
        return copy

    greet((along_x, along_y))
    x_on = send(term(corner, 0), first_x.at[1], along_x, 0)
    y_on = send(term(corner, 1), first_y.at[1], along_y, 1)
    x_own = send(term(along_x, 0), first_x.at[0], along_x, 2)
    y_own = send(term(along_y, 1), first_y.at[0], along_y, 3)

    def added(one, two):
        return (one.astype(jnp.float32) + two.astype(jnp.float32)).astype(jnp.bfloat16)

    x_on.wait_recv()
    staged[0] = added(term(along_y, 0)[...], first_x[1])
    y_last = send(staged.at[0], second.at[0], along_y, 4)
    y_on.wait_recv()
    staged[1] = added(term(along_x, 1)[...], first_y[1])
    x_last = send(staged.at[1], second.at[1], along_x, 5)
    x_own.wait_recv()
    out_ref[:half] = term(me, 0)[...].astype(jnp.float32) + first_x[0].astype(jnp.float32)
    y_own.wait_recv()
    out_ref[half:] = term(me, 1)[...].astype(jnp.float32) + first_y[0].astype(jnp.float32)
    y_last.wait_recv()
    out_ref[:half] += second[0].astype(jnp.float32)
    x_last.wait_recv()
    out_ref[half:] += second[1].astype(jnp.float32)
    for copy in (x_on, y_on, x_own, y_own, y_last, x_last):
        copy.wait_send()


def square_reduce(terms, ready, name):
    rows, width = terms.shape[0] // 4, terms.shape[1]
    part = pltpu.VMEM((2, rows // 2, width), jnp.bfloat16)
    return pl.pallas_call(
        reduce_kernel,
        out_shape=jax.ShapeDtypeStruct((rows, width), jnp.float32),
        in_specs=[pl.BlockSpec(memory_space=pltpu.VMEM), pl.BlockSpec(memory_space=pl.ANY)],
        out_specs=pl.BlockSpec(memory_space=pltpu.VMEM),
        scratch_shapes=[
            part,
            part,
            part,
            part,
            pltpu.SemaphoreType.DMA((6,)),
            pltpu.SemaphoreType.DMA((6,)),
        ],
        compiler_params=pltpu.CompilerParams(
            collective_id=name, has_side_effects=True, vmem_limit_bytes=24 * 1024 * 1024
        ),
        cost_estimate=pl.CostEstimate(flops=0, bytes_accessed=rows * width * 240, transcendentals=0),
        name="square_reduce",
    )(terms, ready)


def start_kernel(
    x_ref, gain_ref, shift_ref, dy_ref, bias_ref, wq_wide, wo_wide, gate_wide, down_wide,
    a_all, dy_all, bias_all, wq_all, wo_all, normed_out, recip_out, gate_out, down_out,
    a_ref, wq_ref, wo_ref, gate_here, down_here,
    square_send, square_recv, bias_send, bias_recv, line_send, line_recv, core_send, core_recv, local_sem,
):
    place, along_x, along_y = partners()
    me = lax.axis_index("dp")
    chip, core = me // 2, me % 2
    sibling = me + 1 - 2 * core
    rows = a_ref.shape[0]
    low = jnp.bfloat16
    half = rows // 2
    depth = wq_ref.shape[1]

    def start(source, target, send_sem, recv_sem, device):
        copy = pltpu.make_async_remote_copy(
            src_ref=source, dst_ref=target, send_sem=send_sem, recv_sem=recv_sem,
            device_id=device, device_id_type=MESH,
        )
        copy.start()
        return copy

    def piece(part, owner):
        if part < 3:
            return wq_all.at[part, pl.ds(pl.multiple_of(owner * depth, depth), depth)]
        width = wo_ref.shape[1]
        return wo_all.at[:, pl.ds(pl.multiple_of(owner * width, width), width)]

    def own(part):
        return wq_ref.at[part] if part < 3 else wo_ref

    def turned(step):
        return 2 * ((chip + step) % 4) + core

    here = [
        pltpu.make_async_copy(gate_wide, gate_here, local_sem.at[6]),
        pltpu.make_async_copy(down_wide, down_here, local_sem.at[7]),
    ]
    for copy in here:
        copy.start()
    wq_ref[...] = wq_wide[...].astype(low)
    wo_ref[...] = wo_wide[...].astype(low)
    bias_all[me] = bias_ref[...]

    barrier = pltpu.get_barrier_semaphore()
    for step in range(1, 8):
        pl.semaphore_signal(barrier, inc=1, device_id={"dp": (me + step) % 8}, device_id_type=MESH)
    for device in (along_x, along_y):
        pl.semaphore_signal(barrier, inc=1, device_id={"tensor": device}, device_id_type=MESH)
    pl.semaphore_wait(barrier, 9)

    def rows_of(whole, owner, which):
        return whole.at[pl.ds(pl.multiple_of(owner * rows + which * half, half), half)]

    def square_first(block, whole, base):
        halves = [block.at[pl.ds(0, half)], block.at[pl.ds(half, half)]]
        plan = [(0, along_x), (1, along_y), (1, along_x), (0, along_y)]
        return [
            start(halves[which], rows_of(whole, place, which), square_send.at[base + i], square_recv.at[base + i], {"tensor": device})
            for i, (which, device) in enumerate(plan)
        ]

    def square_next(whole, base, copies):
        copies[0].wait_recv()
        on_y = start(rows_of(whole, along_x, 0), rows_of(whole, along_x, 0), square_send.at[base + 4], square_recv.at[base + 4], {"tensor": along_y})
        copies[1].wait_recv()
        on_x = start(rows_of(whole, along_y, 1), rows_of(whole, along_y, 1), square_send.at[base + 5], square_recv.at[base + 5], {"tensor": along_x})
        return copies + [on_y, on_x]

    bias_copies = [
        start(bias_all.at[me], bias_all.at[me], bias_send.at[step], bias_recv.at[step], {"dp": (me + step) % 8})
        for step in range(1, 8)
    ]

    def line(part, slot, step, source=None):
        owner = me if source is None else source
        return pltpu.make_async_remote_copy(
            src_ref=own(part) if source is None else piece(part, source),
            dst_ref=piece(part, owner),
            send_sem=line_send.at[part, slot if source is None else 0],
            recv_sem=line_recv.at[part, slot],
            device_id={"dp": turned(step)},
            device_id_type=MESH,
        )

    def to_sibling(part, slot):
        owner = turned(slot)
        return start(
            own(part) if slot == 0 else piece(part, owner), piece(part, owner),
            core_send.at[part, slot], core_recv.at[part, slot], {"dp": sibling},
        )

    for part in range(4):
        line(part, 2, 2).start()

        @pl.when(chip % 2 == 0)
        def _():
            line(part, 3, 1).start()

        @pl.when(chip % 2 == 1)
        def _():
            line(part, 1, 3).start()

    def came(part, slot):
        line(part, slot, 4 - slot).wait_recv()

    def onward(part):
        @pl.when(chip == 2)
        def _():
            line(part, 1, 1, turned(2)).start()
            line(part, 1, 3).start()

        @pl.when(chip == 1)
        def _():
            line(part, 3, 3, turned(2)).start()
            line(part, 3, 1).start()

    siblings = [to_sibling(part, 0) for part in range(4)]
    values = x_ref[...].astype(jnp.float32)
    centred = values - jnp.mean(values, -1, keepdims=True)
    recip = lax.rsqrt(jnp.mean(centred * centred, -1, keepdims=True) + norm_eps)
    recip_out[...] = recip
    normed_out[...] = centred * recip
    a_ref[...] = (normed_out[...] * gain_ref[...] + shift_ref[...]).astype(low)
    a_copies = square_first(a_ref, a_all, 0)
    locals_ = [
        pltpu.make_async_copy(a_ref, a_all.at[pl.ds(pl.multiple_of(place * rows, rows), rows)], local_sem.at[0]),
        pltpu.make_async_copy(dy_ref, dy_all.at[pl.ds(pl.multiple_of(place * rows, rows), rows)], local_sem.at[1]),
    ] + [pltpu.make_async_copy(own(part), piece(part, me), local_sem.at[2 + part]) for part in range(4)]
    for copy in locals_:
        copy.start()
    for copy, source, target in zip(here, (gate_here, down_here), (gate_out, down_out)):
        copy.wait()
        target[...] = source[...].astype(low)
    a_copies = square_next(a_all, 0, a_copies)
    dy_copies = square_first(dy_ref, dy_all, 6)
    for part in range(4):
        came(part, 2)
        onward(part)
        siblings.append(to_sibling(part, 2))
    dy_copies = square_next(dy_all, 6, dy_copies)
    for part in range(4):
        for slot in (1, 3):
            came(part, slot)
            siblings.append(to_sibling(part, slot))
    for copy in a_copies[2:] + dy_copies[2:] + bias_copies + siblings:
        copy.wait_recv()
    for copy in a_copies + dy_copies + bias_copies + siblings:
        copy.wait_send()
    for part in range(4):
        line(part, 2, 2).wait_send()

        @pl.when(chip < 3)
        def _():
            line(part, 3, 1).wait_send()

        @pl.when(chip > 0)
        def _():
            line(part, 1, 3).wait_send()

        @pl.when(chip == 2)
        def _():
            line(part, 1, 1, turned(2)).wait_send()

        @pl.when(chip == 1)
        def _():
            line(part, 3, 3, turned(2)).wait_send()

    for copy in locals_:
        copy.wait()


def start_gather(x, gain, shift, dy, bias, wq, wo, gate, down):
    dma = pltpu.SemaphoreType.DMA
    low, wide = jnp.bfloat16, jnp.float32
    anywhere = pl.BlockSpec(memory_space=pl.ANY)
    local_ = pl.BlockSpec(memory_space=pltpu.VMEM)
    shape = jax.ShapeDtypeStruct
    rows, model = x.shape
    return pl.pallas_call(
        start_kernel,
        out_shape=(
            shape((4 * rows, model), low),
            shape((4 * rows, model), low),
            shape((8, *bias.shape), bias.dtype),
            shape((wq.shape[0], 8 * wq.shape[1], wq.shape[2]), low),
            shape((wo.shape[0], 8 * wo.shape[1]), low),
            shape((rows, model), wide),
            shape((rows, 1), wide),
            shape(gate.shape, low),
            shape(down.shape, low),
        ),
        in_specs=[local_] * 7 + [anywhere] * 2,
        out_specs=(anywhere, anywhere, local_, anywhere, anywhere, local_, local_, local_, local_),
        scratch_shapes=[
            pltpu.VMEM((rows, model), low),
            pltpu.VMEM(wq.shape, low),
            pltpu.VMEM(wo.shape, low),
            pltpu.VMEM(gate.shape, wide),
            pltpu.VMEM(down.shape, wide),
            dma((12,)), dma((12,)), dma((8,)), dma((8,)),
            dma((4, 4)), dma((4, 4)), dma((4, 4)), dma((4, 4)), dma((8,)),
        ],
        compiler_params=pltpu.CompilerParams(
            collective_id=2, has_side_effects=True, vmem_limit_bytes=48 * 1024 * 1024
        ),
        cost_estimate=pl.CostEstimate(flops=0, bytes_accessed=200_000_000, transcendentals=0),
        name="start_gather",
    )(x, gain, shift, dy, bias, wq, wo, gate, down)


def last_kernel(
    first_ref, proj_ref, normed_ref, recip_ref, gain_ref, grad_ref, second_ref, bias_ref,
    input_out, proj_out, vector_out, bias_out,
    square_x, square_y, staged, square_last, mine, near,
    corners, vector_mine, vector_came, vector_slots, bias_mine, bias_came, bias_slots,
    square_send, square_recv, vector_send, vector_recv, bias_send, bias_recv, core_send, core_recv, line_send, line_recv,
):
    place, along_x, along_y = partners()
    corner = 3 - place
    me = lax.axis_index("dp")
    chip, core = me // 2, me % 2
    sibling = me + 1 - 2 * core
    width = proj_out.shape[1]
    rows = input_out.shape[0]
    half = rows // 2
    low, wide = jnp.bfloat16, jnp.float32

    def start(source, target, send_sem, recv_sem, device):
        copy = pltpu.make_async_remote_copy(
            src_ref=source, dst_ref=target, send_sem=send_sem, recv_sem=recv_sem,
            device_id=device, device_id_type=MESH,
        )
        copy.start()
        return copy

    barrier = pltpu.get_barrier_semaphore()
    chips = [{"dp": (me + 2 * step) % 8} for step in (1, 2, 3)]
    square = [{"tensor": device} for device in (along_x, along_y, corner)]
    for other in square + [{"dp": sibling}] + chips:
        pl.semaphore_signal(barrier, inc=1, device_id=other, device_id_type=MESH)
    pl.semaphore_wait(barrier, 7)

    def turned(slot, which):
        return 2 * ((chip + slot) % 4) + which

    def proj_part(owner):
        return proj_ref.at[:, pl.ds(pl.multiple_of(owner * width, width), width)]

    exchange = {
        slot: start(
            proj_part(turned(slot, 1 - core)), mine.at[slot], core_send.at[slot], core_recv.at[slot], {"dp": sibling}
        )
        for slot in (3, 1, 2, 0)
    }

    def line(slot, step, part):
        return pltpu.make_async_remote_copy(
            src_ref=mine.at[slot], dst_ref=near.at[part], send_sem=line_send.at[part], recv_sem=line_recv.at[part],
            device_id={"dp": turned(step, core)}, device_id_type=MESH,
        )

    def term(owner, part):
        return first_ref.at[pl.ds(pl.multiple_of(owner * rows + part * half, half), half)]

    def rows_at(owner, part):
        return term(owner, part)[...].astype(wide)

    plan = [
        (term(corner, 0), square_x.at[1], square[0]),
        (term(corner, 1), square_y.at[1], square[1]),
        (term(along_x, 0), square_x.at[0], square[0]),
        (term(along_y, 1), square_y.at[0], square[1]),
    ]
    copies = [
        start(source, target, square_send.at[i], square_recv.at[i], device)
        for i, (source, target, device) in enumerate(plan)
    ]
    for slot in (3, 1, 2):
        exchange[slot].wait_recv()
        mine[slot] = (mine[slot].astype(wide) + proj_part(turned(slot, core))[...].astype(wide)).astype(low)
        if slot == 3:

            @pl.when(chip == 0)
            def _():
                line(3, 1, 0).start()

            @pl.when((chip == 1) | (chip == 2))
            def _():
                line(3, 3, 3).start()

        elif slot == 1:

            @pl.when(chip == 3)
            def _():
                line(1, 3, 0).start()

            @pl.when((chip == 1) | (chip == 2))
            def _():
                line(1, 1, 1).start()

        else:

            @pl.when((chip == 0) | (chip == 3))
            def _():
                line(2, 2, 2).start()

    bias_mine[...] = bias_ref[...]
    bias_copies = [start(bias_mine, bias_came, bias_send.at[0], bias_recv.at[0], {"dp": sibling})]
    bias_copies[0].wait_recv()
    bias_slots[chip] = bias_mine[...] + bias_came[...]
    bias_copies += [
        start(bias_slots.at[chip], bias_slots.at[chip], bias_send.at[1 + i], bias_recv.at[1 + i], chips[i])
        for i in range(3)
    ]
    copies[0].wait_recv()
    staged[0] = (rows_at(along_y, 0) + square_x[1].astype(wide)).astype(low)
    copies.append(start(staged.at[0], square_last.at[0], square_send.at[4], square_recv.at[4], square[1]))
    copies[1].wait_recv()
    staged[1] = (rows_at(along_x, 1) + square_y[1].astype(wide)).astype(low)
    copies.append(start(staged.at[1], square_last.at[1], square_send.at[5], square_recv.at[5], square[0]))

    @pl.when((chip == 1) | (chip == 2))
    def _():
        line(0, 1, 0).wait_recv()
        mine[2] = (mine[2].astype(wide) + near[0].astype(wide)).astype(low)
        line(2, 2, 2).start()

    @pl.when(chip == 0)
    def _():
        line(3, 1, 0).wait_send()
        line(1, 1, 1).start()

    @pl.when(chip == 3)
    def _():
        line(1, 3, 0).wait_send()
        line(3, 3, 3).start()

    gain = gain_ref[...]
    vector_gain = jnp.zeros_like(gain)
    vector_shift = jnp.zeros_like(gain)
    for part, came in enumerate((square_x, square_y)):
        here = slice(part * half, (part + 1) * half)
        copies[2 + part].wait_recv()
        copies[4 + part].wait_recv()
        grad = rows_at(place, part) + came[0].astype(wide) + square_last[part].astype(wide)
        normed = normed_ref[here, :]
        vector_gain += jnp.sum(grad * normed, 0, keepdims=True)
        vector_shift += jnp.sum(grad, 0, keepdims=True)
        scaled = grad * gain
        inner = (
            scaled
            - jnp.mean(scaled, -1, keepdims=True)
            - normed * jnp.mean(scaled * normed, -1, keepdims=True)
        )
        input_out[here, :] = grad_ref[here, :] + recip_ref[here, :] * inner
    corners[place, 0:1, :] = vector_gain
    corners[place, 1:2, :] = second_ref[0:1, :]
    corners[place, 2:3, :] = vector_shift
    corners[place, 3:4, :] = second_ref[1:2, :]
    vector_copies = [
        start(corners.at[place], corners.at[place], vector_send.at[i], vector_recv.at[i], square[i]) for i in range(3)
    ]
    for copy in vector_copies:
        copy.wait_recv()
    vector_mine[...] = (corners[0] + corners[1]) + (corners[2] + corners[3])
    vector_copies.append(start(vector_mine, vector_came, vector_send.at[3], vector_recv.at[3], {"dp": sibling}))
    vector_copies[3].wait_recv()
    vector_slots[chip] = vector_mine[...] + vector_came[...]
    vector_copies += [
        start(vector_slots.at[chip], vector_slots.at[chip], vector_send.at[4 + i], vector_recv.at[4 + i], chips[i])
        for i in range(3)
    ]
    for copy in vector_copies[4:] + bias_copies[1:]:
        copy.wait_recv()
    vector_out[...] = (vector_slots[0] + vector_slots[1]) + (vector_slots[2] + vector_slots[3])
    bias_out[...] = (bias_slots[0] + bias_slots[1]) + (bias_slots[2] + bias_slots[3])

    exchange[0].wait_recv()
    line(2, 2, 2).wait_recv()

    @pl.when(chip > 0)
    def _():
        line(1, 1, 1).wait_recv()

    @pl.when(chip < 3)
    def _():
        line(3, 3, 3).wait_recv()

    total = proj_part(turned(0, core))[...].astype(wide) + mine[0].astype(wide) + near[2].astype(wide)
    total = total + jnp.where(chip > 0, near[1].astype(wide), 0.0)
    proj_out[...] = total + jnp.where(chip < 3, near[3].astype(wide), 0.0)
    for copy in copies + vector_copies + bias_copies + list(exchange.values()):
        copy.wait_send()
    line(2, 2, 2).wait_send()

    @pl.when(chip < 3)
    def _():
        line(1, 1, 1).wait_send()

    @pl.when(chip > 0)
    def _():
        line(3, 3, 3).wait_send()


def last_reduce(first, proj, normed, recip, gain, grad, second, bias):
    dma = pltpu.SemaphoreType.DMA
    low, wide = jnp.bfloat16, jnp.float32
    shape, vmem = jax.ShapeDtypeStruct, pltpu.VMEM
    rows, model = normed.shape
    pair = vmem((2, rows // 2, model), low)
    blocks = vmem((4, proj.shape[0], proj.shape[1] // 8), low)
    return pl.pallas_call(
        last_kernel,
        out_shape=(
            shape((rows, model), wide),
            shape((proj.shape[0], proj.shape[1] // 8), wide),
            shape((4, model), wide),
            shape(bias.shape, wide),
        ),
        in_specs=[pl.BlockSpec(memory_space=pltpu.VMEM)] * 8,
        out_specs=(pl.BlockSpec(memory_space=pltpu.VMEM),) * 4,
        scratch_shapes=[
            pair, pair, pair, pair, blocks, blocks,
            vmem((4, 4, model), wide),
            vmem((4, model), wide),
            vmem((4, model), wide),
            vmem((4, 4, model), wide),
            vmem(bias.shape, wide),
            vmem(bias.shape, wide),
            vmem((4, *bias.shape), wide),
            dma((6,)), dma((6,)), dma((7,)), dma((7,)), dma((4,)), dma((4,)),
            dma((4,)), dma((4,)), dma((4,)), dma((4,)),
        ],
        compiler_params=pltpu.CompilerParams(
            collective_id=3, has_side_effects=True, vmem_limit_bytes=40 * 1024 * 1024
        ),
        cost_estimate=pl.CostEstimate(flops=0, bytes_accessed=120_000_000, transcendentals=0),
        name="last_reduce",
    )(first, proj, normed, recip, gain, grad, second, bias)


def after(late, early):
    return lax.optimization_barrier((late, early))[0]


class Plain:
    def gather_rows(self, block):
        return lax.all_gather(block, "tensor", axis=0, tiled=True)

    def reduce_rows(self, terms, ready, name):
        return lax.psum_scatter(terms, "tensor", scatter_dimension=0, tiled=True).astype(jnp.float32)

    def begin(self, x, gain, shift, dy, bias, w_qkv, w_output, gate_up, down):
        low = jnp.bfloat16
        out, normed, recip = layer_norm(x.astype(jnp.float32), gain, shift)
        return (
            self.gather_rows(out.astype(low)),
            self.gather_rows(dy),
            lax.all_gather(bias, "dp", axis=2, tiled=True),
            gather_dp(w_qkv.astype(low), 1),
            gather_dp(w_output.astype(low), 1),
            normed,
            recip,
            gate_up.astype(low),
            down.astype(low),
        )

    reduce_beside = reduce_rows

    def finish(self, first, proj, normed, recip, gain, grad, second, bias):
        first = self.reduce_rows(first, None, 0)
        vectors = jnp.stack([jnp.sum(first * normed, 0), second[0], jnp.sum(first, 0), second[1]])
        input_grad = grad + norm_back(first, normed, recip, gain)
        return input_grad, scatter_dp(proj, 1), lax.psum(vectors, ("dp", "tensor")), lax.psum(bias, "dp")


class Line(Plain):
    def gather_rows(self, block):
        return square_gather(block)

    def reduce_rows(self, terms, ready, name):
        return square_reduce(terms, ready, name)

    def begin(self, x, gain, shift, dy, bias, w_qkv, w_output, gate_up, down):
        parts, heads, few = bias.shape
        a, dy, came, *others = start_gather(
            x, gain.reshape(1, -1), shift.reshape(1, -1), dy, self.flat(bias), w_qkv, w_output, gate_up, down
        )
        came = came.reshape(8, -1)[:, : parts * heads * few].reshape(8, parts, heads, few)
        return a, dy, came.transpose(1, 2, 0, 3).reshape(parts, heads, -1), *others

    def flat(self, values):
        values = values.astype(jnp.float32).reshape(-1)
        width = -(-values.shape[0] // 1024) * 1024
        return jnp.pad(values, (0, width - values.shape[0])).reshape(8, -1)

    def reduce_beside(self, terms, ready, name):
        me = lax.axis_index("tensor")
        rows = terms.shape[0] // 4
        parts = [lax.dynamic_slice_in_dim(terms, (me ^ step) * rows, rows, 0) for step in range(4)]
        total = parts[0].astype(jnp.float32)
        for step in (3, 1, 2):
            came = lax.ppermute(parts[step], "tensor", [(i, i ^ step) for i in range(4)])
            total = total + came.astype(jnp.float32)
        return total

    def finish(self, first, proj, normed, recip, gain, grad, second, bias):
        input_grad, proj_grad, vectors, total = last_reduce(
            first, proj, normed, recip, gain.reshape(1, -1), grad, second, self.flat(bias)
        )
        return input_grad, proj_grad, vectors, total.reshape(-1)[: bias.size].reshape(bias.shape)


def row_major(values):
    return with_layout_constraint(values, Layout(tuple(range(values.ndim))))


def gather_dp(block, axis):
    return row_major(lax.all_gather(block.astype(jnp.bfloat16), "dp", axis=axis, tiled=True))


def scatter_dp(terms, axis):
    return lax.psum_scatter(terms.astype(jnp.bfloat16), "dp", scatter_dimension=axis, tiled=True)


def local(
    routes,
    inputs,
    cotangent,
    gains,
    shifts,
    qkv_weight,
    biases,
    out_weight,
    gate_up,
    down_weight,
    momentum_gains,
    momentum_shifts,
    momentum_qkv,
    momentum_biases,
    momentum_out,
    momentum_gate,
    momentum_down,
    variance_gains,
    variance_shifts,
    variance_qkv,
    variance_biases,
    variance_out,
    variance_gate,
    variance_down,
):
    low = jnp.bfloat16
    local_heads = biases.shape[1]
    local_width = qkv_weight.shape[2]
    head_size = local_width // local_heads
    xin = inputs.astype(jnp.float32)
    a_all, dy_all, bias_all, w_qkv, w_output, first_normed, first_recip, gate_low, down_low = routes.begin(
        inputs, gains[0], shifts[0], cotangent, biases.astype(low), qkv_weight, out_weight, gate_up, down_weight
    )
    bias_all = bias_all.reshape(3, local_width).astype(jnp.float32)
    w_gate_up = gather_dp(after(gate_low, w_output), 1)
    lin = jnp.einsum("rd,kdc->krc", a_all, w_qkv, preferred_element_type=jnp.float32)
    qkv, heads, logs = attention_forward(lin, bias_all, head_size)
    resid = xin + routes.reduce_rows(mxu(heads, w_output, NN).astype(low), logs, 4)
    second_out, second_normed, second_recip = layer_norm(resid, gains[1], shifts[1])
    m_all = routes.gather_rows(second_out.astype(low))
    w_down = gather_dp(after(down_low, (w_gate_up, m_all)), 1)
    gate_vals = jnp.einsum("rd,kdc->krc", m_all, w_gate_up, preferred_element_type=jnp.float32)
    gate_lin, upward = gate_vals[0], gate_vals[1]
    sigmoid_gate = jax.nn.sigmoid(gate_lin)
    silu_gate = gate_lin * sigmoid_gate
    hidden = (silu_gate * upward).astype(low)
    down_terms = mxu(hidden, dy_all, TN).astype(low)
    down_grad = scatter_dp(down_terms, 1)
    w_down = after(w_down, down_terms)
    block_terms = mxu(hidden, w_down, NN).astype(low)
    down_sum = routes.reduce_beside(block_terms, None, 6)
    hidden_grad = mxu(dy_all, after(w_down, block_terms), NT)
    gate_grad_low = (
        hidden_grad * upward * sigmoid_gate * (1.0 + gate_lin * (1.0 - sigmoid_gate))
    ).astype(low)
    up_grad_low = (hidden_grad * silu_gate).astype(low)
    both_grads = jnp.stack([gate_grad_low, up_grad_low], 0)
    gate_terms = jnp.einsum("rd,krc->kdc", m_all, both_grads, preferred_element_type=jnp.float32)
    gate_terms = row_major(gate_terms.astype(low))
    second_terms = jnp.einsum(
        "krc,kdc->rd", both_grads, w_gate_up, preferred_element_type=jnp.float32
    ).astype(low)
    block_out = (resid + down_sum).astype(low)
    gate_grad = scatter_dp(after(gate_terms, (down_grad, second_terms, block_out)), 1)
    second_grad = routes.reduce_rows(after(second_terms, down_grad), block_out[:16, :128], 5)
    resid_grad = cotangent.astype(jnp.float32) + norm_back(
        second_grad, second_normed, second_recip, gains[1]
    )
    gain_second = jnp.sum(second_grad * second_normed, 0)
    shift_second = jnp.sum(second_grad, 0)
    resid_full = routes.gather_rows(resid_grad.astype(low))
    out_terms = mxu(heads, resid_full, TN).astype(low)
    heads_grad = mxu(resid_full, w_output, NT).astype(low)
    lin_grads, bias_terms = attention_backward(qkv, heads_grad, logs, head_size)
    qkv_terms = jnp.einsum("rd,krc->kdc", a_all, lin_grads, preferred_element_type=jnp.float32)
    qkv_terms = row_major(qkv_terms.astype(low))
    first_terms = jnp.einsum(
        "krc,kdc->rd", lin_grads, w_qkv, preferred_element_type=jnp.float32
    ).astype(low)
    qkv_grad = scatter_dp(after(qkv_terms, gate_grad), 1)
    input_grad, out_grad, vectors, bias_sum = routes.finish(
        first_terms,
        out_terms,
        first_normed,
        first_recip,
        gains[0],
        resid_grad,
        jnp.stack([gain_second, shift_second]),
        bias_terms,
    )
    gains_grad, shifts_grad = vectors[:2], vectors[2:]
    down_grad, gate_grad, out_grad = (
        grad.astype(jnp.float32) for grad in (*after((down_grad, gate_grad), vectors), out_grad)
    )
    qkv_grad = qkv_grad.astype(jnp.float32)
    per_dp = biases.shape[2]
    biases_grad = lax.dynamic_slice_in_dim(
        bias_sum.reshape(3, local_heads, head_size), lax.axis_index("dp") * per_dp, per_dp, 2
    )
    gain_new = adamw(gains, gains_grad, momentum_gains, variance_gains, 0.0, vector_rate)
    shift_new = adamw(shifts, shifts_grad, momentum_shifts, variance_shifts, 0.0, vector_rate)
    qkv_new = adamw(qkv_weight, qkv_grad, momentum_qkv, variance_qkv, decay_rate, learn_rate)
    bias_new = adamw(biases, biases_grad, momentum_biases, variance_biases, 0.0, vector_rate)
    out_new = adamw(out_weight, out_grad, momentum_out, variance_out, decay_rate, learn_rate)
    gate_new = adamw(gate_up, gate_grad, momentum_gate, variance_gate, decay_rate, learn_rate)
    down_new = adamw(down_weight, down_grad, momentum_down, variance_down, decay_rate, learn_rate)
    return (
        block_out,
        input_grad,
        gains_grad,
        shifts_grad,
        qkv_grad,
        biases_grad,
        out_grad,
        gate_grad,
        down_grad,
        gain_new[0],
        shift_new[0],
        qkv_new[0],
        bias_new[0],
        out_new[0],
        gate_new[0],
        down_new[0],
        gain_new[1],
        shift_new[1],
        qkv_new[1],
        bias_new[1],
        out_new[1],
        gate_new[1],
        down_new[1],
        gain_new[2],
        shift_new[2],
        qkv_new[2],
        bias_new[2],
        out_new[2],
        gate_new[2],
        down_new[2],
    )


def solution(mesh):
    routes = Line() if dict(mesh.shape) == {"dp": 8, "tensor": 4} else Plain()

    def step(*arrays):
        return local(routes, *arrays)

    return jax.shard_map(
        step,
        mesh=mesh,
        in_specs=(
            P(("dp", "tensor"), None),
            P(("dp", "tensor"), None),
            P(),
            P(),
            P(None, "dp", "tensor"),
            P(None, "tensor", "dp"),
            P("tensor", "dp"),
            P(None, "dp", "tensor"),
            P("tensor", "dp"),
            P(),
            P(),
            P(None, "dp", "tensor"),
            P(None, "tensor", "dp"),
            P("tensor", "dp"),
            P(None, "dp", "tensor"),
            P("tensor", "dp"),
            P(),
            P(),
            P(None, "dp", "tensor"),
            P(None, "tensor", "dp"),
            P("tensor", "dp"),
            P(None, "dp", "tensor"),
            P("tensor", "dp"),
        ),
        out_specs=(
            P(("dp", "tensor"), None),
            P(("dp", "tensor"), None),
            P(),
            P(),
            P(None, "dp", "tensor"),
            P(None, "tensor", "dp"),
            P("tensor", "dp"),
            P(None, "dp", "tensor"),
            P("tensor", "dp"),
            P(),
            P(),
            P(None, "dp", "tensor"),
            P(None, "tensor", "dp"),
            P("tensor", "dp"),
            P(None, "dp", "tensor"),
            P("tensor", "dp"),
            P(),
            P(),
            P(None, "dp", "tensor"),
            P(None, "tensor", "dp"),
            P("tensor", "dp"),
            P(None, "dp", "tensor"),
            P("tensor", "dp"),
            P(),
            P(),
            P(None, "dp", "tensor"),
            P(None, "tensor", "dp"),
            P("tensor", "dp"),
            P(None, "dp", "tensor"),
            P("tensor", "dp"),
        ),
        check_vma=False,
    )
```

```python
import functools

import jax
import jax.numpy as jnp
import numpy as np
from jax import lax
from jax.experimental import pallas as pl
from jax.experimental.layout import Layout, with_layout_constraint
from jax.experimental.pallas import tpu as pltpu
from jax.sharding import PartitionSpec as P

ROT = 16
SEQ = 1024
ADAM_STEP = 3


norm_eps = 1e-05
learn_rate = 0.03
vector_rate = 0.25
decay_rate = 0.1
adam_eps = 1e-08


def layer_norm(values, gain, shift):
    centred = values - jnp.mean(values, -1, keepdims=True)
    recip = lax.rsqrt(jnp.mean(centred * centred, -1, keepdims=True) + norm_eps)
    normed = centred * recip
    return (normed * gain + shift, normed, recip)


def norm_back(grad, normed, recip, gain):
    scaled = grad * gain
    inner = (
        scaled
        - jnp.mean(scaled, -1, keepdims=True)
        - normed * jnp.mean(scaled * normed, -1, keepdims=True)
    )
    return recip * inner


def adamw(weight, grad, moment, second, decay, rate):
    moment_new = 0.9 * moment + 0.1 * grad
    second_new = 0.95 * second + 0.05 * grad * grad
    fixed_one = 1.0 - 0.9**ADAM_STEP
    fixed_two = 1.0 - 0.95**ADAM_STEP
    change = moment_new / fixed_one / (jnp.sqrt(second_new / fixed_two) + adam_eps) + decay * weight
    return (weight - rate * change, moment_new, second_new)


def lane_head(shape, head_size):
    return lax.broadcasted_iota(jnp.int32, shape, len(shape) - 1) // head_size


def turn(values, tables, sign=1.0):
    width = values.shape[-1]
    own, ahead, behind = (jnp.concatenate([table] * (width // table.shape[-1]), 1) for table in tables)
    ahead = pltpu.roll(values, width - ROT // 2, 1) * ahead
    behind = pltpu.roll(values, ROT // 2, 1) * behind
    return values * own + sign * (ahead + behind)


def turn_tables(head_size):
    halfway = ROT // 2
    lane = np.arange(max(128, head_size)) % head_size
    position = np.arange(SEQ).astype(np.float32)
    frequency = np.power(np.float32(10000.0), -2.0 * (lane % halfway).astype(np.float32) / ROT)
    angles = position[:, None] * frequency.astype(np.float32)[None, :]
    cosine, sine = np.cos(angles), np.sin(angles)
    tables = [
        np.where(lane < ROT, cosine, 1.0),
        np.where(lane < halfway, -sine, 0.0),
        np.where((lane >= halfway) & (lane < ROT), sine, 0.0),
    ]
    return jnp.asarray(np.stack(tables).astype(np.float32))


LOG2E = 1.4426950408889634
NT = (((1,), (1,)), ((), ()))
NN = (((1,), (0,)), ((), ()))
TN = (((0,), (0,)), ((), ()))


def mxu(left, right, dims):
    return lax.dot_general(left, right, dims, preferred_element_type=jnp.float32)


def forward_kernel(head_size, lin_ref, bias_ref, table_ref, qkv_ref, out_ref, lse_ref):
    rows, width = out_ref.shape
    low = jnp.bfloat16
    step = min(256, rows)
    for part in range(3):
        for begin in range(0, rows, step):
            here = slice(begin, begin + step)
            values = lin_ref[part, here, :] + bias_ref[part : part + 1, :]
            if part < 2:
                values = turn(values, [table_ref[i, here, :] for i in range(3)])
            qkv_ref[part, here, :] = values.astype(low)
    owner = lane_head((step, width), head_size)
    lanes = lax.broadcasted_iota(jnp.int32, (step, 128), 1)
    for begin in range(0, rows, step):
        end = begin + step
        query = qkv_ref[0, begin:end, :]
        result = jnp.zeros((step, width), jnp.float32)
        logs = jnp.zeros((step, 128), jnp.float32)
        keep = lax.broadcasted_iota(jnp.int32, (step, step), 0) >= lax.broadcasted_iota(
            jnp.int32, (step, step), 1
        )
        for head in range(width // head_size):
            mine = jnp.where(owner == head, query, jnp.zeros_like(query))
            scores = mxu(mine, qkv_ref[1, :end, :], NT)
            last = jnp.where(keep, scores[:, begin:], -1e30)
            scores = jnp.concatenate([scores[:, :begin], last], 1) if begin else last
            top = jnp.max(scores, 1, keepdims=True)
            expo = jnp.exp2((scores - top) * (0.125 * LOG2E))
            total = jnp.sum(expo, 1, keepdims=True)
            found = mxu(expo.astype(low), qkv_ref[2, :end, :], NN)
            result = jnp.where(owner == head, found / total, result)
            logs = jnp.where(lanes == head, top * (0.125 * LOG2E) + jnp.log2(total), logs)
        out_ref[begin:end, :] = result.astype(low)
        lse_ref[:, begin:end] = logs.T[:8]


def attention_forward(lin, bias, head_size):
    _, rows, width = lin.shape
    lanes = min(256, width)
    groups = width // lanes
    tables = turn_tables(head_size)
    low = jnp.bfloat16
    return pl.pallas_call(
        functools.partial(forward_kernel, head_size),
        grid=(rows // SEQ, groups),
        out_shape=(
            jax.ShapeDtypeStruct((3, rows, width), low),
            jax.ShapeDtypeStruct((rows, width), low),
            jax.ShapeDtypeStruct((groups, 8, rows), jnp.float32),
        ),
        in_specs=[
            pl.BlockSpec((3, SEQ, lanes), lambda i, j: (0, i, j)),
            pl.BlockSpec((3, lanes), lambda i, j: (0, j)),
            pl.BlockSpec(tables.shape, lambda i, j: (0, 0, 0)),
        ],
        out_specs=(
            pl.BlockSpec((3, SEQ, lanes), lambda i, j: (0, i, j)),
            pl.BlockSpec((SEQ, lanes), lambda i, j: (i, j)),
            pl.BlockSpec((None, 8, SEQ), lambda i, j: (j, 0, i)),
        ),
        compiler_params=pltpu.CompilerParams(vmem_limit_bytes=48 * 1024 * 1024),
        cost_estimate=pl.CostEstimate(
            flops=rows * SEQ * width * 8, bytes_accessed=rows * width * 26, transcendentals=0
        ),
        name="attend_forward",
    )(lin, bias, tables)


def backward_kernel(head_size, qkv_ref, grad_ref, lse_ref, table_ref, out_ref, sum_ref, acc_ref):
    _, rows, width = qkv_ref.shape
    low = jnp.bfloat16
    step = min(256, rows)
    owner = lane_head((step, width), head_size)
    acc_ref[...] = jnp.zeros_like(acc_ref)
    blank = jnp.zeros((step, width), low)
    for begin in range(0, rows, step):
        end = begin + step
        query = qkv_ref[0, begin:end, :]
        grad = grad_ref[begin:end, :]
        keep = lax.broadcasted_iota(jnp.int32, (step, step), 1) >= lax.broadcasted_iota(
            jnp.int32, (step, step), 0
        )
        query_grad = jnp.zeros((step, width), jnp.float32)
        for head in range(width // head_size):
            mine = jnp.where(owner == head, query, blank)
            grad_mine = jnp.where(owner == head, grad, blank)
            scores = mxu(qkv_ref[1, :end, :], mine, NT)
            expo = jnp.exp2(scores * (0.125 * LOG2E) - lse_ref[head : head + 1, begin:end])
            last = jnp.where(keep, expo[begin:, :], 0.0)
            probs = jnp.concatenate([expo[:begin], last], 0) if begin else last
            prob_grad = mxu(qkv_ref[2, :end, :], grad_mine, NT)
            inner = jnp.sum(probs * prob_grad, 0, keepdims=True)
            score_grad = (probs * (prob_grad - inner)).astype(low)
            acc_ref[0, :end, :] += mxu(score_grad, mine, NN)
            acc_ref[1, :end, :] += mxu(probs.astype(low), grad_mine, NN)
            found = mxu(score_grad, qkv_ref[1, :end, :], TN)
            query_grad = jnp.where(owner == head, found, query_grad)
        turned = turn(0.125 * query_grad, [table_ref[i, begin:end, :] for i in range(3)], -1.0).astype(low)
        out_ref[0, begin:end, :] = turned
        added = jnp.sum(turned.astype(jnp.float32), 0, keepdims=True)
        sum_ref[0:1, :] = added if begin == 0 else sum_ref[0:1, :] + added
    for begin in range(0, rows, step):
        here = slice(begin, begin + step)
        turned = turn(0.125 * acc_ref[0, here, :], [table_ref[i, here, :] for i in range(3)], -1.0).astype(low)
        out_ref[1, here, :] = turned
        added = jnp.sum(turned.astype(jnp.float32), 0, keepdims=True)
        sum_ref[1:2, :] = added if begin == 0 else sum_ref[1:2, :] + added
        turned = acc_ref[1, here, :].astype(low)
        out_ref[2, here, :] = turned
        added = jnp.sum(turned.astype(jnp.float32), 0, keepdims=True)
        sum_ref[2:3, :] = added if begin == 0 else sum_ref[2:3, :] + added


def attention_backward(qkv, grad, logs, head_size):
    _, rows, width = qkv.shape
    lanes = min(256, width)
    groups = width // lanes
    tables = turn_tables(head_size)
    low = jnp.bfloat16
    grads, sums = pl.pallas_call(
        functools.partial(backward_kernel, head_size),
        grid=(rows // SEQ, groups),
        out_shape=(
            jax.ShapeDtypeStruct((3, rows, width), low),
            jax.ShapeDtypeStruct((rows // SEQ, 3, width), jnp.float32),
        ),
        in_specs=[
            pl.BlockSpec((3, SEQ, lanes), lambda i, j: (0, i, j)),
            pl.BlockSpec((SEQ, lanes), lambda i, j: (i, j)),
            pl.BlockSpec((None, 8, SEQ), lambda i, j: (j, 0, i)),
            pl.BlockSpec(tables.shape, lambda i, j: (0, 0, 0)),
        ],
        out_specs=(
            pl.BlockSpec((3, SEQ, lanes), lambda i, j: (0, i, j)),
            pl.BlockSpec((None, 3, lanes), lambda i, j: (i, 0, j)),
        ),
        scratch_shapes=[pltpu.VMEM((2, SEQ, lanes), jnp.float32)],
        compiler_params=pltpu.CompilerParams(vmem_limit_bytes=48 * 1024 * 1024),
        cost_estimate=pl.CostEstimate(
            flops=rows * SEQ * width * 20, bytes_accessed=rows * width * 26, transcendentals=0
        ),
        name="attend_backward",
    )(qkv, grad, logs, tables)
    return grads, jnp.sum(sums, 0)


MESH = pl.DeviceIdType.MESH


def partners():
    me = lax.axis_index("tensor")
    return me, me + 1 - 2 * (me % 2), (me + 2) % 4


def greet(devices):
    barrier = pltpu.get_barrier_semaphore()
    for device in devices:
        pl.semaphore_signal(barrier, inc=1, device_id={"tensor": device}, device_id_type=MESH)
    pl.semaphore_wait(barrier, len(devices))


def gather_kernel(block_ref, whole_ref, send_sem, recv_sem, local_sem):
    me, along_x, along_y = partners()
    rows = block_ref.shape[0]
    half = rows // 2

    def part(owner, which):
        return whole_ref.at[pl.ds(pl.multiple_of(owner * rows + which * half, half), half)]

    def send(source, owner, which, target, index):
        copy = pltpu.make_async_remote_copy(
            src_ref=source,
            dst_ref=part(owner, which),
            send_sem=send_sem.at[index],
            recv_sem=recv_sem.at[index],
            device_id={"tensor": target},
            device_id_type=MESH,
        )
        copy.start()
        return copy

    mine = pltpu.make_async_copy(block_ref, whole_ref.at[pl.ds(pl.multiple_of(me * rows, rows), rows)], local_sem)
    mine.start()
    greet((along_x, along_y))
    halves = [block_ref.at[pl.ds(0, half)], block_ref.at[pl.ds(half, half)]]
    x_first = send(halves[0], me, 0, along_x, 0)
    y_first = send(halves[1], me, 1, along_y, 1)
    x_second = send(halves[1], me, 1, along_x, 2)
    y_second = send(halves[0], me, 0, along_y, 3)
    x_first.wait_recv()
    y_third = send(part(along_x, 0), along_x, 0, along_y, 4)
    y_first.wait_recv()
    x_third = send(part(along_y, 1), along_y, 1, along_x, 5)
    for copy in (x_second, y_second, y_third, x_third):
        copy.wait_recv()
    for copy in (x_first, y_first, x_second, y_second, y_third, x_third):
        copy.wait_send()
    mine.wait()


def square_gather(block):
    rows, width = block.shape
    return pl.pallas_call(
        gather_kernel,
        out_shape=jax.ShapeDtypeStruct((4 * rows, width), block.dtype),
        in_specs=[pl.BlockSpec(memory_space=pltpu.VMEM)],
        out_specs=pl.BlockSpec(memory_space=pl.ANY),
        scratch_shapes=[
            pltpu.SemaphoreType.DMA((6,)),
            pltpu.SemaphoreType.DMA((6,)),
            pltpu.SemaphoreType.DMA,
        ],
        compiler_params=pltpu.CompilerParams(collective_id=0, has_side_effects=True),
        cost_estimate=pl.CostEstimate(flops=0, bytes_accessed=rows * width * 120, transcendentals=0),
        name="square_gather",
    )(block)


def reduce_kernel(terms_ref, ready_ref, out_ref, first_x, first_y, staged, second, send_sem, recv_sem):
    del ready_ref
    me, along_x, along_y = partners()
    rows = out_ref.shape[0]
    half = rows // 2
    corner = 3 - me

    def term(owner, which):
        return terms_ref.at[pl.ds(pl.multiple_of(owner * rows + which * half, half), half)]

    def send(source, target_ref, target, index):
        copy = pltpu.make_async_remote_copy(
            src_ref=source,
            dst_ref=target_ref,
            send_sem=send_sem.at[index],
            recv_sem=recv_sem.at[index],
            device_id={"tensor": target},
            device_id_type=MESH,
        )
        copy.start()
        return copy

    greet((along_x, along_y))
    x_on = send(term(corner, 0), first_x.at[1], along_x, 0)
    y_on = send(term(corner, 1), first_y.at[1], along_y, 1)
    x_own = send(term(along_x, 0), first_x.at[0], along_x, 2)
    y_own = send(term(along_y, 1), first_y.at[0], along_y, 3)

    def added(one, two):
        return (one.astype(jnp.float32) + two.astype(jnp.float32)).astype(jnp.bfloat16)

    x_on.wait_recv()
    staged[0] = added(term(along_y, 0)[...], first_x[1])
    y_last = send(staged.at[0], second.at[0], along_y, 4)
    y_on.wait_recv()
    staged[1] = added(term(along_x, 1)[...], first_y[1])
    x_last = send(staged.at[1], second.at[1], along_x, 5)
    x_own.wait_recv()
    out_ref[:half] = term(me, 0)[...].astype(jnp.float32) + first_x[0].astype(jnp.float32)
    y_own.wait_recv()
    out_ref[half:] = term(me, 1)[...].astype(jnp.float32) + first_y[0].astype(jnp.float32)
    y_last.wait_recv()
    out_ref[:half] += second[0].astype(jnp.float32)
    x_last.wait_recv()
    out_ref[half:] += second[1].astype(jnp.float32)
    for copy in (x_on, y_on, x_own, y_own, y_last, x_last):
        copy.wait_send()


def square_reduce(terms, ready, name):
    rows, width = terms.shape[0] // 4, terms.shape[1]
    part = pltpu.VMEM((2, rows // 2, width), jnp.bfloat16)
    return pl.pallas_call(
        reduce_kernel,
        out_shape=jax.ShapeDtypeStruct((rows, width), jnp.float32),
        in_specs=[pl.BlockSpec(memory_space=pltpu.VMEM), pl.BlockSpec(memory_space=pl.ANY)],
        out_specs=pl.BlockSpec(memory_space=pltpu.VMEM),
        scratch_shapes=[
            part,
            part,
            part,
            part,
            pltpu.SemaphoreType.DMA((6,)),
            pltpu.SemaphoreType.DMA((6,)),
        ],
        compiler_params=pltpu.CompilerParams(
            collective_id=name, has_side_effects=True, vmem_limit_bytes=24 * 1024 * 1024
        ),
        cost_estimate=pl.CostEstimate(flops=0, bytes_accessed=rows * width * 240, transcendentals=0),
        name="square_reduce",
    )(terms, ready)


def start_kernel(
    x_from, gain_ref, shift_ref, dy_from, bias_ref, wq_from, wo_from, gate_from, down_from,
    a_all, dy_all, bias_all, wq_all, wo_all, normed_out, recip_out, gate_out, down_out,
    a_ref, wq_ref, wo_ref, x_ref, dy_ref, wq_wide, wo_wide, gate_wide, down_wide,
    square_send, square_recv, bias_send, bias_recv, line_send, line_recv, core_send, core_recv, local_sem,
):
    place, along_x, along_y = partners()
    me = lax.axis_index("dp")
    chip, core = me // 2, me % 2
    sibling = me + 1 - 2 * core
    rows = a_ref.shape[0]
    low = jnp.bfloat16
    half = rows // 2
    depth = wq_ref.shape[1]

    def start(source, target, send_sem, recv_sem, device):
        copy = pltpu.make_async_remote_copy(
            src_ref=source, dst_ref=target, send_sem=send_sem, recv_sem=recv_sem,
            device_id=device, device_id_type=MESH,
        )
        copy.start()
        return copy

    def piece(part, owner):
        if part < 3:
            return wq_all.at[part, pl.ds(pl.multiple_of(owner * depth, depth), depth)]
        width = wo_ref.shape[1]
        return wo_all.at[:, pl.ds(pl.multiple_of(owner * width, width), width)]

    def own(part):
        return wq_ref.at[part] if part < 3 else wo_ref

    def turned(step):
        return 2 * ((chip + step) % 4) + core

    moves = (
        (wq_from, wq_wide), (wo_from, wo_wide), (x_from, x_ref), (dy_from, dy_ref), (gate_from, gate_wide),
        (down_from, down_wide),
    )
    here = [pltpu.make_async_copy(source, target, local_sem.at[6 + i]) for i, (source, target) in enumerate(moves)]
    for copy in here:
        copy.start()
    bias_all[me] = bias_ref[...]

    barrier = pltpu.get_barrier_semaphore()
    for step in range(1, 8):
        pl.semaphore_signal(barrier, inc=1, device_id={"dp": (me + step) % 8}, device_id_type=MESH)
    for device in (along_x, along_y):
        pl.semaphore_signal(barrier, inc=1, device_id={"tensor": device}, device_id_type=MESH)
    here[0].wait()
    wq_ref[...] = wq_wide[...].astype(low)
    here[1].wait()
    wo_ref[...] = wo_wide[...].astype(low)
    pl.semaphore_wait(barrier, 9)

    def rows_of(whole, owner, which):
        return whole.at[pl.ds(pl.multiple_of(owner * rows + which * half, half), half)]

    def square_first(block, whole, base):
        halves = [block.at[pl.ds(0, half)], block.at[pl.ds(half, half)]]
        plan = [(0, along_x), (1, along_y), (1, along_x), (0, along_y)]
        return [
            start(halves[which], rows_of(whole, place, which), square_send.at[base + i], square_recv.at[base + i], {"tensor": device})
            for i, (which, device) in enumerate(plan)
        ]

    def square_next(whole, base, copies):
        copies[0].wait_recv()
        on_y = start(rows_of(whole, along_x, 0), rows_of(whole, along_x, 0), square_send.at[base + 4], square_recv.at[base + 4], {"tensor": along_y})
        copies[1].wait_recv()
        on_x = start(rows_of(whole, along_y, 1), rows_of(whole, along_y, 1), square_send.at[base + 5], square_recv.at[base + 5], {"tensor": along_x})
        return copies + [on_y, on_x]

    bias_copies = [
        start(bias_all.at[me], bias_all.at[me], bias_send.at[step], bias_recv.at[step], {"dp": (me + step) % 8})
        for step in range(1, 8)
    ]

    def line(part, slot, step, source=None):
        owner = me if source is None else source
        return pltpu.make_async_remote_copy(
            src_ref=own(part) if source is None else piece(part, source),
            dst_ref=piece(part, owner),
            send_sem=line_send.at[part, slot if source is None else 0],
            recv_sem=line_recv.at[part, slot],
            device_id={"dp": turned(step)},
            device_id_type=MESH,
        )

    def to_sibling(part, slot):
        owner = turned(slot)
        return start(
            own(part) if slot == 0 else piece(part, owner), piece(part, owner),
            core_send.at[part, slot], core_recv.at[part, slot], {"dp": sibling},
        )

    for part in range(4):
        line(part, 2, 2).start()

        @pl.when(chip % 2 == 0)
        def _():
            line(part, 3, 1).start()

        @pl.when(chip % 2 == 1)
        def _():
            line(part, 1, 3).start()

    def came(part, slot):
        line(part, slot, 4 - slot).wait_recv()

    def onward(part):
        @pl.when(chip == 2)
        def _():
            line(part, 1, 1, turned(2)).start()
            line(part, 1, 3).start()

        @pl.when(chip == 1)
        def _():
            line(part, 3, 3, turned(2)).start()
            line(part, 3, 1).start()

    siblings = [to_sibling(part, 0) for part in range(4)]
    here[2].wait()
    values = x_ref[...].astype(jnp.float32)
    centred = values - jnp.mean(values, -1, keepdims=True)
    recip = lax.rsqrt(jnp.mean(centred * centred, -1, keepdims=True) + norm_eps)
    recip_out[...] = recip
    normed_out[...] = centred * recip
    a_ref[...] = (normed_out[...] * gain_ref[...] + shift_ref[...]).astype(low)
    a_copies = square_first(a_ref, a_all, 0)
    here[3].wait()
    locals_ = [
        pltpu.make_async_copy(a_ref, a_all.at[pl.ds(pl.multiple_of(place * rows, rows), rows)], local_sem.at[0]),
        pltpu.make_async_copy(dy_ref, dy_all.at[pl.ds(pl.multiple_of(place * rows, rows), rows)], local_sem.at[1]),
    ] + [pltpu.make_async_copy(own(part), piece(part, me), local_sem.at[2 + part]) for part in range(4)]
    for copy in locals_:
        copy.start()
    for copy, source, target in zip(here[4:], (gate_wide, down_wide), (gate_out, down_out)):
        copy.wait()
        target[...] = source[...].astype(low)
    a_copies = square_next(a_all, 0, a_copies)
    dy_copies = square_first(dy_ref, dy_all, 6)
    for part in range(4):
        came(part, 2)
        onward(part)
        siblings.append(to_sibling(part, 2))
    dy_copies = square_next(dy_all, 6, dy_copies)
    for part in range(4):
        for slot in (1, 3):
            came(part, slot)
            siblings.append(to_sibling(part, slot))
    for copy in a_copies[2:] + dy_copies[2:] + bias_copies + siblings:
        copy.wait_recv()
    for copy in a_copies + dy_copies + bias_copies + siblings:
        copy.wait_send()
    for part in range(4):
        line(part, 2, 2).wait_send()

        @pl.when(chip < 3)
        def _():
            line(part, 3, 1).wait_send()

        @pl.when(chip > 0)
        def _():
            line(part, 1, 3).wait_send()

        @pl.when(chip == 2)
        def _():
            line(part, 1, 1, turned(2)).wait_send()

        @pl.when(chip == 1)
        def _():
            line(part, 3, 3, turned(2)).wait_send()

    for copy in locals_:
        copy.wait()


def start_gather(x, gain, shift, dy, bias, wq, wo, gate, down):
    dma = pltpu.SemaphoreType.DMA
    low, wide = jnp.bfloat16, jnp.float32
    anywhere = pl.BlockSpec(memory_space=pl.ANY)
    local_ = pl.BlockSpec(memory_space=pltpu.VMEM)
    shape = jax.ShapeDtypeStruct
    rows, model = x.shape
    return pl.pallas_call(
        start_kernel,
        out_shape=(
            shape((4 * rows, model), low),
            shape((4 * rows, model), low),
            shape((8, *bias.shape), bias.dtype),
            shape((wq.shape[0], 8 * wq.shape[1], wq.shape[2]), low),
            shape((wo.shape[0], 8 * wo.shape[1]), low),
            shape((rows, model), wide),
            shape((rows, 1), wide),
            shape(gate.shape, low),
            shape(down.shape, low),
        ),
        in_specs=[anywhere, local_, local_, anywhere, local_] + [anywhere] * 4,
        out_specs=(anywhere, anywhere, local_, anywhere, anywhere, local_, local_, local_, local_),
        scratch_shapes=[
            pltpu.VMEM((rows, model), low),
            pltpu.VMEM(wq.shape, low),
            pltpu.VMEM(wo.shape, low),
            pltpu.VMEM(x.shape, low),
            pltpu.VMEM(dy.shape, low),
            pltpu.VMEM(wq.shape, wide),
            pltpu.VMEM(wo.shape, wide),
            pltpu.VMEM(gate.shape, wide),
            pltpu.VMEM(down.shape, wide),
            dma((12,)), dma((12,)), dma((8,)), dma((8,)),
            dma((4, 4)), dma((4, 4)), dma((4, 4)), dma((4, 4)), dma((12,)),
        ],
        compiler_params=pltpu.CompilerParams(
            collective_id=2, has_side_effects=True, vmem_limit_bytes=60 * 1024 * 1024
        ),
        cost_estimate=pl.CostEstimate(flops=0, bytes_accessed=200_000_000, transcendentals=0),
        name="start_gather",
    )(x, gain, shift, dy, bias, wq, wo, gate, down)


def back_kernel(
    terms_ref, ready_ref, resid_ref, gain_ref, dy_ref, whole_ref, grad_out, second_out,
    first_x, first_y, staged, second, normed, low_ref,
    send_sem, recv_sem, row_send, row_recv, local_sem,
):
    del ready_ref
    me, along_x, along_y = partners()
    rows = grad_out.shape[0]
    half = rows // 2
    corner = 3 - me
    low, wide = jnp.bfloat16, jnp.float32

    def term(owner, which):
        return terms_ref.at[pl.ds(pl.multiple_of(owner * rows + which * half, half), half)]

    def part(owner, which):
        return whole_ref.at[pl.ds(pl.multiple_of(owner * rows + which * half, half), half)]

    def start(source, target_ref, target, sends, receives, index):
        copy = pltpu.make_async_remote_copy(
            src_ref=source,
            dst_ref=target_ref,
            send_sem=sends.at[index],
            recv_sem=receives.at[index],
            device_id={"tensor": target},
            device_id_type=MESH,
        )
        copy.start()
        return copy

    greet((along_x, along_y))
    x_on = start(term(corner, 0), first_x.at[1], along_x, send_sem, recv_sem, 0)
    y_on = start(term(corner, 1), first_y.at[1], along_y, send_sem, recv_sem, 1)
    x_own = start(term(along_x, 0), first_x.at[0], along_x, send_sem, recv_sem, 2)
    y_own = start(term(along_y, 1), first_y.at[0], along_y, send_sem, recv_sem, 3)
    resid = resid_ref[...]
    centred = resid - jnp.mean(resid, -1, keepdims=True)
    recip = lax.rsqrt(jnp.mean(centred * centred, -1, keepdims=True) + norm_eps)
    normed[...] = centred * recip
    x_on.wait_recv()
    staged[0] = (term(along_y, 0)[...].astype(wide) + first_x[1].astype(wide)).astype(low)
    y_last = start(staged.at[0], second.at[0], along_y, send_sem, recv_sem, 4)
    y_on.wait_recv()
    staged[1] = (term(along_x, 1)[...].astype(wide) + first_y[1].astype(wide)).astype(low)
    x_last = start(staged.at[1], second.at[1], along_x, send_sem, recv_sem, 5)
    gain = gain_ref[...]
    sums = [jnp.zeros_like(gain), jnp.zeros_like(gain)]
    for which, own, last, came in ((0, x_own, y_last, first_x), (1, y_own, x_last, first_y)):
        here = slice(which * half, (which + 1) * half)
        own.wait_recv()
        last.wait_recv()
        grad = term(me, which)[...].astype(wide) + came[0].astype(wide) + second[which].astype(wide)
        scaled = grad * gain
        inner = (
            scaled
            - jnp.mean(scaled, -1, keepdims=True)
            - normed[here, :] * jnp.mean(scaled * normed[here, :], -1, keepdims=True)
        )
        total = dy_ref[here, :].astype(wide) + recip[here, :] * inner
        grad_out[here, :] = total
        low_ref[here, :] = total.astype(low)
        if which == 0:
            copies = [start(low_ref.at[pl.ds(0, half)], part(me, 0), along_x, row_send, row_recv, 0)]
        else:
            copies += [
                start(low_ref.at[pl.ds(half, half)], part(me, 1), along_y, row_send, row_recv, 1),
                start(low_ref.at[pl.ds(half, half)], part(me, 1), along_x, row_send, row_recv, 2),
                start(low_ref.at[pl.ds(0, half)], part(me, 0), along_y, row_send, row_recv, 3),
            ]
        sums[0] += jnp.sum(grad * normed[here, :], 0, keepdims=True)
        sums[1] += jnp.sum(grad, 0, keepdims=True)
    mine = pltpu.make_async_copy(low_ref, whole_ref.at[pl.ds(pl.multiple_of(me * rows, rows), rows)], local_sem)
    mine.start()
    second_out[0:1, :] = sums[0]
    second_out[1:2, :] = sums[1]
    copies[0].wait_recv()
    copies.append(start(part(along_x, 0), part(along_x, 0), along_y, row_send, row_recv, 4))
    copies[1].wait_recv()
    copies.append(start(part(along_y, 1), part(along_y, 1), along_x, row_send, row_recv, 5))
    for copy in copies[2:]:
        copy.wait_recv()
    for copy in [x_on, y_on, x_own, y_own, y_last, x_last] + copies:
        copy.wait_send()
    mine.wait()


def square_back(terms, ready, resid, gain, dy):
    dma = pltpu.SemaphoreType.DMA
    low, wide = jnp.bfloat16, jnp.float32
    shape, vmem = jax.ShapeDtypeStruct, pltpu.VMEM
    rows, width = resid.shape
    anywhere, local_ = pl.BlockSpec(memory_space=pl.ANY), pl.BlockSpec(memory_space=pltpu.VMEM)
    pair = vmem((2, rows // 2, width), low)
    return pl.pallas_call(
        back_kernel,
        out_shape=(shape((4 * rows, width), low), shape((rows, width), wide), shape((2, width), wide)),
        in_specs=[local_, anywhere, local_, local_, local_],
        out_specs=(anywhere, local_, local_),
        scratch_shapes=[
            pair, pair, pair, pair, vmem((rows, width), wide), vmem((rows, width), low),
            dma((6,)), dma((6,)), dma((6,)), dma((6,)), dma,
        ],
        compiler_params=pltpu.CompilerParams(
            collective_id=1, has_side_effects=True, vmem_limit_bytes=32 * 1024 * 1024
        ),
        cost_estimate=pl.CostEstimate(flops=0, bytes_accessed=rows * width * 400, transcendentals=0),
        name="square_back",
    )(terms, ready, resid, gain, dy)


def last_kernel(
    first_ref, proj_ref, normed_ref, recip_ref, gain_ref, second_ref, bias_ref,
    step_out, proj_out, vector_out, bias_out,
    square_x, square_y, staged, square_last, mine, near,
    corners, vector_mine, vector_came, vector_slots, bias_mine, bias_came, bias_slots,
    square_send, square_recv, vector_send, vector_recv, bias_send, bias_recv, core_send, core_recv, line_send, line_recv,
):
    place, along_x, along_y = partners()
    corner = 3 - place
    me = lax.axis_index("dp")
    chip, core = me // 2, me % 2
    sibling = me + 1 - 2 * core
    width = proj_out.shape[1]
    rows = step_out.shape[0]
    half = rows // 2
    low, wide = jnp.bfloat16, jnp.float32

    def start(source, target, send_sem, recv_sem, device):
        copy = pltpu.make_async_remote_copy(
            src_ref=source, dst_ref=target, send_sem=send_sem, recv_sem=recv_sem,
            device_id=device, device_id_type=MESH,
        )
        copy.start()
        return copy

    barrier = pltpu.get_barrier_semaphore()
    chips = [{"dp": (me + 2 * step) % 8} for step in (1, 2, 3)]
    square = [{"tensor": device} for device in (along_x, along_y, corner)]
    for other in square + [{"dp": sibling}] + chips:
        pl.semaphore_signal(barrier, inc=1, device_id=other, device_id_type=MESH)
    pl.semaphore_wait(barrier, 7)

    def turned(slot, which):
        return 2 * ((chip + slot) % 4) + which

    def proj_part(owner):
        return proj_ref.at[:, pl.ds(pl.multiple_of(owner * width, width), width)]

    exchange = {
        slot: start(
            proj_part(turned(slot, 1 - core)), mine.at[slot], core_send.at[slot], core_recv.at[slot], {"dp": sibling}
        )
        for slot in (3, 1, 2, 0)
    }

    def line(slot, step, part):
        return pltpu.make_async_remote_copy(
            src_ref=mine.at[slot], dst_ref=near.at[part], send_sem=line_send.at[part], recv_sem=line_recv.at[part],
            device_id={"dp": turned(step, core)}, device_id_type=MESH,
        )

    def term(owner, part):
        return first_ref.at[pl.ds(pl.multiple_of(owner * rows + part * half, half), half)]

    def rows_at(owner, part):
        return term(owner, part)[...].astype(wide)

    plan = [
        (term(corner, 0), square_x.at[1], square[0]),
        (term(corner, 1), square_y.at[1], square[1]),
        (term(along_x, 0), square_x.at[0], square[0]),
        (term(along_y, 1), square_y.at[0], square[1]),
    ]
    copies = [
        start(source, target, square_send.at[i], square_recv.at[i], device)
        for i, (source, target, device) in enumerate(plan)
    ]
    for slot in (3, 1, 2):
        exchange[slot].wait_recv()
        mine[slot] = (mine[slot].astype(wide) + proj_part(turned(slot, core))[...].astype(wide)).astype(low)
        if slot == 3:

            @pl.when(chip == 0)
            def _():
                line(3, 1, 0).start()

            @pl.when((chip == 1) | (chip == 2))
            def _():
                line(3, 3, 3).start()

        elif slot == 1:

            @pl.when(chip == 3)
            def _():
                line(1, 3, 0).start()

            @pl.when((chip == 1) | (chip == 2))
            def _():
                line(1, 1, 1).start()

        else:

            @pl.when((chip == 0) | (chip == 3))
            def _():
                line(2, 2, 2).start()

    bias_mine[...] = bias_ref[...]
    bias_copies = [start(bias_mine, bias_came, bias_send.at[0], bias_recv.at[0], {"dp": sibling})]
    bias_copies[0].wait_recv()
    bias_slots[chip] = bias_mine[...] + bias_came[...]
    bias_copies += [
        start(bias_slots.at[chip], bias_slots.at[chip], bias_send.at[1 + i], bias_recv.at[1 + i], chips[i])
        for i in range(3)
    ]
    copies[0].wait_recv()
    staged[0] = (rows_at(along_y, 0) + square_x[1].astype(wide)).astype(low)
    copies.append(start(staged.at[0], square_last.at[0], square_send.at[4], square_recv.at[4], square[1]))
    copies[1].wait_recv()
    staged[1] = (rows_at(along_x, 1) + square_y[1].astype(wide)).astype(low)
    copies.append(start(staged.at[1], square_last.at[1], square_send.at[5], square_recv.at[5], square[0]))

    @pl.when((chip == 1) | (chip == 2))
    def _():
        line(0, 1, 0).wait_recv()
        mine[2] = (mine[2].astype(wide) + near[0].astype(wide)).astype(low)
        line(2, 2, 2).start()

    @pl.when(chip == 0)
    def _():
        line(3, 1, 0).wait_send()
        line(1, 1, 1).start()

    @pl.when(chip == 3)
    def _():
        line(1, 3, 0).wait_send()
        line(3, 3, 3).start()

    gain = gain_ref[...]
    vector_gain = jnp.zeros_like(gain)
    vector_shift = jnp.zeros_like(gain)
    for part, came in enumerate((square_x, square_y)):
        here = slice(part * half, (part + 1) * half)
        copies[2 + part].wait_recv()
        copies[4 + part].wait_recv()
        grad = rows_at(place, part) + came[0].astype(wide) + square_last[part].astype(wide)
        normed = normed_ref[here, :]
        vector_gain += jnp.sum(grad * normed, 0, keepdims=True)
        vector_shift += jnp.sum(grad, 0, keepdims=True)
        scaled = grad * gain
        inner = (
            scaled
            - jnp.mean(scaled, -1, keepdims=True)
            - normed * jnp.mean(scaled * normed, -1, keepdims=True)
        )
        step_out[here, :] = recip_ref[here, :] * inner
    corners[place, 0:1, :] = vector_gain
    corners[place, 1:2, :] = second_ref[0:1, :]
    corners[place, 2:3, :] = vector_shift
    corners[place, 3:4, :] = second_ref[1:2, :]
    vector_copies = [
        start(corners.at[place], corners.at[place], vector_send.at[i], vector_recv.at[i], square[i]) for i in range(3)
    ]
    for copy in vector_copies:
        copy.wait_recv()
    vector_mine[...] = (corners[0] + corners[1]) + (corners[2] + corners[3])
    vector_copies.append(start(vector_mine, vector_came, vector_send.at[3], vector_recv.at[3], {"dp": sibling}))
    vector_copies[3].wait_recv()
    vector_slots[chip] = vector_mine[...] + vector_came[...]
    vector_copies += [
        start(vector_slots.at[chip], vector_slots.at[chip], vector_send.at[4 + i], vector_recv.at[4 + i], chips[i])
        for i in range(3)
    ]
    for copy in vector_copies[4:] + bias_copies[1:]:
        copy.wait_recv()
    vector_out[...] = (vector_slots[0] + vector_slots[1]) + (vector_slots[2] + vector_slots[3])
    bias_out[...] = (bias_slots[0] + bias_slots[1]) + (bias_slots[2] + bias_slots[3])

    exchange[0].wait_recv()
    line(2, 2, 2).wait_recv()

    @pl.when(chip > 0)
    def _():
        line(1, 1, 1).wait_recv()

    @pl.when(chip < 3)
    def _():
        line(3, 3, 3).wait_recv()

    total = proj_part(turned(0, core))[...].astype(wide) + mine[0].astype(wide) + near[2].astype(wide)
    total = total + jnp.where(chip > 0, near[1].astype(wide), 0.0)
    proj_out[...] = total + jnp.where(chip < 3, near[3].astype(wide), 0.0)
    for copy in copies + vector_copies + bias_copies + list(exchange.values()):
        copy.wait_send()
    line(2, 2, 2).wait_send()

    @pl.when(chip < 3)
    def _():
        line(1, 1, 1).wait_send()

    @pl.when(chip > 0)
    def _():
        line(3, 3, 3).wait_send()


def last_reduce(first, proj, normed, recip, gain, second, bias):
    dma = pltpu.SemaphoreType.DMA
    low, wide = jnp.bfloat16, jnp.float32
    shape, vmem = jax.ShapeDtypeStruct, pltpu.VMEM
    rows, model = normed.shape
    pair = vmem((2, rows // 2, model), low)
    blocks = vmem((4, proj.shape[0], proj.shape[1] // 8), low)
    return pl.pallas_call(
        last_kernel,
        out_shape=(
            shape((rows, model), wide),
            shape((proj.shape[0], proj.shape[1] // 8), wide),
            shape((4, model), wide),
            shape(bias.shape, wide),
        ),
        in_specs=[pl.BlockSpec(memory_space=pltpu.VMEM)] * 7,
        out_specs=(pl.BlockSpec(memory_space=pltpu.VMEM),) * 4,
        scratch_shapes=[
            pair, pair, pair, pair, blocks, blocks,
            vmem((4, 4, model), wide),
            vmem((4, model), wide),
            vmem((4, model), wide),
            vmem((4, 4, model), wide),
            vmem(bias.shape, wide),
            vmem(bias.shape, wide),
            vmem((4, *bias.shape), wide),
            dma((6,)), dma((6,)), dma((7,)), dma((7,)), dma((4,)), dma((4,)),
            dma((4,)), dma((4,)), dma((4,)), dma((4,)),
        ],
        compiler_params=pltpu.CompilerParams(
            collective_id=3, has_side_effects=True, vmem_limit_bytes=40 * 1024 * 1024
        ),
        cost_estimate=pl.CostEstimate(flops=0, bytes_accessed=120_000_000, transcendentals=0),
        name="last_reduce",
    )(first, proj, normed, recip, gain, second, bias)


def after(late, early):
    return lax.optimization_barrier((late, early))[0]


class Plain:
    def gather_rows(self, block):
        return lax.all_gather(block, "tensor", axis=0, tiled=True)

    def reduce_rows(self, terms, ready, name):
        return lax.psum_scatter(terms, "tensor", scatter_dimension=0, tiled=True).astype(jnp.float32)

    def begin(self, x, gain, shift, dy, bias, w_qkv, w_output, gate_up, down):
        low = jnp.bfloat16
        out, normed, recip = layer_norm(x.astype(jnp.float32), gain, shift)
        return (
            self.gather_rows(out.astype(low)),
            self.gather_rows(dy),
            lax.all_gather(bias, "dp", axis=2, tiled=True),
            gather_dp(w_qkv.astype(low), 1),
            gather_dp(w_output.astype(low), 1),
            normed,
            recip,
            gate_up.astype(low),
            down.astype(low),
        )

    def reduce_beside(self, terms):
        return (self.reduce_rows(terms, None, 0),)

    def back(self, terms, ready, resid, gain, dy):
        grad = self.reduce_rows(terms, None, 0)
        _, normed, recip = layer_norm(resid, gain, gain)
        total = dy.astype(jnp.float32) + norm_back(grad, normed, recip, gain)
        sums = jnp.stack([jnp.sum(grad * normed, 0), jnp.sum(grad, 0)])
        return self.gather_rows(total.astype(jnp.bfloat16)), total, sums

    def finish(self, first, proj, normed, recip, gain, second, bias):
        first = self.reduce_rows(first, None, 0)
        vectors = jnp.stack([jnp.sum(first * normed, 0), second[0], jnp.sum(first, 0), second[1]])
        step = norm_back(first, normed, recip, gain)
        return step, scatter_dp(proj, 1), lax.psum(vectors, ("dp", "tensor")), lax.psum(bias, "dp")


class Line(Plain):
    def gather_rows(self, block):
        return square_gather(block)

    def reduce_rows(self, terms, ready, name):
        return square_reduce(terms, ready, name)

    def begin(self, x, gain, shift, dy, bias, w_qkv, w_output, gate_up, down):
        parts, heads, few = bias.shape
        a, dy, came, *others = start_gather(
            x, gain.reshape(1, -1), shift.reshape(1, -1), dy, self.flat(bias), w_qkv, w_output, gate_up, down
        )
        came = came.reshape(8, -1)[:, : parts * heads * few].reshape(8, parts, heads, few)
        return a, dy, came.transpose(1, 2, 0, 3).reshape(parts, heads, -1), *others

    def flat(self, values):
        values = values.astype(jnp.float32).reshape(-1)
        width = -(-values.shape[0] // 1024) * 1024
        return jnp.pad(values, (0, width - values.shape[0])).reshape(8, -1)

    def reduce_beside(self, terms):
        me = lax.axis_index("tensor")
        rows = terms.shape[0] // 4
        parts = [lax.dynamic_slice_in_dim(terms, (me ^ step) * rows, rows, 0) for step in range(4)]
        for step in (3, 1, 2):
            parts[step] = lax.ppermute(parts[step], "tensor", [(i, i ^ step) for i in range(4)])
        return tuple(parts)

    def back(self, terms, ready, resid, gain, dy):
        return square_back(terms, ready, resid, gain.reshape(1, -1), dy)

    def finish(self, first, proj, normed, recip, gain, second, bias):
        step, proj_grad, vectors, total = last_reduce(
            first, proj, normed, recip, gain.reshape(1, -1), second, self.flat(bias)
        )
        return step, proj_grad, vectors, total.reshape(-1)[: bias.size].reshape(bias.shape)


def row_major(values):
    return with_layout_constraint(values, Layout(tuple(range(values.ndim))))


def gather_dp(block, axis):
    return row_major(lax.all_gather(block.astype(jnp.bfloat16), "dp", axis=axis, tiled=True))


def scatter_dp(terms, axis):
    return lax.psum_scatter(terms.astype(jnp.bfloat16), "dp", scatter_dimension=axis, tiled=True)


def local(
    routes,
    inputs,
    cotangent,
    gains,
    shifts,
    qkv_weight,
    biases,
    out_weight,
    gate_up,
    down_weight,
    momentum_gains,
    momentum_shifts,
    momentum_qkv,
    momentum_biases,
    momentum_out,
    momentum_gate,
    momentum_down,
    variance_gains,
    variance_shifts,
    variance_qkv,
    variance_biases,
    variance_out,
    variance_gate,
    variance_down,
):
    low = jnp.bfloat16
    local_heads = biases.shape[1]
    local_width = qkv_weight.shape[2]
    head_size = local_width // local_heads
    xin = inputs.astype(jnp.float32)
    a_all, dy_all, bias_all, w_qkv, w_output, first_normed, first_recip, gate_low, down_low = routes.begin(
        inputs, gains[0], shifts[0], cotangent, biases.astype(low), qkv_weight, out_weight, gate_up, down_weight
    )
    bias_all = bias_all.reshape(3, local_width).astype(jnp.float32)
    w_gate_up = gather_dp(after(gate_low, w_output), 1)
    lin = jnp.einsum("rd,kdc->krc", a_all, w_qkv, preferred_element_type=jnp.float32)
    qkv, heads, logs = attention_forward(lin, bias_all, head_size)
    resid = xin + routes.reduce_rows(mxu(heads, w_output, NN).astype(low), logs, 4)
    second_out, _, _ = layer_norm(resid, gains[1], shifts[1])
    m_all = routes.gather_rows(second_out.astype(low))
    w_down = gather_dp(after(down_low, (w_gate_up, m_all)), 1)
    gate_vals = jnp.einsum("rd,kdc->krc", m_all, w_gate_up, preferred_element_type=jnp.float32)
    gate_lin, upward = gate_vals[0], gate_vals[1]
    sigmoid_gate = jax.nn.sigmoid(gate_lin)
    silu_gate = gate_lin * sigmoid_gate
    hidden = (silu_gate * upward).astype(low)
    down_terms = mxu(hidden, dy_all, TN).astype(low)
    down_grad = scatter_dp(down_terms, 1)
    w_down = after(w_down, down_terms)
    block_terms = mxu(hidden, w_down, NN).astype(low)
    down_parts = routes.reduce_beside(block_terms)
    hidden_grad = mxu(dy_all, after(w_down, block_terms), NT)
    gate_grad_low = (
        hidden_grad * upward * sigmoid_gate * (1.0 + gate_lin * (1.0 - sigmoid_gate))
    ).astype(low)
    up_grad_low = (hidden_grad * silu_gate).astype(low)
    both_grads = jnp.stack([gate_grad_low, up_grad_low], 0)
    gate_terms = jnp.einsum("rd,krc->kdc", m_all, both_grads, preferred_element_type=jnp.float32)
    gate_terms = row_major(gate_terms.astype(low))
    second_terms = jnp.einsum(
        "krc,kdc->rd", both_grads, w_gate_up, preferred_element_type=jnp.float32
    ).astype(low)
    gate_grad = scatter_dp(after(gate_terms, (down_grad, second_terms, down_parts)), 1)
    resid_full, resid_grad, second_sums = routes.back(
        after(second_terms, down_grad), down_grad[:16, :128], resid, gains[1], cotangent
    )
    out_terms = mxu(heads, resid_full, TN).astype(low)
    heads_grad = mxu(resid_full, w_output, NT).astype(low)
    lin_grads, bias_terms = attention_backward(qkv, heads_grad, logs, head_size)
    qkv_terms = jnp.einsum("rd,krc->kdc", a_all, lin_grads, preferred_element_type=jnp.float32)
    qkv_terms = row_major(qkv_terms.astype(low))
    first_terms = jnp.einsum(
        "krc,kdc->rd", lin_grads, w_qkv, preferred_element_type=jnp.float32
    ).astype(low)
    qkv_grad = scatter_dp(after(qkv_terms, gate_grad), 1)
    input_step, out_grad, vectors, bias_sum = routes.finish(
        first_terms,
        out_terms,
        first_normed,
        first_recip,
        gains[0],
        second_sums,
        bias_terms,
    )
    input_grad = resid_grad + input_step
    block_out = resid
    for part in after(down_parts, vectors):
        block_out = block_out + part.astype(jnp.float32)
    block_out = block_out.astype(low)
    gains_grad, shifts_grad = vectors[:2], vectors[2:]
    down_grad, gate_grad, out_grad = (
        grad.astype(jnp.float32) for grad in (*after((down_grad, gate_grad), vectors), out_grad)
    )
    qkv_grad = qkv_grad.astype(jnp.float32)
    per_dp = biases.shape[2]
    biases_grad = lax.dynamic_slice_in_dim(
        bias_sum.reshape(3, local_heads, head_size), lax.axis_index("dp") * per_dp, per_dp, 2
    )
    gain_new = adamw(gains, gains_grad, momentum_gains, variance_gains, 0.0, vector_rate)
    shift_new = adamw(shifts, shifts_grad, momentum_shifts, variance_shifts, 0.0, vector_rate)
    qkv_new = adamw(qkv_weight, qkv_grad, momentum_qkv, variance_qkv, decay_rate, learn_rate)
    bias_new = adamw(biases, biases_grad, momentum_biases, variance_biases, 0.0, vector_rate)
    out_new = adamw(out_weight, out_grad, momentum_out, variance_out, decay_rate, learn_rate)
    gate_new = adamw(gate_up, gate_grad, momentum_gate, variance_gate, decay_rate, learn_rate)
    down_new = adamw(down_weight, down_grad, momentum_down, variance_down, decay_rate, learn_rate)
    return (
        block_out,
        input_grad,
        gains_grad,
        shifts_grad,
        qkv_grad,
        biases_grad,
        out_grad,
        gate_grad,
        down_grad,
        gain_new[0],
        shift_new[0],
        qkv_new[0],
        bias_new[0],
        out_new[0],
        gate_new[0],
        down_new[0],
        gain_new[1],
        shift_new[1],
        qkv_new[1],
        bias_new[1],
        out_new[1],
        gate_new[1],
        down_new[1],
        gain_new[2],
        shift_new[2],
        qkv_new[2],
        bias_new[2],
        out_new[2],
        gate_new[2],
        down_new[2],
    )


def solution(mesh):
    routes = Line() if dict(mesh.shape) == {"dp": 8, "tensor": 4} else Plain()

    def step(*arrays):
        return local(routes, *arrays)

    return jax.shard_map(
        step,
        mesh=mesh,
        in_specs=(
            P(("dp", "tensor"), None),
            P(("dp", "tensor"), None),
            P(),
            P(),
            P(None, "dp", "tensor"),
            P(None, "tensor", "dp"),
            P("tensor", "dp"),
            P(None, "dp", "tensor"),
            P("tensor", "dp"),
            P(),
            P(),
            P(None, "dp", "tensor"),
            P(None, "tensor", "dp"),
            P("tensor", "dp"),
            P(None, "dp", "tensor"),
            P("tensor", "dp"),
            P(),
            P(),
            P(None, "dp", "tensor"),
            P(None, "tensor", "dp"),
            P("tensor", "dp"),
            P(None, "dp", "tensor"),
            P("tensor", "dp"),
        ),
        out_specs=(
            P(("dp", "tensor"), None),
            P(("dp", "tensor"), None),
            P(),
            P(),
            P(None, "dp", "tensor"),
            P(None, "tensor", "dp"),
            P("tensor", "dp"),
            P(None, "dp", "tensor"),
            P("tensor", "dp"),
            P(),
            P(),
            P(None, "dp", "tensor"),
            P(None, "tensor", "dp"),
            P("tensor", "dp"),
            P(None, "dp", "tensor"),
            P("tensor", "dp"),
            P(),
            P(),
            P(None, "dp", "tensor"),
            P(None, "tensor", "dp"),
            P("tensor", "dp"),
            P(None, "dp", "tensor"),
            P("tensor", "dp"),
            P(),
            P(),
            P(None, "dp", "tensor"),
            P(None, "tensor", "dp"),
            P("tensor", "dp"),
            P(None, "dp", "tensor"),
            P("tensor", "dp"),
        ),
        check_vma=False,
    )
```

```python
import functools

import jax
import jax.numpy as jnp
import numpy as np
from jax import lax
from jax.experimental import pallas as pl
from jax.experimental.layout import Layout, with_layout_constraint
from jax.experimental.pallas import tpu as pltpu
from jax.sharding import PartitionSpec as P

ROT = 16
SEQ = 1024
ADAM_STEP = 3


norm_eps = 1e-05
learn_rate = 0.03
vector_rate = 0.25
decay_rate = 0.1
adam_eps = 1e-08


def layer_norm(values, gain, shift):
    centred = values - jnp.mean(values, -1, keepdims=True)
    recip = lax.rsqrt(jnp.mean(centred * centred, -1, keepdims=True) + norm_eps)
    normed = centred * recip
    return (normed * gain + shift, normed, recip)


def norm_back(grad, normed, recip, gain):
    scaled = grad * gain
    inner = (
        scaled
        - jnp.mean(scaled, -1, keepdims=True)
        - normed * jnp.mean(scaled * normed, -1, keepdims=True)
    )
    return recip * inner


def adamw(weight, grad, moment, second, decay, rate):
    moment_new = 0.9 * moment + 0.1 * grad
    second_new = 0.95 * second + 0.05 * grad * grad
    fixed_one = 1.0 - 0.9**ADAM_STEP
    fixed_two = 1.0 - 0.95**ADAM_STEP
    change = moment_new / fixed_one / (jnp.sqrt(second_new / fixed_two) + adam_eps) + decay * weight
    return (weight - rate * change, moment_new, second_new)


def lane_head(shape, head_size):
    return lax.broadcasted_iota(jnp.int32, shape, len(shape) - 1) // head_size


def turn(values, tables, sign=1.0):
    width = values.shape[-1]
    own, ahead, behind = (jnp.concatenate([table] * (width // table.shape[-1]), 1) for table in tables)
    ahead = pltpu.roll(values, width - ROT // 2, 1) * ahead
    behind = pltpu.roll(values, ROT // 2, 1) * behind
    return values * own + sign * (ahead + behind)


def turn_tables(head_size):
    halfway = ROT // 2
    lane = np.arange(max(128, head_size)) % head_size
    position = np.arange(SEQ).astype(np.float32)
    frequency = np.power(np.float32(10000.0), -2.0 * (lane % halfway).astype(np.float32) / ROT)
    angles = position[:, None] * frequency.astype(np.float32)[None, :]
    cosine, sine = np.cos(angles), np.sin(angles)
    tables = [
        np.where(lane < ROT, cosine, 1.0),
        np.where(lane < halfway, -sine, 0.0),
        np.where((lane >= halfway) & (lane < ROT), sine, 0.0),
    ]
    return jnp.asarray(np.stack(tables).astype(np.float32))


LOG2E = 1.4426950408889634
NT = (((1,), (1,)), ((), ()))
NN = (((1,), (0,)), ((), ()))
TN = (((0,), (0,)), ((), ()))


def mxu(left, right, dims):
    return lax.dot_general(left, right, dims, preferred_element_type=jnp.float32)


def forward_kernel(head_size, lin_ref, bias_ref, table_ref, qkv_ref, out_ref, lse_ref):
    rows, width = out_ref.shape
    low = jnp.bfloat16
    step = min(256, rows)
    for part in range(3):
        for begin in range(0, rows, step):
            here = slice(begin, begin + step)
            values = lin_ref[part, here, :] + bias_ref[part : part + 1, :]
            if part < 2:
                values = turn(values, [table_ref[i, here, :] for i in range(3)])
            qkv_ref[part, here, :] = values.astype(low)
    owner = lane_head((step, width), head_size)
    lanes = lax.broadcasted_iota(jnp.int32, (step, 128), 1)
    for begin in range(0, rows, step):
        end = begin + step
        query = qkv_ref[0, begin:end, :]
        result = jnp.zeros((step, width), jnp.float32)
        logs = jnp.zeros((step, 128), jnp.float32)
        keep = lax.broadcasted_iota(jnp.int32, (step, step), 0) >= lax.broadcasted_iota(
            jnp.int32, (step, step), 1
        )
        for head in range(width // head_size):
            mine = jnp.where(owner == head, query, jnp.zeros_like(query))
            scores = mxu(mine, qkv_ref[1, :end, :], NT)
            last = jnp.where(keep, scores[:, begin:], -1e30)
            scores = jnp.concatenate([scores[:, :begin], last], 1) if begin else last
            top = jnp.max(scores, 1, keepdims=True)
            expo = jnp.exp2((scores - top) * (0.125 * LOG2E))
            total = jnp.sum(expo, 1, keepdims=True)
            found = mxu(expo.astype(low), qkv_ref[2, :end, :], NN)
            result = jnp.where(owner == head, found / total, result)
            logs = jnp.where(lanes == head, top * (0.125 * LOG2E) + jnp.log2(total), logs)
        out_ref[begin:end, :] = result.astype(low)
        lse_ref[:, begin:end] = logs.T[:8]


def attention_forward(lin, bias, head_size):
    _, rows, width = lin.shape
    lanes = min(256, width)
    groups = width // lanes
    tables = turn_tables(head_size)
    low = jnp.bfloat16
    return pl.pallas_call(
        functools.partial(forward_kernel, head_size),
        grid=(rows // SEQ, groups),
        out_shape=(
            jax.ShapeDtypeStruct((3, rows, width), low),
            jax.ShapeDtypeStruct((rows, width), low),
            jax.ShapeDtypeStruct((groups, 8, rows), jnp.float32),
        ),
        in_specs=[
            pl.BlockSpec((3, SEQ, lanes), lambda i, j: (0, i, j)),
            pl.BlockSpec((3, lanes), lambda i, j: (0, j)),
            pl.BlockSpec(tables.shape, lambda i, j: (0, 0, 0)),
        ],
        out_specs=(
            pl.BlockSpec((3, SEQ, lanes), lambda i, j: (0, i, j)),
            pl.BlockSpec((SEQ, lanes), lambda i, j: (i, j)),
            pl.BlockSpec((None, 8, SEQ), lambda i, j: (j, 0, i)),
        ),
        compiler_params=pltpu.CompilerParams(vmem_limit_bytes=48 * 1024 * 1024),
        cost_estimate=pl.CostEstimate(
            flops=rows * SEQ * width * 8, bytes_accessed=rows * width * 26, transcendentals=0
        ),
        name="attend_forward",
    )(lin, bias, tables)


def backward_kernel(head_size, qkv_ref, grad_ref, lse_ref, table_ref, out_ref, sum_ref, acc_ref):
    _, rows, width = qkv_ref.shape
    low = jnp.bfloat16
    step = min(256, rows)
    owner = lane_head((step, width), head_size)
    acc_ref[...] = jnp.zeros_like(acc_ref)
    blank = jnp.zeros((step, width), low)
    for begin in range(0, rows, step):
        end = begin + step
        query = qkv_ref[0, begin:end, :]
        grad = grad_ref[begin:end, :]
        keep = lax.broadcasted_iota(jnp.int32, (step, step), 1) >= lax.broadcasted_iota(
            jnp.int32, (step, step), 0
        )
        query_grad = jnp.zeros((step, width), jnp.float32)
        for head in range(width // head_size):
            mine = jnp.where(owner == head, query, blank)
            grad_mine = jnp.where(owner == head, grad, blank)
            scores = mxu(qkv_ref[1, :end, :], mine, NT)
            expo = jnp.exp2(scores * (0.125 * LOG2E) - lse_ref[head : head + 1, begin:end])
            last = jnp.where(keep, expo[begin:, :], 0.0)
            probs = jnp.concatenate([expo[:begin], last], 0) if begin else last
            prob_grad = mxu(qkv_ref[2, :end, :], grad_mine, NT)
            inner = jnp.sum(probs * prob_grad, 0, keepdims=True)
            score_grad = (probs * (prob_grad - inner)).astype(low)
            acc_ref[0, :end, :] += mxu(score_grad, mine, NN)
            acc_ref[1, :end, :] += mxu(probs.astype(low), grad_mine, NN)
            found = mxu(score_grad, qkv_ref[1, :end, :], TN)
            query_grad = jnp.where(owner == head, found, query_grad)
        turned = turn(0.125 * query_grad, [table_ref[i, begin:end, :] for i in range(3)], -1.0).astype(low)
        out_ref[0, begin:end, :] = turned
        added = jnp.sum(turned.astype(jnp.float32), 0, keepdims=True)
        sum_ref[0:1, :] = added if begin == 0 else sum_ref[0:1, :] + added
    for begin in range(0, rows, step):
        here = slice(begin, begin + step)
        turned = turn(0.125 * acc_ref[0, here, :], [table_ref[i, here, :] for i in range(3)], -1.0).astype(low)
        out_ref[1, here, :] = turned
        added = jnp.sum(turned.astype(jnp.float32), 0, keepdims=True)
        sum_ref[1:2, :] = added if begin == 0 else sum_ref[1:2, :] + added
        turned = acc_ref[1, here, :].astype(low)
        out_ref[2, here, :] = turned
        added = jnp.sum(turned.astype(jnp.float32), 0, keepdims=True)
        sum_ref[2:3, :] = added if begin == 0 else sum_ref[2:3, :] + added


def attention_backward(qkv, grad, logs, head_size):
    _, rows, width = qkv.shape
    lanes = min(256, width)
    groups = width // lanes
    tables = turn_tables(head_size)
    low = jnp.bfloat16
    grads, sums = pl.pallas_call(
        functools.partial(backward_kernel, head_size),
        grid=(rows // SEQ, groups),
        out_shape=(
            jax.ShapeDtypeStruct((3, rows, width), low),
            jax.ShapeDtypeStruct((rows // SEQ, 3, width), jnp.float32),
        ),
        in_specs=[
            pl.BlockSpec((3, SEQ, lanes), lambda i, j: (0, i, j)),
            pl.BlockSpec((SEQ, lanes), lambda i, j: (i, j)),
            pl.BlockSpec((None, 8, SEQ), lambda i, j: (j, 0, i)),
            pl.BlockSpec(tables.shape, lambda i, j: (0, 0, 0)),
        ],
        out_specs=(
            pl.BlockSpec((3, SEQ, lanes), lambda i, j: (0, i, j)),
            pl.BlockSpec((None, 3, lanes), lambda i, j: (i, 0, j)),
        ),
        scratch_shapes=[pltpu.VMEM((2, SEQ, lanes), jnp.float32)],
        compiler_params=pltpu.CompilerParams(vmem_limit_bytes=48 * 1024 * 1024),
        cost_estimate=pl.CostEstimate(
            flops=rows * SEQ * width * 20, bytes_accessed=rows * width * 26, transcendentals=0
        ),
        name="attend_backward",
    )(qkv, grad, logs, tables)
    return grads, jnp.sum(sums, 0)


MESH = pl.DeviceIdType.MESH


def partners():
    me = lax.axis_index("tensor")
    return me, me + 1 - 2 * (me % 2), (me + 2) % 4


def greet(devices):
    barrier = pltpu.get_barrier_semaphore()
    for device in devices:
        pl.semaphore_signal(barrier, inc=1, device_id={"tensor": device}, device_id_type=MESH)
    pl.semaphore_wait(barrier, len(devices))


def gather_kernel(block_ref, whole_ref, send_sem, recv_sem, local_sem):
    me, along_x, along_y = partners()
    rows = block_ref.shape[0]
    half = rows // 2

    def part(owner, which):
        return whole_ref.at[pl.ds(pl.multiple_of(owner * rows + which * half, half), half)]

    def send(source, owner, which, target, index):
        copy = pltpu.make_async_remote_copy(
            src_ref=source,
            dst_ref=part(owner, which),
            send_sem=send_sem.at[index],
            recv_sem=recv_sem.at[index],
            device_id={"tensor": target},
            device_id_type=MESH,
        )
        copy.start()
        return copy

    mine = pltpu.make_async_copy(block_ref, whole_ref.at[pl.ds(pl.multiple_of(me * rows, rows), rows)], local_sem)
    mine.start()
    greet((along_x, along_y))
    halves = [block_ref.at[pl.ds(0, half)], block_ref.at[pl.ds(half, half)]]
    x_first = send(halves[0], me, 0, along_x, 0)
    y_first = send(halves[1], me, 1, along_y, 1)
    x_second = send(halves[1], me, 1, along_x, 2)
    y_second = send(halves[0], me, 0, along_y, 3)
    x_first.wait_recv()
    y_third = send(part(along_x, 0), along_x, 0, along_y, 4)
    y_first.wait_recv()
    x_third = send(part(along_y, 1), along_y, 1, along_x, 5)
    for copy in (x_second, y_second, y_third, x_third):
        copy.wait_recv()
    for copy in (x_first, y_first, x_second, y_second, y_third, x_third):
        copy.wait_send()
    mine.wait()


def square_gather(block):
    rows, width = block.shape
    return pl.pallas_call(
        gather_kernel,
        out_shape=jax.ShapeDtypeStruct((4 * rows, width), block.dtype),
        in_specs=[pl.BlockSpec(memory_space=pltpu.VMEM)],
        out_specs=pl.BlockSpec(memory_space=pl.ANY),
        scratch_shapes=[
            pltpu.SemaphoreType.DMA((6,)),
            pltpu.SemaphoreType.DMA((6,)),
            pltpu.SemaphoreType.DMA,
        ],
        compiler_params=pltpu.CompilerParams(collective_id=0, has_side_effects=True),
        cost_estimate=pl.CostEstimate(flops=0, bytes_accessed=rows * width * 120, transcendentals=0),
        name="square_gather",
    )(block)


def reduce_kernel(terms_ref, ready_ref, out_ref, first_x, first_y, staged, second, send_sem, recv_sem):
    del ready_ref
    me, along_x, along_y = partners()
    rows = out_ref.shape[0]
    half = rows // 2
    corner = 3 - me

    def term(owner, which):
        return terms_ref.at[pl.ds(pl.multiple_of(owner * rows + which * half, half), half)]

    def send(source, target_ref, target, index):
        copy = pltpu.make_async_remote_copy(
            src_ref=source,
            dst_ref=target_ref,
            send_sem=send_sem.at[index],
            recv_sem=recv_sem.at[index],
            device_id={"tensor": target},
            device_id_type=MESH,
        )
        copy.start()
        return copy

    greet((along_x, along_y))
    x_on = send(term(corner, 0), first_x.at[1], along_x, 0)
    y_on = send(term(corner, 1), first_y.at[1], along_y, 1)
    x_own = send(term(along_x, 0), first_x.at[0], along_x, 2)
    y_own = send(term(along_y, 1), first_y.at[0], along_y, 3)

    def added(one, two):
        return (one.astype(jnp.float32) + two.astype(jnp.float32)).astype(jnp.bfloat16)

    x_on.wait_recv()
    staged[0] = added(term(along_y, 0)[...], first_x[1])
    y_last = send(staged.at[0], second.at[0], along_y, 4)
    y_on.wait_recv()
    staged[1] = added(term(along_x, 1)[...], first_y[1])
    x_last = send(staged.at[1], second.at[1], along_x, 5)
    x_own.wait_recv()
    out_ref[:half] = term(me, 0)[...].astype(jnp.float32) + first_x[0].astype(jnp.float32)
    y_own.wait_recv()
    out_ref[half:] = term(me, 1)[...].astype(jnp.float32) + first_y[0].astype(jnp.float32)
    y_last.wait_recv()
    out_ref[:half] += second[0].astype(jnp.float32)
    x_last.wait_recv()
    out_ref[half:] += second[1].astype(jnp.float32)
    for copy in (x_on, y_on, x_own, y_own, y_last, x_last):
        copy.wait_send()


def square_reduce(terms, ready, name):
    rows, width = terms.shape[0] // 4, terms.shape[1]
    part = pltpu.VMEM((2, rows // 2, width), jnp.bfloat16)
    return pl.pallas_call(
        reduce_kernel,
        out_shape=jax.ShapeDtypeStruct((rows, width), jnp.float32),
        in_specs=[pl.BlockSpec(memory_space=pltpu.VMEM), pl.BlockSpec(memory_space=pl.ANY)],
        out_specs=pl.BlockSpec(memory_space=pltpu.VMEM),
        scratch_shapes=[
            part,
            part,
            part,
            part,
            pltpu.SemaphoreType.DMA((6,)),
            pltpu.SemaphoreType.DMA((6,)),
        ],
        compiler_params=pltpu.CompilerParams(
            collective_id=name, has_side_effects=True, vmem_limit_bytes=24 * 1024 * 1024
        ),
        cost_estimate=pl.CostEstimate(flops=0, bytes_accessed=rows * width * 240, transcendentals=0),
        name="square_reduce",
    )(terms, ready)


def start_kernel(
    x_from, gain_ref, shift_ref, dy_from, bias_ref, wq_from, wo_from, gate_from, down_from,
    a_all, dy_all, bias_all, wq_all, wo_all, normed_out, recip_out, gate_out, down_out,
    a_ref, wq_ref, wo_ref, x_ref, dy_ref, wq_wide, wo_wide, gate_wide, down_wide,
    square_send, square_recv, bias_send, bias_recv, line_send, line_recv, core_send, core_recv, local_sem,
):
    place, along_x, along_y = partners()
    me = lax.axis_index("dp")
    chip, core = me // 2, me % 2
    sibling = me + 1 - 2 * core
    rows = a_ref.shape[0]
    low = jnp.bfloat16
    half = rows // 2
    depth = wq_ref.shape[1]

    def start(source, target, send_sem, recv_sem, device):
        copy = pltpu.make_async_remote_copy(
            src_ref=source, dst_ref=target, send_sem=send_sem, recv_sem=recv_sem,
            device_id=device, device_id_type=MESH,
        )
        copy.start()
        return copy

    def piece(part, owner):
        if part < 3:
            return wq_all.at[part, pl.ds(pl.multiple_of(owner * depth, depth), depth)]
        width = wo_ref.shape[1]
        return wo_all.at[:, pl.ds(pl.multiple_of(owner * width, width), width)]

    def own(part):
        return wq_ref.at[part] if part < 3 else wo_ref

    def turned(step):
        return 2 * ((chip + step) % 4) + core

    moves = (
        (wq_from, wq_wide), (wo_from, wo_wide), (x_from, x_ref), (dy_from, dy_ref), (gate_from, gate_wide),
        (down_from, down_wide),
    )
    here = [pltpu.make_async_copy(source, target, local_sem.at[6 + i]) for i, (source, target) in enumerate(moves)]
    for copy in here:
        copy.start()
    bias_all[me] = bias_ref[...].astype(low).astype(jnp.float32)

    barrier = pltpu.get_barrier_semaphore()
    for step in range(1, 8):
        pl.semaphore_signal(barrier, inc=1, device_id={"dp": (me + step) % 8}, device_id_type=MESH)
    for device in (along_x, along_y):
        pl.semaphore_signal(barrier, inc=1, device_id={"tensor": device}, device_id_type=MESH)
    here[0].wait()
    wq_ref[...] = wq_wide[...].astype(low)
    here[1].wait()
    wo_ref[...] = wo_wide[...].astype(low)
    pl.semaphore_wait(barrier, 9)

    def rows_of(whole, owner, which):
        return whole.at[pl.ds(pl.multiple_of(owner * rows + which * half, half), half)]

    def square_first(block, whole, base):
        halves = [block.at[pl.ds(0, half)], block.at[pl.ds(half, half)]]
        plan = [(0, along_x), (1, along_y), (1, along_x), (0, along_y)]
        return [
            start(halves[which], rows_of(whole, place, which), square_send.at[base + i], square_recv.at[base + i], {"tensor": device})
            for i, (which, device) in enumerate(plan)
        ]

    def square_next(whole, base, copies):
        copies[0].wait_recv()
        on_y = start(rows_of(whole, along_x, 0), rows_of(whole, along_x, 0), square_send.at[base + 4], square_recv.at[base + 4], {"tensor": along_y})
        copies[1].wait_recv()
        on_x = start(rows_of(whole, along_y, 1), rows_of(whole, along_y, 1), square_send.at[base + 5], square_recv.at[base + 5], {"tensor": along_x})
        return copies + [on_y, on_x]

    bias_copies = [
        start(bias_all.at[me], bias_all.at[me], bias_send.at[step], bias_recv.at[step], {"dp": (me + step) % 8})
        for step in range(1, 8)
    ]

    def line(part, slot, step, source=None):
        owner = me if source is None else source
        return pltpu.make_async_remote_copy(
            src_ref=own(part) if source is None else piece(part, source),
            dst_ref=piece(part, owner),
            send_sem=line_send.at[part, slot if source is None else 0],
            recv_sem=line_recv.at[part, slot],
            device_id={"dp": turned(step)},
            device_id_type=MESH,
        )

    def to_sibling(part, slot):
        owner = turned(slot)
        return start(
            own(part) if slot == 0 else piece(part, owner), piece(part, owner),
            core_send.at[part, slot], core_recv.at[part, slot], {"dp": sibling},
        )

    for part in range(4):
        line(part, 2, 2).start()

        @pl.when(chip % 2 == 0)
        def _():
            line(part, 3, 1).start()

        @pl.when(chip % 2 == 1)
        def _():
            line(part, 1, 3).start()

    def came(part, slot):
        line(part, slot, 4 - slot).wait_recv()

    def onward(part):
        @pl.when(chip == 2)
        def _():
            line(part, 1, 1, turned(2)).start()
            line(part, 1, 3).start()

        @pl.when(chip == 1)
        def _():
            line(part, 3, 3, turned(2)).start()
            line(part, 3, 1).start()

    siblings = [to_sibling(part, 0) for part in range(4)]
    here[2].wait()
    values = x_ref[...].astype(jnp.float32)
    centred = values - jnp.mean(values, -1, keepdims=True)
    recip = lax.rsqrt(jnp.mean(centred * centred, -1, keepdims=True) + norm_eps)
    recip_out[...] = recip
    normed_out[...] = centred * recip
    a_ref[...] = (normed_out[...] * gain_ref[0:1, :] + shift_ref[0:1, :]).astype(low)
    a_copies = square_first(a_ref, a_all, 0)
    here[3].wait()
    locals_ = [
        pltpu.make_async_copy(a_ref, a_all.at[pl.ds(pl.multiple_of(place * rows, rows), rows)], local_sem.at[0]),
        pltpu.make_async_copy(dy_ref, dy_all.at[pl.ds(pl.multiple_of(place * rows, rows), rows)], local_sem.at[1]),
    ] + [pltpu.make_async_copy(own(part), piece(part, me), local_sem.at[2 + part]) for part in range(4)]
    for copy in locals_:
        copy.start()
    for copy, source, target in zip(here[4:], (gate_wide, down_wide), (gate_out, down_out)):
        copy.wait()
        target[...] = source[...].astype(low)
    a_copies = square_next(a_all, 0, a_copies)
    dy_copies = square_first(dy_ref, dy_all, 6)
    for part in range(4):
        came(part, 2)
        onward(part)
        siblings.append(to_sibling(part, 2))
    dy_copies = square_next(dy_all, 6, dy_copies)
    for part in range(4):
        for slot in (1, 3):
            came(part, slot)
            siblings.append(to_sibling(part, slot))
    for copy in a_copies[2:] + dy_copies[2:] + bias_copies + siblings:
        copy.wait_recv()
    for copy in a_copies + dy_copies + bias_copies + siblings:
        copy.wait_send()
    for part in range(4):
        line(part, 2, 2).wait_send()

        @pl.when(chip < 3)
        def _():
            line(part, 3, 1).wait_send()

        @pl.when(chip > 0)
        def _():
            line(part, 1, 3).wait_send()

        @pl.when(chip == 2)
        def _():
            line(part, 1, 1, turned(2)).wait_send()

        @pl.when(chip == 1)
        def _():
            line(part, 3, 3, turned(2)).wait_send()

    for copy in locals_:
        copy.wait()


def start_gather(x, gains, shifts, dy, bias, wq, wo, gate, down):
    dma = pltpu.SemaphoreType.DMA
    low, wide = jnp.bfloat16, jnp.float32
    anywhere = pl.BlockSpec(memory_space=pl.ANY)
    local_ = pl.BlockSpec(memory_space=pltpu.VMEM)
    shape = jax.ShapeDtypeStruct
    rows, model = x.shape
    return pl.pallas_call(
        start_kernel,
        out_shape=(
            shape((4 * rows, model), low),
            shape((4 * rows, model), low),
            shape((8, *bias.shape), bias.dtype),
            shape((wq.shape[0], 8 * wq.shape[1], wq.shape[2]), low),
            shape((wo.shape[0], 8 * wo.shape[1]), low),
            shape((rows, model), wide),
            shape((rows, 1), wide),
            shape(gate.shape, low),
            shape(down.shape, low),
        ),
        in_specs=[anywhere, local_, local_, anywhere, local_] + [anywhere] * 4,
        out_specs=(anywhere, anywhere, local_, anywhere, anywhere, local_, local_, local_, local_),
        scratch_shapes=[
            pltpu.VMEM((rows, model), low),
            pltpu.VMEM(wq.shape, low),
            pltpu.VMEM(wo.shape, low),
            pltpu.VMEM(x.shape, low),
            pltpu.VMEM(dy.shape, low),
            pltpu.VMEM(wq.shape, wide),
            pltpu.VMEM(wo.shape, wide),
            pltpu.VMEM(gate.shape, wide),
            pltpu.VMEM(down.shape, wide),
            dma((12,)), dma((12,)), dma((8,)), dma((8,)),
            dma((4, 4)), dma((4, 4)), dma((4, 4)), dma((4, 4)), dma((12,)),
        ],
        compiler_params=pltpu.CompilerParams(
            collective_id=2, has_side_effects=True, vmem_limit_bytes=60 * 1024 * 1024
        ),
        cost_estimate=pl.CostEstimate(flops=0, bytes_accessed=200_000_000, transcendentals=0),
        name="start_gather",
    )(x, gains, shifts, dy, bias, wq, wo, gate, down)


def back_kernel(
    terms_ref, ready_ref, resid_ref, gain_ref, dy_ref, whole_ref, grad_out, second_out,
    first_x, first_y, staged, second, normed, low_ref,
    send_sem, recv_sem, row_send, row_recv, local_sem,
):
    del ready_ref
    me, along_x, along_y = partners()
    rows = grad_out.shape[0]
    half = rows // 2
    corner = 3 - me
    low, wide = jnp.bfloat16, jnp.float32

    def term(owner, which):
        return terms_ref.at[pl.ds(pl.multiple_of(owner * rows + which * half, half), half)]

    def part(owner, which):
        return whole_ref.at[pl.ds(pl.multiple_of(owner * rows + which * half, half), half)]

    def start(source, target_ref, target, sends, receives, index):
        copy = pltpu.make_async_remote_copy(
            src_ref=source,
            dst_ref=target_ref,
            send_sem=sends.at[index],
            recv_sem=receives.at[index],
            device_id={"tensor": target},
            device_id_type=MESH,
        )
        copy.start()
        return copy

    greet((along_x, along_y))
    x_on = start(term(corner, 0), first_x.at[1], along_x, send_sem, recv_sem, 0)
    y_on = start(term(corner, 1), first_y.at[1], along_y, send_sem, recv_sem, 1)
    x_own = start(term(along_x, 0), first_x.at[0], along_x, send_sem, recv_sem, 2)
    y_own = start(term(along_y, 1), first_y.at[0], along_y, send_sem, recv_sem, 3)
    resid = resid_ref[...]
    centred = resid - jnp.mean(resid, -1, keepdims=True)
    recip = lax.rsqrt(jnp.mean(centred * centred, -1, keepdims=True) + norm_eps)
    normed[...] = centred * recip
    x_on.wait_recv()
    staged[0] = (term(along_y, 0)[...].astype(wide) + first_x[1].astype(wide)).astype(low)
    y_last = start(staged.at[0], second.at[0], along_y, send_sem, recv_sem, 4)
    y_on.wait_recv()
    staged[1] = (term(along_x, 1)[...].astype(wide) + first_y[1].astype(wide)).astype(low)
    x_last = start(staged.at[1], second.at[1], along_x, send_sem, recv_sem, 5)
    gain = gain_ref[...]
    sums = [jnp.zeros_like(gain), jnp.zeros_like(gain)]
    for which, own, last, came in ((0, x_own, y_last, first_x), (1, y_own, x_last, first_y)):
        here = slice(which * half, (which + 1) * half)
        own.wait_recv()
        last.wait_recv()
        grad = term(me, which)[...].astype(wide) + came[0].astype(wide) + second[which].astype(wide)
        scaled = grad * gain
        inner = (
            scaled
            - jnp.mean(scaled, -1, keepdims=True)
            - normed[here, :] * jnp.mean(scaled * normed[here, :], -1, keepdims=True)
        )
        total = dy_ref[here, :].astype(wide) + recip[here, :] * inner
        grad_out[here, :] = total
        low_ref[here, :] = total.astype(low)
        if which == 0:
            copies = [start(low_ref.at[pl.ds(0, half)], part(me, 0), along_x, row_send, row_recv, 0)]
        else:
            copies += [
                start(low_ref.at[pl.ds(half, half)], part(me, 1), along_y, row_send, row_recv, 1),
                start(low_ref.at[pl.ds(half, half)], part(me, 1), along_x, row_send, row_recv, 2),
                start(low_ref.at[pl.ds(0, half)], part(me, 0), along_y, row_send, row_recv, 3),
            ]
        sums[0] += jnp.sum(grad * normed[here, :], 0, keepdims=True)
        sums[1] += jnp.sum(grad, 0, keepdims=True)
    mine = pltpu.make_async_copy(low_ref, whole_ref.at[pl.ds(pl.multiple_of(me * rows, rows), rows)], local_sem)
    mine.start()
    second_out[0:1, :] = sums[0]
    second_out[1:2, :] = sums[1]
    copies[0].wait_recv()
    copies.append(start(part(along_x, 0), part(along_x, 0), along_y, row_send, row_recv, 4))
    copies[1].wait_recv()
    copies.append(start(part(along_y, 1), part(along_y, 1), along_x, row_send, row_recv, 5))
    for copy in copies[2:]:
        copy.wait_recv()
    for copy in [x_on, y_on, x_own, y_own, y_last, x_last] + copies:
        copy.wait_send()
    mine.wait()


def square_back(terms, ready, resid, gain, dy):
    dma = pltpu.SemaphoreType.DMA
    low, wide = jnp.bfloat16, jnp.float32
    shape, vmem = jax.ShapeDtypeStruct, pltpu.VMEM
    rows, width = resid.shape
    anywhere, local_ = pl.BlockSpec(memory_space=pl.ANY), pl.BlockSpec(memory_space=pltpu.VMEM)
    pair = vmem((2, rows // 2, width), low)
    return pl.pallas_call(
        back_kernel,
        out_shape=(shape((4 * rows, width), low), shape((rows, width), wide), shape((2, width), wide)),
        in_specs=[local_, anywhere, local_, local_, local_],
        out_specs=(anywhere, local_, local_),
        scratch_shapes=[
            pair, pair, pair, pair, vmem((rows, width), wide), vmem((rows, width), low),
            dma((6,)), dma((6,)), dma((6,)), dma((6,)), dma,
        ],
        compiler_params=pltpu.CompilerParams(
            collective_id=1, has_side_effects=True, vmem_limit_bytes=32 * 1024 * 1024
        ),
        cost_estimate=pl.CostEstimate(flops=0, bytes_accessed=rows * width * 400, transcendentals=0),
        name="square_back",
    )(terms, ready, resid, gain, dy)


def last_kernel(
    first_ref, proj_ref, normed_ref, recip_ref, gain_ref, second_ref, bias_ref,
    step_out, proj_out, vector_out, bias_out,
    square_x, square_y, staged, square_last, mine, near,
    corners, vector_mine, vector_came, vector_slots, bias_mine, bias_came, bias_slots,
    square_send, square_recv, vector_send, vector_recv, bias_send, bias_recv, core_send, core_recv, line_send, line_recv,
):
    place, along_x, along_y = partners()
    corner = 3 - place
    me = lax.axis_index("dp")
    chip, core = me // 2, me % 2
    sibling = me + 1 - 2 * core
    width = proj_out.shape[1]
    rows = step_out.shape[0]
    half = rows // 2
    low, wide = jnp.bfloat16, jnp.float32

    def start(source, target, send_sem, recv_sem, device):
        copy = pltpu.make_async_remote_copy(
            src_ref=source, dst_ref=target, send_sem=send_sem, recv_sem=recv_sem,
            device_id=device, device_id_type=MESH,
        )
        copy.start()
        return copy

    barrier = pltpu.get_barrier_semaphore()
    chips = [{"dp": (me + 2 * step) % 8} for step in (1, 2, 3)]
    square = [{"tensor": device} for device in (along_x, along_y, corner)]
    for other in square + [{"dp": sibling}] + chips:
        pl.semaphore_signal(barrier, inc=1, device_id=other, device_id_type=MESH)
    pl.semaphore_wait(barrier, 7)

    def turned(slot, which):
        return 2 * ((chip + slot) % 4) + which

    def proj_part(owner):
        return proj_ref.at[:, pl.ds(pl.multiple_of(owner * width, width), width)]

    exchange = {
        slot: start(
            proj_part(turned(slot, 1 - core)), mine.at[slot], core_send.at[slot], core_recv.at[slot], {"dp": sibling}
        )
        for slot in (3, 1, 2, 0)
    }

    def line(slot, step, part):
        return pltpu.make_async_remote_copy(
            src_ref=mine.at[slot], dst_ref=near.at[part], send_sem=line_send.at[part], recv_sem=line_recv.at[part],
            device_id={"dp": turned(step, core)}, device_id_type=MESH,
        )

    def term(owner, part):
        return first_ref.at[pl.ds(pl.multiple_of(owner * rows + part * half, half), half)]

    def rows_at(owner, part):
        return term(owner, part)[...].astype(wide)

    plan = [
        (term(corner, 0), square_x.at[1], square[0]),
        (term(corner, 1), square_y.at[1], square[1]),
        (term(along_x, 0), square_x.at[0], square[0]),
        (term(along_y, 1), square_y.at[0], square[1]),
    ]
    copies = [
        start(source, target, square_send.at[i], square_recv.at[i], device)
        for i, (source, target, device) in enumerate(plan)
    ]
    for slot in (3, 1, 2):
        exchange[slot].wait_recv()
        mine[slot] = (mine[slot].astype(wide) + proj_part(turned(slot, core))[...].astype(wide)).astype(low)
        if slot == 3:

            @pl.when(chip == 0)
            def _():
                line(3, 1, 0).start()

            @pl.when((chip == 1) | (chip == 2))
            def _():
                line(3, 3, 3).start()

        elif slot == 1:

            @pl.when(chip == 3)
            def _():
                line(1, 3, 0).start()

            @pl.when((chip == 1) | (chip == 2))
            def _():
                line(1, 1, 1).start()

        else:

            @pl.when((chip == 0) | (chip == 3))
            def _():
                line(2, 2, 2).start()

    bias_mine[...] = bias_ref[...]
    bias_copies = [start(bias_mine, bias_came, bias_send.at[0], bias_recv.at[0], {"dp": sibling})]
    bias_copies[0].wait_recv()
    bias_slots[chip] = bias_mine[...] + bias_came[...]
    bias_copies += [
        start(bias_slots.at[chip], bias_slots.at[chip], bias_send.at[1 + i], bias_recv.at[1 + i], chips[i])
        for i in range(3)
    ]
    copies[0].wait_recv()
    staged[0] = (rows_at(along_y, 0) + square_x[1].astype(wide)).astype(low)
    copies.append(start(staged.at[0], square_last.at[0], square_send.at[4], square_recv.at[4], square[1]))
    copies[1].wait_recv()
    staged[1] = (rows_at(along_x, 1) + square_y[1].astype(wide)).astype(low)
    copies.append(start(staged.at[1], square_last.at[1], square_send.at[5], square_recv.at[5], square[0]))

    @pl.when((chip == 1) | (chip == 2))
    def _():
        line(0, 1, 0).wait_recv()
        mine[2] = (mine[2].astype(wide) + near[0].astype(wide)).astype(low)
        line(2, 2, 2).start()

    @pl.when(chip == 0)
    def _():
        line(3, 1, 0).wait_send()
        line(1, 1, 1).start()

    @pl.when(chip == 3)
    def _():
        line(1, 3, 0).wait_send()
        line(3, 3, 3).start()

    gain = gain_ref[...]
    vector_gain = jnp.zeros_like(gain)
    vector_shift = jnp.zeros_like(gain)
    for part, came in enumerate((square_x, square_y)):
        here = slice(part * half, (part + 1) * half)
        copies[2 + part].wait_recv()
        copies[4 + part].wait_recv()
        grad = rows_at(place, part) + came[0].astype(wide) + square_last[part].astype(wide)
        normed = normed_ref[here, :]
        vector_gain += jnp.sum(grad * normed, 0, keepdims=True)
        vector_shift += jnp.sum(grad, 0, keepdims=True)
        scaled = grad * gain
        inner = (
            scaled
            - jnp.mean(scaled, -1, keepdims=True)
            - normed * jnp.mean(scaled * normed, -1, keepdims=True)
        )
        step_out[here, :] = recip_ref[here, :] * inner
    corners[place, 0:1, :] = vector_gain
    corners[place, 1:2, :] = second_ref[0:1, :]
    corners[place, 2:3, :] = vector_shift
    corners[place, 3:4, :] = second_ref[1:2, :]
    vector_copies = [
        start(corners.at[place], corners.at[place], vector_send.at[i], vector_recv.at[i], square[i]) for i in range(3)
    ]
    for copy in vector_copies:
        copy.wait_recv()
    vector_mine[...] = (corners[0] + corners[1]) + (corners[2] + corners[3])
    vector_copies.append(start(vector_mine, vector_came, vector_send.at[3], vector_recv.at[3], {"dp": sibling}))
    vector_copies[3].wait_recv()
    vector_slots[chip] = vector_mine[...] + vector_came[...]
    vector_copies += [
        start(vector_slots.at[chip], vector_slots.at[chip], vector_send.at[4 + i], vector_recv.at[4 + i], chips[i])
        for i in range(3)
    ]
    for copy in vector_copies[4:] + bias_copies[1:]:
        copy.wait_recv()
    vector_out[...] = (vector_slots[0] + vector_slots[1]) + (vector_slots[2] + vector_slots[3])
    bias_out[...] = (bias_slots[0] + bias_slots[1]) + (bias_slots[2] + bias_slots[3])

    exchange[0].wait_recv()
    line(2, 2, 2).wait_recv()

    @pl.when(chip > 0)
    def _():
        line(1, 1, 1).wait_recv()

    @pl.when(chip < 3)
    def _():
        line(3, 3, 3).wait_recv()

    total = proj_part(turned(0, core))[...].astype(wide) + mine[0].astype(wide) + near[2].astype(wide)
    total = total + jnp.where(chip > 0, near[1].astype(wide), 0.0)
    proj_out[...] = total + jnp.where(chip < 3, near[3].astype(wide), 0.0)
    for copy in copies + vector_copies + bias_copies + list(exchange.values()):
        copy.wait_send()
    line(2, 2, 2).wait_send()

    @pl.when(chip < 3)
    def _():
        line(1, 1, 1).wait_send()

    @pl.when(chip > 0)
    def _():
        line(3, 3, 3).wait_send()


def last_reduce(first, proj, normed, recip, gain, second, bias):
    dma = pltpu.SemaphoreType.DMA
    low, wide = jnp.bfloat16, jnp.float32
    shape, vmem = jax.ShapeDtypeStruct, pltpu.VMEM
    rows, model = normed.shape
    pair = vmem((2, rows // 2, model), low)
    blocks = vmem((4, proj.shape[0], proj.shape[1] // 8), low)
    return pl.pallas_call(
        last_kernel,
        out_shape=(
            shape((rows, model), wide),
            shape((proj.shape[0], proj.shape[1] // 8), wide),
            shape((4, model), wide),
            shape(bias.shape, wide),
        ),
        in_specs=[pl.BlockSpec(memory_space=pltpu.VMEM)] * 7,
        out_specs=(pl.BlockSpec(memory_space=pltpu.VMEM),) * 4,
        scratch_shapes=[
            pair, pair, pair, pair, blocks, blocks,
            vmem((4, 4, model), wide),
            vmem((4, model), wide),
            vmem((4, model), wide),
            vmem((4, 4, model), wide),
            vmem(bias.shape, wide),
            vmem(bias.shape, wide),
            vmem((4, *bias.shape), wide),
            dma((6,)), dma((6,)), dma((7,)), dma((7,)), dma((4,)), dma((4,)),
            dma((4,)), dma((4,)), dma((4,)), dma((4,)),
        ],
        compiler_params=pltpu.CompilerParams(
            collective_id=3, has_side_effects=True, vmem_limit_bytes=40 * 1024 * 1024
        ),
        cost_estimate=pl.CostEstimate(flops=0, bytes_accessed=120_000_000, transcendentals=0),
        name="last_reduce",
    )(first, proj, normed, recip, gain, second, bias)


def after(late, early):
    return lax.optimization_barrier((late, early))[0]


class Plain:
    def gather_rows(self, block):
        return lax.all_gather(block, "tensor", axis=0, tiled=True)

    def reduce_rows(self, terms, ready, name):
        return lax.psum_scatter(terms, "tensor", scatter_dimension=0, tiled=True).astype(jnp.float32)

    def begin(self, x, gains, shifts, dy, bias, w_qkv, w_output, gate_up, down):
        low = jnp.bfloat16
        out, normed, recip = layer_norm(x.astype(jnp.float32), gains[0], shifts[0])
        return (
            self.gather_rows(out.astype(low)),
            self.gather_rows(dy),
            lax.all_gather(bias.astype(low), "dp", axis=2, tiled=True),
            gather_dp(w_qkv.astype(low), 1),
            gather_dp(w_output.astype(low), 1),
            normed,
            recip,
            gate_up.astype(low),
            down.astype(low),
        )

    def reduce_beside(self, terms):
        return (self.reduce_rows(terms, None, 0),)

    def back(self, terms, ready, resid, gain, dy):
        grad = self.reduce_rows(terms, None, 0)
        _, normed, recip = layer_norm(resid, gain, gain)
        total = dy.astype(jnp.float32) + norm_back(grad, normed, recip, gain)
        sums = jnp.stack([jnp.sum(grad * normed, 0), jnp.sum(grad, 0)])
        return self.gather_rows(total.astype(jnp.bfloat16)), total, sums

    def finish(self, first, proj, normed, recip, gain, second, bias):
        first = self.reduce_rows(first, None, 0)
        vectors = jnp.stack([jnp.sum(first * normed, 0), second[0], jnp.sum(first, 0), second[1]])
        step = norm_back(first, normed, recip, gain)
        return step, scatter_dp(proj, 1), lax.psum(vectors, ("dp", "tensor")), lax.psum(bias, "dp")


class Line(Plain):
    def gather_rows(self, block):
        return square_gather(block)

    def reduce_rows(self, terms, ready, name):
        return square_reduce(terms, ready, name)

    def begin(self, x, gains, shifts, dy, bias, w_qkv, w_output, gate_up, down):
        a, dy, came, *others = start_gather(x, gains, shifts, dy, bias, w_qkv, w_output, gate_up, down)
        return a, dy, came.transpose(1, 2, 0, 3).reshape(*bias.shape[:2], -1), *others

    def flat(self, values):
        values = values.astype(jnp.float32).reshape(-1)
        width = -(-values.shape[0] // 1024) * 1024
        return jnp.pad(values, (0, width - values.shape[0])).reshape(8, -1)

    def reduce_beside(self, terms):
        me = lax.axis_index("tensor")
        rows = terms.shape[0] // 4
        parts = [lax.dynamic_slice_in_dim(terms, (me ^ step) * rows, rows, 0) for step in range(4)]
        for step in (3, 1, 2):
            parts[step] = lax.ppermute(parts[step], "tensor", [(i, i ^ step) for i in range(4)])
        return tuple(parts)

    def back(self, terms, ready, resid, gain, dy):
        return square_back(terms, ready, resid, gain.reshape(1, -1), dy)

    def finish(self, first, proj, normed, recip, gain, second, bias):
        step, proj_grad, vectors, total = last_reduce(
            first, proj, normed, recip, gain.reshape(1, -1), second, self.flat(bias)
        )
        return step, proj_grad, vectors, total.reshape(-1)[: bias.size].reshape(bias.shape)


def row_major(values):
    return with_layout_constraint(values, Layout(tuple(range(values.ndim))))


def gather_dp(block, axis):
    return row_major(lax.all_gather(block.astype(jnp.bfloat16), "dp", axis=axis, tiled=True))


def scatter_dp(terms, axis):
    return lax.psum_scatter(terms.astype(jnp.bfloat16), "dp", scatter_dimension=axis, tiled=True)


def local(
    routes,
    inputs,
    cotangent,
    gains,
    shifts,
    qkv_weight,
    biases,
    out_weight,
    gate_up,
    down_weight,
    momentum_gains,
    momentum_shifts,
    momentum_qkv,
    momentum_biases,
    momentum_out,
    momentum_gate,
    momentum_down,
    variance_gains,
    variance_shifts,
    variance_qkv,
    variance_biases,
    variance_out,
    variance_gate,
    variance_down,
):
    low = jnp.bfloat16
    local_heads = biases.shape[1]
    local_width = qkv_weight.shape[2]
    head_size = local_width // local_heads
    xin = inputs.astype(jnp.float32)
    a_all, dy_all, bias_all, w_qkv, w_output, first_normed, first_recip, gate_low, down_low = routes.begin(
        inputs, gains, shifts, cotangent, biases, qkv_weight, out_weight, gate_up, down_weight
    )
    bias_all = bias_all.reshape(3, local_width).astype(jnp.float32)
    w_gate_up = gather_dp(after(gate_low, w_output), 1)
    lin = jnp.einsum("rd,kdc->krc", a_all, w_qkv, preferred_element_type=jnp.float32)
    qkv, heads, logs = attention_forward(lin, bias_all, head_size)
    resid = xin + routes.reduce_rows(mxu(heads, w_output, NN).astype(low), logs, 4)
    second_out, _, _ = layer_norm(resid, gains[1], shifts[1])
    m_all = routes.gather_rows(second_out.astype(low))
    w_down = gather_dp(after(down_low, (w_gate_up, m_all)), 1)
    gate_vals = jnp.einsum("rd,kdc->krc", m_all, w_gate_up, preferred_element_type=jnp.float32)
    gate_lin, upward = gate_vals[0], gate_vals[1]
    sigmoid_gate = jax.nn.sigmoid(gate_lin)
    silu_gate = gate_lin * sigmoid_gate
    hidden = (silu_gate * upward).astype(low)
    down_terms = mxu(hidden, dy_all, TN).astype(low)
    down_grad = scatter_dp(down_terms, 1)
    w_down = after(w_down, down_terms)
    block_terms = mxu(hidden, w_down, NN).astype(low)
    down_parts = routes.reduce_beside(block_terms)
    hidden_grad = mxu(dy_all, after(w_down, block_terms), NT)
    gate_grad_low = (
        hidden_grad * upward * sigmoid_gate * (1.0 + gate_lin * (1.0 - sigmoid_gate))
    ).astype(low)
    up_grad_low = (hidden_grad * silu_gate).astype(low)
    both_grads = jnp.stack([gate_grad_low, up_grad_low], 0)
    gate_terms = jnp.einsum("rd,krc->kdc", m_all, both_grads, preferred_element_type=jnp.float32)
    gate_terms = row_major(gate_terms.astype(low))
    second_terms = jnp.einsum(
        "krc,kdc->rd", both_grads, w_gate_up, preferred_element_type=jnp.float32
    ).astype(low)
    gate_grad = scatter_dp(after(gate_terms, (down_grad, second_terms, down_parts)), 1)
    resid_full, resid_grad, second_sums = routes.back(
        after(second_terms, down_grad), down_grad[:16, :128], resid, gains[1], cotangent
    )
    out_terms = mxu(heads, resid_full, TN).astype(low)
    heads_grad = mxu(resid_full, w_output, NT).astype(low)
    lin_grads, bias_terms = attention_backward(qkv, heads_grad, logs, head_size)
    qkv_terms = jnp.einsum("rd,krc->kdc", a_all, lin_grads, preferred_element_type=jnp.float32)
    qkv_terms = row_major(qkv_terms.astype(low))
    first_terms = jnp.einsum(
        "krc,kdc->rd", lin_grads, w_qkv, preferred_element_type=jnp.float32
    ).astype(low)
    qkv_grad = scatter_dp(after(qkv_terms, (gate_grad, out_terms)), 1)
    input_step, out_grad, vectors, bias_sum = routes.finish(
        first_terms,
        out_terms,
        first_normed,
        first_recip,
        gains[0],
        second_sums,
        bias_terms,
    )
    input_grad = resid_grad + input_step
    block_out = resid
    for part in after(down_parts, vectors):
        block_out = block_out + part.astype(jnp.float32)
    block_out = block_out.astype(low)
    gains_grad, shifts_grad = vectors[:2], vectors[2:]
    down_grad, gate_grad, out_grad = (
        grad.astype(jnp.float32) for grad in (*after((down_grad, gate_grad), vectors), out_grad)
    )
    qkv_grad = qkv_grad.astype(jnp.float32)
    per_dp = biases.shape[2]
    biases_grad = lax.dynamic_slice_in_dim(
        bias_sum.reshape(3, local_heads, head_size), lax.axis_index("dp") * per_dp, per_dp, 2
    )
    gain_new = adamw(gains, gains_grad, momentum_gains, variance_gains, 0.0, vector_rate)
    shift_new = adamw(shifts, shifts_grad, momentum_shifts, variance_shifts, 0.0, vector_rate)
    qkv_new = adamw(qkv_weight, qkv_grad, momentum_qkv, variance_qkv, decay_rate, learn_rate)
    bias_new = adamw(biases, biases_grad, momentum_biases, variance_biases, 0.0, vector_rate)
    out_new = adamw(out_weight, out_grad, momentum_out, variance_out, decay_rate, learn_rate)
    gate_new = adamw(gate_up, gate_grad, momentum_gate, variance_gate, decay_rate, learn_rate)
    down_new = adamw(down_weight, down_grad, momentum_down, variance_down, decay_rate, learn_rate)
    return (
        block_out,
        input_grad,
        gains_grad,
        shifts_grad,
        qkv_grad,
        biases_grad,
        out_grad,
        gate_grad,
        down_grad,
        gain_new[0],
        shift_new[0],
        qkv_new[0],
        bias_new[0],
        out_new[0],
        gate_new[0],
        down_new[0],
        gain_new[1],
        shift_new[1],
        qkv_new[1],
        bias_new[1],
        out_new[1],
        gate_new[1],
        down_new[1],
        gain_new[2],
        shift_new[2],
        qkv_new[2],
        bias_new[2],
        out_new[2],
        gate_new[2],
        down_new[2],
    )


def solution(mesh):
    routes = Line() if dict(mesh.shape) == {"dp": 8, "tensor": 4} else Plain()

    def step(*arrays):
        return local(routes, *arrays)

    return jax.shard_map(
        step,
        mesh=mesh,
        in_specs=(
            P(("dp", "tensor"), None),
            P(("dp", "tensor"), None),
            P(),
            P(),
            P(None, "dp", "tensor"),
            P(None, "tensor", "dp"),
            P("tensor", "dp"),
            P(None, "dp", "tensor"),
            P("tensor", "dp"),
            P(),
            P(),
            P(None, "dp", "tensor"),
            P(None, "tensor", "dp"),
            P("tensor", "dp"),
            P(None, "dp", "tensor"),
            P("tensor", "dp"),
            P(),
            P(),
            P(None, "dp", "tensor"),
            P(None, "tensor", "dp"),
            P("tensor", "dp"),
            P(None, "dp", "tensor"),
            P("tensor", "dp"),
        ),
        out_specs=(
            P(("dp", "tensor"), None),
            P(("dp", "tensor"), None),
            P(),
            P(),
            P(None, "dp", "tensor"),
            P(None, "tensor", "dp"),
            P("tensor", "dp"),
            P(None, "dp", "tensor"),
            P("tensor", "dp"),
            P(),
            P(),
            P(None, "dp", "tensor"),
            P(None, "tensor", "dp"),
            P("tensor", "dp"),
            P(None, "dp", "tensor"),
            P("tensor", "dp"),
            P(),
            P(),
            P(None, "dp", "tensor"),
            P(None, "tensor", "dp"),
            P("tensor", "dp"),
            P(None, "dp", "tensor"),
            P("tensor", "dp"),
            P(),
            P(),
            P(None, "dp", "tensor"),
            P(None, "tensor", "dp"),
            P("tensor", "dp"),
            P(None, "dp", "tensor"),
            P("tensor", "dp"),
        ),
        check_vma=False,
    )
```
